32 devices in a mesh: page: 8 (over z, x), pb: 4 (over y, core).
Axes of the slice: x: 2, y: 2, z: 4, core: 2. Of those that a mesh axis runs over, the one named last changes fastest.
Arguments:
- tokens: bfloat16 [24, 512, 768], P('page', 'pb'), may hold values from -6 to 6
- cotangent: bfloat16 [24, 512, 768], P('page', 'pb'), may hold values from -6 to 6
- boxes: int32 [4, 24, 512], P(None, 'page', 'pb'), may hold values from 0 to 3400, as said below
- resolution: int32 [2, 24], P(None, 'page'), may hold values from 600 to 3400, as said below
- padding: int32 [24, 512], P('page', 'pb'), may hold values from 0 to 1, as said below
- query_weight: bfloat16 [768, 768], P(('page', 'pb')), may hold values from -0.21875 to 0.21875
- keys_weight: bfloat16 [768, 768], P(('page', 'pb')), may hold values from -0.21875 to 0.21875
- values_weight: bfloat16 [768, 768], P(('page', 'pb')), may hold values from -0.21875 to 0.21875
- output_weight: bfloat16 [768, 768], P(('page', 'pb')), may hold values from -1.25 to 1.25
- query_place: bfloat16 [768, 768], P(('page', 'pb')), may hold values from -0.5 to 0.5
- keys_place: bfloat16 [768, 768], P(('page', 'pb')), may hold values from -0.5 to 0.5
- inner_weight: bfloat16 [768, 3072], P(('page', 'pb')), may hold values from -0.21875 to 0.21875
- outer_weight: bfloat16 [3072, 768], P(('page', 'pb')), may hold values from -0.109375 to 0.109375
- query_bias: bfloat16 [768], P(('page', 'pb')), may hold values from -3 to 3
- keys_bias: bfloat16 [768], P(('page', 'pb')), may hold values from -3 to 3
- values_bias: bfloat16 [768], P(('page', 'pb')), may hold values from -3 to 3
- output_bias: bfloat16 [768], P(('page', 'pb')), may hold values from -3 to 3
- inner_bias: bfloat16 [3072], P(('page', 'pb')), may hold values from -3 to 3
- outer_bias: bfloat16 [768], P(('page', 'pb')), may hold values from -3 to 3
- first_gain: bfloat16 [768], P(('page', 'pb')), may hold values from 0.25 to 1.75
- first_shift: bfloat16 [768], P(('page', 'pb')), may hold values from -3 to 3
- second_gain: bfloat16 [768], P(('page', 'pb')), may hold values from 0.25 to 1.75
- second_shift: bfloat16 [768], P(('page', 'pb')), may hold values from -3 to 3
Outputs:
- layer_output: bfloat16 [24, 512, 768], P('page', 'pb')
- tokens_grad: float32 [24, 512, 768], P('page', 'pb')
- query_weight_grad: float32 [768, 768], P(('page', 'pb'))
- keys_weight_grad: float32 [768, 768], P(('page', 'pb'))
- values_weight_grad: float32 [768, 768], P(('page', 'pb'))
- output_weight_grad: float32 [768, 768], P(('page', 'pb'))
- query_place_grad: float32 [768, 768], P(('page', 'pb'))
- keys_place_grad: float32 [768, 768], P(('page', 'pb'))
- inner_weight_grad: float32 [768, 3072], P(('page', 'pb'))
- outer_weight_grad: float32 [3072, 768], P(('page', 'pb'))
- query_bias_grad: float32 [768], P(('page', 'pb'))
- keys_bias_grad: float32 [768], P(('page', 'pb'))
- values_bias_grad: float32 [768], P(('page', 'pb'))
- output_bias_grad: float32 [768], P(('page', 'pb'))
- inner_bias_grad: float32 [3072], P(('page', 'pb'))
- outer_bias_grad: float32 [768], P(('page', 'pb'))
- first_gain_grad: float32 [768], P(('page', 'pb'))
- first_shift_grad: float32 [768], P(('page', 'pb'))
- second_gain_grad: float32 [768], P(('page', 'pb'))
- second_shift_grad: float32 [768], P(('page', 'pb'))
The draws below stay inside these ranges and needn't reach their ends.
Inputs may be any that keep to these rules, and one draw needn't show every extreme that they name: `boxes`: rows hold x0, y0, x1, y1 in pixels with 0 <= x0 <= x1 <= the page's width and 0 <= y0 <= y1 <= its height; each page's first token spans the page's full height. `resolution`: row 0 holds each page's width in pixels, row 1 its height. `padding`: each page's ones form a prefix of 128 or more tokens; among pages k * 3 to (k + 1) * 3 - 1 one page has more than 384 ones.
All inputs are finite; a program needn't handle non-finite values.
Results may differ from the reference program's by a relative error of at most 0.028.
Values may be sent and summed in bfloat16 or wider, within the bound.
No kernel may reach another device: no remote copies, remote signals or barrier semaphores. Data moves between devices by JAX's collectives and lax.ppermute only.
A program may use at most 192 MiB of HBM per device.

```python
import math
import jax
import jax.numpy as jnp
from jax import lax

D = 768
HEADS = 12
HD = 64
FF = 3072
FREQ = 192
PAGE_LEN = 512
PAGES_DEV = 3
PAGES = 24


def page_sizes(key):
    inner_key = jax.random.fold_in(key, 101)
    width_key, height_key, pick_key = jax.random.split(inner_key, 3)
    widths = jax.random.randint(width_key, (PAGES,), 600, 2601)
    heights = jax.random.randint(height_key, (PAGES,), 800, 3401)
    picked = jax.random.randint(pick_key, (2,), 0, PAGES)
    widths = widths.at[picked[0]].set(600)
    heights = heights.at[picked[1]].set(3400)
    return jnp.stack([widths, heights]).astype(jnp.int32)


def draw_resolution(key, part):
    shared = page_sizes(key)
    return shared


def draw_boxes(key, part):
    shared = page_sizes(key)
    key = jax.random.fold_in(key, 5)
    left_key, right_key, top_key, bottom_key = jax.random.split(key, 4)
    widths = shared[0][:, None]
    heights = shared[1][:, None]
    shape = (PAGES, PAGE_LEN)
    left = jax.random.randint(left_key, shape, 0, widths)
    right = jax.random.randint(right_key, shape, left, widths + 1)
    top = jax.random.randint(top_key, shape, 0, heights)
    bottom = jax.random.randint(bottom_key, shape, top, heights + 1)
    top = top.at[:, 0].set(0)
    bottom = bottom.at[:, 0].set(shared[1])
    return jnp.stack([left, top, right, bottom]).astype(jnp.int32)


def draw_padding(key, part):
    key = jax.random.fold_in(key, 7)
    length_key, pick_key, long_key = jax.random.split(key, 3)
    lengths = jax.random.randint(length_key, (PAGES,), PAGE_LEN // 4, PAGE_LEN + 1)
    run_count = PAGES // PAGES_DEV
    filled = jnp.arange(run_count) * PAGES_DEV + jax.random.randint(pick_key, (run_count,), 0, PAGES_DEV)
    long_lengths = jax.random.randint(long_key, (run_count,), 3 * PAGE_LEN // 4 + 1, PAGE_LEN + 1)
    lengths = lengths.at[filled].set(long_lengths)
    positions = jnp.arange(PAGE_LEN)
    return (positions[None, :] < lengths[:, None]).astype(jnp.int32)


def raised(drawn, key, source, target, parts, factor):
    owner, partner = [(jnp.arange(drawn.shape[dim]) // (drawn.shape[dim] // parts)).reshape([-1 if axis == dim else 1 for axis in range(drawn.ndim)]) for dim in (source, target)]
    chosen = jax.random.permutation(key, parts)[partner]
    strong = (owner == chosen) | (owner == (partner + parts // 2) % parts)
    return jnp.where(strong, factor * drawn, drawn)


def block_scale(own_key, extent, shards, least, top_value):
    loudness, own = 1.0, jax.random.fold_in(own_key, 6)
    for position, parts in shards:
        steps = jnp.exp(jax.random.uniform(jax.random.fold_in(own, position), (parts,), jnp.float32, least / len(shards), top_value / len(shards)))
        loudness = loudness * jnp.repeat(steps, extent[position] // parts).reshape([-1 if axis == position else 1 for axis in range(len(extent))])
    return loudness


def normal_values(key, extent, scale, limit, cuts=(), held_as=jnp.bfloat16):
    drawn = scale * jax.random.normal(key, extent, jnp.float32)
    if cuts:
        drawn = drawn * block_scale(key, extent, cuts, -0.22, 0.18)
    return jnp.clip(drawn, -limit, limit).astype(held_as)


def bell_draw_with(own_key, dims, deviation, most, cuts, heavy, held_as=jnp.bfloat16):
    values = deviation * jax.random.normal(own_key, dims, jnp.float32)
    if cuts:
        values = values * block_scale(own_key, dims, cuts, -0.22, 0.18)
    return jnp.clip(raised(values, jax.random.fold_in(own_key, 3), *heavy), -most, most).astype(held_as)


def setup_inputs(seed: int = 0) -> dict:
    seeds = jax.random.split(jax.random.key(seed), 24)
    return {
        "tokens": bell_draw_with(seeds[0], (PAGES, PAGE_LEN, D), 1.0, 6.0, ((0, 8), (1, 4)), (0, 2, 8, 2.0)),
        "cotangent": normal_values(seeds[1], (PAGES, PAGE_LEN, D), 1.0, 6.0, ((0, 8), (1, 4))),
        "boxes": draw_boxes(jax.random.fold_in(seeds[23], 71), 0),
        "resolution": draw_resolution(jax.random.fold_in(seeds[23], 71), 0),
        "padding": draw_padding(jax.random.fold_in(seeds[23], 71), 0),
        "query_weight": normal_values(seeds[5], (D, D), D ** -0.5, 0.21875, ((0, 32),)),
        "keys_weight": normal_values(seeds[6], (D, D), D ** -0.5, 0.21875, ((0, 32),)),
        "values_weight": normal_values(seeds[7], (D, D), D ** -0.5, 0.21875, ((0, 32),)),
        "output_weight": normal_values(seeds[8], (D, D), (D // 32) ** -0.5, 1.25, ((0, 32),)),
        "query_place": normal_values(seeds[9], (D, 4 * FREQ), (2 * HD) ** -0.5, 0.5, ((0, 32),)),
        "keys_place": normal_values(seeds[10], (D, 4 * FREQ), (2 * HD) ** -0.5, 0.5, ((0, 32),)),
        "inner_weight": normal_values(seeds[11], (D, FF), D ** -0.5, 0.21875, ((0, 32),)),
        "outer_weight": normal_values(seeds[12], (FF, D), FF ** -0.5, 0.109375, ((0, 32),)),
        "query_bias": normal_values(seeds[13], (D,), 0.5, 3.0, ((0, 32),)),
        "keys_bias": normal_values(seeds[14], (D,), 0.5, 3.0, ((0, 32),)),
        "values_bias": normal_values(seeds[15], (D,), 0.5, 3.0, ((0, 32),)),
        "output_bias": normal_values(seeds[16], (D,), 0.5, 3.0, ((0, 32),)),
        "inner_bias": normal_values(seeds[17], (FF,), 0.5, 3.0, ((0, 32),)),
        "outer_bias": normal_values(seeds[18], (D,), 0.5, 3.0, ((0, 32),)),
        "first_gain": jnp.clip(1.0 + 0.15 * jax.random.normal(seeds[19], (D,), jnp.float32), 0.25, 1.75).astype(jnp.bfloat16),
        "first_shift": normal_values(seeds[20], (D,), 0.5, 3.0, ((0, 32),)),
        "second_gain": jnp.clip(1.0 + 0.15 * jax.random.normal(seeds[21], (D,), jnp.float32), 0.25, 1.75).astype(jnp.bfloat16),
        "second_shift": normal_values(seeds[22], (D,), 0.5, 3.0, ((0, 32),)),
    }


finest = lax.Precision.HIGHEST

@jax.custom_vjp
def low(v):
    return lax.optimization_barrier(v.astype(jnp.bfloat16)).astype(jnp.float32)

@jax.custom_vjp
def low_back(v):
    return v

def low_keep(v):
    return (low(v), None)

def low_pass(kept, grad):
    return (grad,)

def back_keep(v):
    return (v, None)

def back_low(kept, grad):
    return (low(grad),)
low.defvjp(low_keep, low_pass)
low_back.defvjp(back_keep, back_low)

def trig_of(boxes, resolution):
    grid_x = (boxes[0] + boxes[2]) * 500 // resolution[0][:, None]
    grid_y = (boxes[1] + boxes[3]) * 500 // resolution[1][:, None]
    grids = jnp.stack([grid_x, grid_y], axis=-1).astype(jnp.float32)
    rates = jnp.exp(jnp.arange(FREQ).astype(jnp.float32) * (-math.log(10000.0) / FREQ))
    angles = grids[..., None] * rates
    return (jnp.sin(angles), jnp.cos(angles))

def features(first, second):
    stacked = jnp.stack([first, second], axis=-2)
    return stacked.reshape(first.shape[:-2] + (4 * first.shape[-1],))

def turn_query(spread, sines, cosines):
    pieces = spread.reshape(spread.shape[:-1] + (2, 2, sines.shape[-1]))
    sine_part = pieces[..., 0, :]
    cosine_part = pieces[..., 1, :]
    turned = jnp.stack([sine_part * cosines + cosine_part * sines, cosine_part * cosines - sine_part * sines], axis=-2)
    return turned.reshape(spread.shape)

def turn_key(spread, sines, cosines):
    pieces = spread.reshape(spread.shape[:-1] + (2, 2, sines.shape[-1]))
    sine_part = pieces[..., 0, :]
    cosine_part = pieces[..., 1, :]
    turned = jnp.stack([sine_part * sines + cosine_part * cosines, cosine_part * sines - sine_part * cosines], axis=-2)
    return turned.reshape(spread.shape)

def layer_norm(values, gain, shift):
    centred = values - lax.optimization_barrier(jnp.mean(values, axis=-1, keepdims=True))
    spread = lax.optimization_barrier(jnp.mean(centred * centred, axis=-1, keepdims=True))
    return centred * lax.rsqrt(spread + 1e-05) * gain + shift

def split_heads(values):
    return values.reshape(values.shape[0], HEADS, HD).transpose(1, 0, 2)

def page_layer(tokens, sines, cosines, key_alive, weights):
    query_weight, keys_weight, values_weight, output_weight, query_place, keys_place, inner_weight, outer_weight, query_bias, keys_bias, values_bias, output_bias, inner_bias, outer_bias, first_gain, first_shift, second_gain, second_shift = weights
    length = tokens.shape[0]
    queries = low_back(low(jnp.dot(tokens, query_weight, precision=finest) + query_bias))
    keys_all = low_back(low(jnp.dot(tokens, keys_weight, precision=finest) + keys_bias))
    values_all = low_back(low(jnp.dot(tokens, values_weight, precision=finest) + values_bias))
    key_feats = low(features(sines, cosines))
    query_feats = low(features(cosines, sines))
    heads_q = split_heads(queries)
    heads_k = split_heads(keys_all)
    heads_v = split_heads(values_all)
    spread_q = low_back(jnp.einsum('hld,hde->hle', heads_q, query_place.reshape(HEADS, HD, -1), precision=finest))
    turned_q = low(turn_query(spread_q, sines, cosines))
    spread_k = jnp.einsum('hld,hde->hle', heads_k, keys_place.reshape(HEADS, HD, -1), precision=finest)
    turned_k = low(turn_key(spread_k, sines, cosines))
    raw = jnp.einsum('hqd,hkd->hqk', heads_q, heads_k, precision=finest)
    raw = raw + jnp.einsum('hqe,ke->hqk', turned_q, key_feats, precision=finest)
    raw = raw + jnp.einsum('qe,hke->hqk', query_feats, turned_k, precision=finest)
    raw = low_back(raw)
    scores = jnp.where(key_alive[None, None, :], raw * (3.0 * HD) ** (-0.5), -1e+30)
    attend = low(jax.nn.softmax(scores, axis=-1))
    context = jnp.einsum('hqk,hkd->qhd', attend, heads_v, precision=finest).reshape(length, HEADS * HD)
    context = low_back(low(context))
    branch = low_back(jnp.dot(context, output_weight, precision=finest) + output_bias)
    first = layer_norm(tokens + branch, first_gain, first_shift)
    inner = low_back(jnp.dot(low(first), inner_weight, precision=finest) + inner_bias)
    activated = low(jax.nn.gelu(inner, approximate=False))
    outer = low_back(jnp.dot(activated, outer_weight, precision=finest) + outer_bias)
    return layer_norm(first + outer, second_gain, second_shift)

def reference(tokens, cotangent, boxes, resolution, padding, query_weight, keys_weight, values_weight, output_weight, query_place, keys_place, inner_weight, outer_weight, query_bias, keys_bias, values_bias, output_bias, inner_bias, outer_bias, first_gain, first_shift, second_gain, second_shift):
    sines, cosines = trig_of(boxes, resolution)
    key_alive = padding == 1
    params = (query_weight, keys_weight, values_weight, output_weight, query_place, keys_place, inner_weight, outer_weight, query_bias, keys_bias, values_bias, output_bias, inner_bias, outer_bias, first_gain, first_shift, second_gain, second_shift)
    params = tuple((item.astype(jnp.float32) for item in params))
    group_count = PAGES // PAGES_DEV

    def regroup(values):
        return values.reshape((group_count, PAGES_DEV) + values.shape[1:])

    def whole(tokens_f, weights):

        def one_group(item_set):
            part_tokens, part_sines, part_cosines, part_alive = item_set

            def single(tokens_row, sines_row, cosines_row, alive_row):
                return page_layer(tokens_row, sines_row, cosines_row, alive_row, weights)
            return jax.vmap(single)(part_tokens, part_sines, part_cosines, part_alive)
        results = lax.map(jax.checkpoint(one_group), (regroup(tokens_f), regroup(sines), regroup(cosines), regroup(key_alive)))
        return results.reshape(tokens_f.shape)
    output, pullback = jax.vjp(whole, tokens.astype(jnp.float32), params)
    tokens_grad, grads = pullback(cotangent.astype(jnp.float32))
    return (output.astype(jnp.bfloat16), tokens_grad, grads[0], grads[1], grads[2], grads[3], grads[4], grads[5], grads[6], grads[7], grads[8], grads[9], grads[10], grads[11], grads[12], grads[13], grads[14], grads[15], grads[16], grads[17])
```

```python
import functools
import math

import jax
import jax.numpy as jnp
from jax import lax
from jax.experimental import pallas as pl
from jax.experimental.pallas import tpu as pltpu
from jax.sharding import PartitionSpec as P

HEADS = 12
HD = 64
FREQ = 192
D = HEADS * HD
SPAN = 2 * FREQ
LOW = jnp.bfloat16
WIDE = jnp.float32
AXES = ("page", "pb")


def dot(a, b):
    return jnp.dot(a, b, preferred_element_type=WIDE)


def dot_nt(a, b):
    return lax.dot_general(a, b, (((1,), (1,)), ((), ())), preferred_element_type=WIDE)


def dot_tn(a, b):
    return lax.dot_general(a, b, (((0,), (0,)), ((), ())), preferred_element_type=WIDE)


def attend_kernel(heads, tok_ref, w_ref, bias_ref, pq_ref, pk_ref, sin_ref, cos_ref, alive_ref,
                  qkv_ref, soft_ref, ctx_ref):
    blocks, rows = tok_ref.shape[0], tok_ref.shape[2]
    count = blocks * rows
    width = heads * HD
    tok = tok_ref[...].reshape(count, D)
    sines, cosines = sin_ref[0], cos_ref[0]
    sines_low, cosines_low = sines.astype(LOW), cosines.astype(LOW)
    key_feats = jnp.concatenate([sines_low, cosines_low], axis=1)
    query_feats = jnp.concatenate([cosines_low, sines_low], axis=1)
    alive = alive_ref[0] > 0
    qkv = (dot(tok, w_ref[...]) + bias_ref[...]).astype(LOW)
    qkv_ref[0] = qkv
    scaling = (3.0 * HD) ** (-0.5)
    pieces = []
    for h in range(heads):
        q = qkv[:, h * HD:(h + 1) * HD]
        k = qkv[:, width + h * HD:width + (h + 1) * HD]
        v = qkv[:, 2 * width + h * HD:2 * width + (h + 1) * HD]
        spread = dot(q, pq_ref[h])
        s, c = spread[:, :SPAN], spread[:, SPAN:]
        turned_q = jnp.concatenate(
            [(s * cosines + c * sines).astype(LOW), (c * cosines - s * sines).astype(LOW)], axis=1)
        spread = dot(k, pk_ref[h])
        s, c = spread[:, :SPAN], spread[:, SPAN:]
        turned_k = jnp.concatenate(
            [(s * sines + c * cosines).astype(LOW), (c * sines - s * cosines).astype(LOW)], axis=1)
        raw = dot_nt(q, k) + dot_nt(turned_q, key_feats) + dot_nt(query_feats, turned_k)
        scores = jnp.where(alive, raw * scaling, -1e30)
        lifted = jnp.exp(scores - jnp.max(scores, axis=1, keepdims=True))
        soft = (lifted / jnp.sum(lifted, axis=1, keepdims=True)).astype(LOW)
        soft_ref[0, h] = soft
        pieces.append(dot(soft, v).astype(LOW))
    ctx = jnp.concatenate(pieces, axis=1)
    ctx_ref[...] = ctx.reshape(blocks, 1, rows, width)


def attend_call(tok_all, w_qkv, bias, place_q, place_k, sines, cosines, alive):
    blocks, pages, rows, _ = tok_all.shape
    heads = place_q.shape[0]
    width = heads * HD
    count = blocks * rows
    const = lambda shape: pl.BlockSpec(shape, lambda p: (0,) * len(shape))
    return pl.pallas_call(
        functools.partial(attend_kernel, heads),
        grid=(pages,),
        in_specs=[
            pl.BlockSpec((blocks, 1, rows, D), lambda p: (0, p, 0, 0)),
            const((D, 3 * width)),
            const((1, 3 * width)),
            const((heads, HD, 2 * SPAN)),
            const((heads, HD, 2 * SPAN)),
            pl.BlockSpec((1, count, SPAN), lambda p: (p, 0, 0)),
            pl.BlockSpec((1, count, SPAN), lambda p: (p, 0, 0)),
            pl.BlockSpec((1, 1, count), lambda p: (p, 0, 0)),
        ],
        out_specs=[
            pl.BlockSpec((1, count, 3 * width), lambda p: (p, 0, 0)),
            pl.BlockSpec((1, heads, count, count), lambda p: (p, 0, 0, 0)),
            pl.BlockSpec((blocks, 1, rows, width), lambda p: (0, p, 0, 0)),
        ],
        out_shape=[
            jax.ShapeDtypeStruct((pages, count, 3 * width), LOW),
            jax.ShapeDtypeStruct((pages, heads, count, count), LOW),
            jax.ShapeDtypeStruct((blocks, pages, rows, width), LOW),
        ],
        compiler_params=pltpu.CompilerParams(vmem_limit_bytes=56 * 1024 * 1024),
        name="attend",
    )(tok_all, w_qkv, bias, place_q, place_k, sines, cosines, alive)


def attend_back_kernel(heads, qkv_ref, soft_ref, dctx_ref, pq_ref, pk_ref, sin_ref, cos_ref,
                       dqkv_ref, dpq_ref, dpk_ref):
    blocks, rows = dctx_ref.shape[0], dctx_ref.shape[2]
    count = blocks * rows
    width = heads * HD
    sines, cosines = sin_ref[0], cos_ref[0]
    sines_low, cosines_low = sines.astype(LOW), cosines.astype(LOW)
    key_feats = jnp.concatenate([sines_low, cosines_low], axis=1)
    query_feats = jnp.concatenate([cosines_low, sines_low], axis=1)
    qkv = qkv_ref[0]
    dctx = dctx_ref[...].reshape(count, width)
    scaling = (3.0 * HD) ** (-0.5)

    @pl.when(pl.program_id(0) == 0)
    def _():
        dpq_ref[...] = jnp.zeros_like(dpq_ref)
        dpk_ref[...] = jnp.zeros_like(dpk_ref)

    d_q, d_k, d_v = [], [], []
    for h in range(heads):
        q = qkv[:, h * HD:(h + 1) * HD]
        k = qkv[:, width + h * HD:width + (h + 1) * HD]
        v = qkv[:, 2 * width + h * HD:2 * width + (h + 1) * HD]
        dc = dctx[:, h * HD:(h + 1) * HD]
        soft = soft_ref[0, h]
        soft_wide = soft.astype(WIDE)
        attend_grad = dot_nt(dc, v)
        row_dot = jnp.sum(soft_wide * attend_grad, axis=1, keepdims=True)
        raw_grad = (soft_wide * (attend_grad - row_dot) * scaling).astype(LOW)
        d_v.append(dot_tn(soft, dc).astype(LOW))
        turned = dot(raw_grad, key_feats)
        s, c = turned[:, :SPAN], turned[:, SPAN:]
        spread_q = jnp.concatenate(
            [(s * cosines - c * sines).astype(LOW), (s * sines + c * cosines).astype(LOW)], axis=1)
        d_q.append((dot(raw_grad, k) + dot_nt(spread_q, pq_ref[h])).astype(LOW))
        dpq_ref[h] += dot_tn(q, spread_q)
        turned = dot_tn(raw_grad, query_feats)
        s, c = turned[:, :SPAN], turned[:, SPAN:]
        spread_k = jnp.concatenate(
            [(s * sines - c * cosines).astype(LOW), (s * cosines + c * sines).astype(LOW)], axis=1)
        d_k.append((dot_tn(raw_grad, q) + dot_nt(spread_k, pk_ref[h])).astype(LOW))
        dpk_ref[h] += dot_tn(k, spread_k)
    dqkv_ref[0] = jnp.concatenate(d_q + d_k + d_v, axis=1)


def attend_back_call(qkv, soft, dctx, place_q, place_k, sines, cosines):
    blocks, pages, rows, width = dctx.shape
    heads = place_q.shape[0]
    count = blocks * rows
    const = lambda shape: pl.BlockSpec(shape, lambda p: (0,) * len(shape))
    return pl.pallas_call(
        functools.partial(attend_back_kernel, heads),
        grid=(pages,),
        in_specs=[
            pl.BlockSpec((1, count, 3 * width), lambda p: (p, 0, 0)),
            pl.BlockSpec((1, heads, count, count), lambda p: (p, 0, 0, 0)),
            pl.BlockSpec((blocks, 1, rows, width), lambda p: (0, p, 0, 0)),
            const((heads, HD, 2 * SPAN)),
            const((heads, HD, 2 * SPAN)),
            pl.BlockSpec((1, count, SPAN), lambda p: (p, 0, 0)),
            pl.BlockSpec((1, count, SPAN), lambda p: (p, 0, 0)),
        ],
        out_specs=[
            pl.BlockSpec((1, count, 3 * width), lambda p: (p, 0, 0)),
            const((heads, HD, 2 * SPAN)),
            const((heads, HD, 2 * SPAN)),
        ],
        out_shape=[
            jax.ShapeDtypeStruct((pages, count, 3 * width), LOW),
            jax.ShapeDtypeStruct((heads, HD, 2 * SPAN), WIDE),
            jax.ShapeDtypeStruct((heads, HD, 2 * SPAN), WIDE),
        ],
        compiler_params=pltpu.CompilerParams(vmem_limit_bytes=56 * 1024 * 1024),
        name="attend_back",
    )(qkv, soft, dctx, place_q, place_k, sines, cosines)


def swap(value, axis, size, bit):
    return lax.ppermute(value, axis, [(i, i ^ bit) for i in range(size)])


def gather_pb(value, size):
    if size != 4:
        return lax.all_gather(value, "pb", axis=0)
    me = lax.axis_index("pb")
    far = swap(value, "pb", 4, 2)
    near = swap(value, "pb", 4, 1)
    corner = swap(far, "pb", 4, 1)
    out = jnp.zeros((4,) + value.shape, value.dtype)
    for j, piece in enumerate((value, near, far, corner)):
        out = lax.dynamic_update_index_in_dim(out, piece, me ^ j, 0)
    return out


def gather_page(value, size):
    if size != 8:
        return lax.all_gather(value, "page", axis=0)
    me = lax.axis_index("page")
    out = jnp.zeros((8,) + value.shape, value.dtype)
    out = lax.dynamic_update_index_in_dim(out, value, me, 0)
    for step in (2, 4, 6):
        piece = swap(value, "page", 8, step)
        out = lax.dynamic_update_index_in_dim(out, piece, me ^ step, 0)
    mine = out.reshape((4, 2) + value.shape)
    half = me & 1
    mine = lax.dynamic_index_in_dim(mine, half, 1, keepdims=False)
    other = swap(mine, "page", 8, 1)
    both = jnp.zeros((4, 2) + value.shape, value.dtype)
    both = lax.dynamic_update_slice_in_dim(both, mine[:, None], half, 1)
    both = lax.dynamic_update_slice_in_dim(both, other[:, None], 1 - half, 1)
    return both.reshape((8,) + value.shape)


def transpose_roles(value, pages, size):
    inner = pages // size
    pairs = []
    for hi in range(size):
        for lo in range(inner):
            for b in range(size):
                pairs.append(((hi * inner + lo) * size + b, (b * inner + lo) * size + hi))
    return lax.ppermute(value, AXES, pairs)


def scatter_pb(partial, size):
    if size != 4:
        moved = lax.all_to_all(partial.astype(LOW), "pb", 0, 0, tiled=True)
        return jnp.sum(moved.astype(WIDE), axis=0)
    me = lax.axis_index("pb")
    core, row = me & 1, me >> 1
    cut = partial.reshape((2, 2) + partial.shape[1:])
    kept = lax.dynamic_index_in_dim(cut, core, 1, keepdims=False)
    sent = lax.dynamic_index_in_dim(cut, 1 - core, 1, keepdims=False)
    total = kept.astype(WIDE) + swap(sent.astype(LOW), "pb", 4, 1).astype(WIDE)
    kept = lax.dynamic_index_in_dim(total, row, 0, keepdims=False)
    sent = lax.dynamic_index_in_dim(total, 1 - row, 0, keepdims=False)
    return kept + swap(sent.astype(LOW), "pb", 4, 2).astype(WIDE)


def layer_norm(values, gain, shift):
    centred = values - jnp.mean(values, axis=-1, keepdims=True)
    spread = jnp.mean(centred * centred, axis=-1, keepdims=True)
    return centred * lax.rsqrt(spread + 1e-05) * gain + shift


def exact_gelu(values):
    return jax.nn.gelu(values, approximate=False)


def summed_rows(gradient):
    return jnp.sum(gradient.astype(WIDE), axis=0)


def to_halves(place):
    cut = place.reshape(place.shape[:-1] + (2, 2, FREQ))
    return jnp.swapaxes(cut, -3, -2).reshape(place.shape)


def on_device(sizes, tokens, cotangent, boxes, resolution, padding,
              query_weight, keys_weight, values_weight, output_weight, query_place, keys_place,
              inner_weight, outer_weight, query_bias, keys_bias, values_bias, output_bias,
              inner_bias, outer_bias, first_gain, first_shift, second_gain, second_shift):
    page_size, pb_size = sizes
    devices = page_size * pb_size
    pages, rows, _ = tokens.shape
    count = rows * pb_size
    heads = HEADS // pb_size
    width = heads * HD
    own = query_weight.shape[0]
    ff_own = outer_weight.shape[0]
    ff = ff_own * devices
    ff_cuts = ff // D

    small = [output_bias, inner_bias, outer_bias, first_gain, first_shift, second_gain, second_shift]
    lengths = [s.shape[0] for s in small]
    small_row = jnp.concatenate(small)
    small_rows = 8
    small_row = jnp.pad(small_row, (0, small_rows * D - small_row.shape[0])).reshape(small_rows, D)
    packed = jnp.concatenate(
        [output_weight]
        + [inner_weight[:, j * D:(j + 1) * D] for j in range(ff_cuts)]
        + [outer_weight, small_row], axis=0)
    late = lax.all_gather(packed, AXES, axis=0)

    tok_all = gather_pb(tokens, pb_size)
    grid_x = (boxes[0] + boxes[2]) * 500 // resolution[0][:, None]
    grid_y = (boxes[1] + boxes[3]) * 500 // resolution[1][:, None]
    places = gather_pb(jnp.stack([grid_x, grid_y, padding]), pb_size)
    places = places.transpose(1, 2, 0, 3).reshape(3, pages, count)
    rates = jnp.exp(jnp.arange(FREQ).astype(WIDE) * (-math.log(10000.0) / FREQ))
    grids = places[:2].astype(WIDE)
    angles = jnp.concatenate(
        [grids[0][..., None] * rates, grids[1][..., None] * rates], axis=-1)
    sines, cosines = jnp.sin(angles), jnp.cos(angles)
    alive = places[2][:, None, :]

    cols = jnp.stack([query_weight, keys_weight, values_weight]).reshape(3, own, pb_size, width)
    cols = cols.transpose(2, 1, 0, 3).reshape(pb_size, own, 3 * width)
    cols = lax.all_to_all(cols, "pb", 0, 0, tiled=True)
    w_qkv = gather_page(cols, page_size).reshape(D, 3 * width)
    bias_row = jnp.concatenate([query_bias, keys_bias, values_bias])
    bias_row = jnp.pad(bias_row, (0, 8 * D - bias_row.shape[0])).reshape(8, D)
    mixed = jnp.concatenate([to_halves(query_place), to_halves(keys_place), bias_row], axis=0)
    mixed = gather_page(transpose_roles(mixed, page_size, pb_size), page_size)
    inner_pages = page_size // pb_size
    mixed = mixed.reshape((pb_size, inner_pages) + mixed.shape[1:]).swapaxes(0, 1)
    mixed = mixed.reshape((page_size,) + mixed.shape[2:])
    place_q = mixed[:, :own].reshape(heads, HD, 2 * SPAN)
    place_k = mixed[:, own:2 * own].reshape(heads, HD, 2 * SPAN)
    bias_qkv = mixed[:, 2 * own, :3 * own].reshape(page_size, 3, own).swapaxes(0, 1)
    bias_qkv = bias_qkv.reshape(1, 3 * width).astype(WIDE)

    qkv, soft, ctx_heads = attend_call(
        tok_all, w_qkv, bias_qkv, place_q, place_k, sines, cosines, alive)

    ctx = lax.all_to_all(ctx_heads, "pb", 0, 0, tiled=True)
    context = ctx.transpose(1, 2, 0, 3).reshape(pages * rows, D)

    at = 0
    matrix_output = late[:, :own].reshape(D, D)
    at = own
    matrix_inner = jnp.concatenate(
        [late[:, at + j * own:at + (j + 1) * own].reshape(D, D) for j in range(ff_cuts)], axis=1)
    at += own * ff_cuts
    matrix_outer = late[:, at:at + ff_own].reshape(ff, D)
    at += ff_own
    flat = late[:, at:].reshape(devices, small_rows * D)
    vectors, at = [], 0
    for length in lengths:
        vectors.append(flat[:, at:at + length].reshape(devices * length).astype(WIDE))
        at += length
    offset_output, offset_inner, offset_outer, gain_one, shift_one, gain_two, shift_two = vectors

    tok = tokens.reshape(pages * rows, D)
    pre_one = tok.astype(WIDE) + (dot(context, matrix_output) + offset_output)
    first, first_back = jax.vjp(layer_norm, pre_one, gain_one, shift_one)
    first_low = first.astype(LOW)
    inner = dot(first_low, matrix_inner) + offset_inner
    activated, gelu_back = jax.vjp(exact_gelu, inner)
    activated = activated.astype(LOW)
    pre_two = first + (dot(activated, matrix_outer) + offset_outer)
    output, second_back = jax.vjp(layer_norm, pre_two, gain_two, shift_two)
    pre_two_grad, gain_two_grad, shift_two_grad = second_back(
        cotangent.reshape(pages * rows, D).astype(WIDE))
    outer_grad = pre_two_grad.astype(LOW)
    outer_weight_grad = dot_tn(activated, outer_grad)
    inner_grad = gelu_back(dot_nt(outer_grad, matrix_outer))[0].astype(LOW)
    inner_weight_grad = dot_tn(first_low, inner_grad)
    first_grad = pre_two_grad + dot_nt(inner_grad, matrix_inner)
    pre_one_grad, gain_one_grad, shift_one_grad = first_back(first_grad)
    branch_grad = pre_one_grad.astype(LOW)
    output_weight_grad = dot_tn(context, branch_grad)
    context_grad = dot_nt(branch_grad, matrix_output).astype(LOW)

    small_grads = [summed_rows(branch_grad), summed_rows(inner_grad), summed_rows(outer_grad),
                   gain_one_grad, shift_one_grad, gain_two_grad, shift_two_grad]
    small_grads = jnp.concatenate([g.reshape(devices, -1) for g in small_grads], axis=1)
    small_grads = jnp.pad(small_grads, ((0, 0), (0, small_rows * D - small_grads.shape[1])))
    packed_grads = jnp.concatenate(
        [output_weight_grad.astype(LOW).reshape(devices, own, D)]
        + [inner_weight_grad[:, j * D:(j + 1) * D].astype(LOW).reshape(devices, own, D)
           for j in range(ff_cuts)]
        + [outer_weight_grad.astype(LOW).reshape(devices, ff_own, D),
           small_grads.astype(LOW).reshape(devices, small_rows, D)], axis=1)
    late_sum = lax.psum_scatter(packed_grads, AXES, scatter_dimension=0, tiled=False)
    late_sum = late_sum.astype(WIDE)

    dctx = context_grad.reshape(pages, rows, pb_size, width).transpose(2, 0, 1, 3)
    dctx = lax.all_to_all(dctx, "pb", 0, 0, tiled=True)
    dqkv, dpq, dpk = attend_back_call(qkv, soft, dctx, place_q, place_k, sines, cosines)

    dqkv_flat = dqkv.reshape(pages, pb_size, rows, 3 * width)
    partial = jnp.einsum("pbne,de->bpnd", dqkv_flat, w_qkv, preferred_element_type=WIDE)
    tokens_grad = pre_one_grad.reshape(pages, rows, D) + scatter_pb(partial, pb_size)
    d_w = jnp.einsum("bpnd,pbne->de", tok_all, dqkv_flat, preferred_element_type=WIDE)
    d_bias = jnp.sum(dqkv.astype(WIDE), axis=(0, 1))

    d_w = d_w.astype(LOW).reshape(page_size, pb_size * own * 3 * width)
    d_mixed = jnp.stack([dpq.reshape(page_size, own, D), dpk.reshape(page_size, own, D)], axis=1)
    d_mixed = d_mixed.astype(LOW).reshape(page_size, 2 * own * D)
    d_bias = d_bias.astype(LOW).reshape(3, page_size, own).swapaxes(0, 1).reshape(page_size, 3 * own)
    d_mixed = jnp.concatenate([d_mixed, d_bias], axis=1)
    d_mixed = d_mixed.reshape((inner_pages, pb_size) + d_mixed.shape[1:]).swapaxes(0, 1)
    d_mixed = d_mixed.reshape((page_size,) + d_mixed.shape[2:])
    joined = jnp.concatenate([d_w, d_mixed], axis=1)
    total = joined.shape[1]
    padded = -total % (8 * 128)
    joined = jnp.pad(joined, ((0, 0), (0, padded))).reshape(page_size, -1, 128)
    joined = lax.all_to_all(joined, "page", 0, 0, tiled=True)
    joined = jnp.sum(joined.astype(WIDE), axis=0).reshape(-1)
    cut = pb_size * own * 3 * width
    d_cols = joined[:cut].astype(LOW).reshape(pb_size, own, 3 * width)
    d_cols = lax.all_to_all(d_cols, "pb", 0, 0, tiled=True).astype(WIDE)
    d_cols = d_cols.reshape(pb_size, own, 3, width).transpose(2, 1, 0, 3).reshape(3, own, D)
    d_mixed = transpose_roles(joined[cut:cut + 2 * own * D + 3 * own], page_size, pb_size)
    d_places = to_halves(d_mixed[:2 * own * D].reshape(2, own, D))
    d_bias = d_mixed[2 * own * D:].reshape(3, own)

    at = own * (1 + ff_cuts)
    small_sum = late_sum[at + ff_own:].reshape(-1)
    vectors, cursor = [], 0
    for length in lengths:
        vectors.append(small_sum[cursor:cursor + length])
        cursor += length
    return (
        output.astype(LOW).reshape(pages, rows, D),
        tokens_grad,
        d_cols[0], d_cols[1], d_cols[2],
        late_sum[:own],
        d_places[0], d_places[1],
        jnp.concatenate([late_sum[own * (1 + j):own * (2 + j)] for j in range(ff_cuts)], axis=1),
        late_sum[at:at + ff_own],
        d_bias[0], d_bias[1], d_bias[2],
        *vectors,
    )


def solution(mesh):
    rows, vector = P(AXES, None), P(AXES)
    token = P("page", "pb", None)
    in_specs = (token, token, P(None, "page", "pb"), P(None, "page"), P("page", "pb"))
    in_specs = in_specs + (rows,) * 8 + (vector,) * 10
    out_specs = (token, token) + (rows,) * 8 + (vector,) * 10
    sizes = (mesh.shape["page"], mesh.shape["pb"])
    return jax.shard_map(
        functools.partial(on_device, sizes), mesh=mesh, in_specs=in_specs, out_specs=out_specs,
        check_vma=False)
```

```python
import functools
import math

import jax
import jax.numpy as jnp
from jax import lax
from jax.experimental import pallas as pl
from jax.experimental.pallas import tpu as pltpu
from jax.sharding import PartitionSpec as P

HEADS = 12
HD = 64
FREQ = 192
D = HEADS * HD
SPAN = 2 * FREQ
SCALING = (3.0 * HD) ** (-0.5)
LOW = jnp.bfloat16
WIDE = jnp.float32
AXES = ("page", "pb")
VMEM_BYTES = 56 * 1024 * 1024


def dot(a, b):
    return jnp.dot(a, b, preferred_element_type=WIDE)


def dot_nt(a, b):
    return lax.dot_general(a, b, (((1,), (1,)), ((), ())), preferred_element_type=WIDE)


def dot_tn(a, b):
    return lax.dot_general(a, b, (((0,), (0,)), ((), ())), preferred_element_type=WIDE)


def whole(shape):
    return pl.BlockSpec(shape, lambda i, *_: (0,) * len(shape))


def cost(flops, bytes_accessed):
    return pl.CostEstimate(flops=int(flops), bytes_accessed=int(bytes_accessed), transcendentals=0)


def lanes_to(rows, length, start):
    lane = lax.broadcasted_iota(jnp.int32, rows.shape, 1)
    rows = jnp.where(lane < length, rows, 0.0)
    padded = jnp.concatenate([rows, jnp.zeros((rows.shape[0], D - rows.shape[1]), WIDE)], axis=1)
    return pltpu.roll(padded, start, 1)


def halves(place):
    cut = [place[:, i * FREQ:(i + 1) * FREQ] for i in (0, 2, 1, 3)]
    return jnp.concatenate(cut, axis=1)


def pack_kernel(size, at_ref, vec_ref, wq_ref, wk_ref, wv_ref, pq_ref, pk_ref, wo_ref, wi_ref, wu_ref,
                late_ref, cols_ref, mixed_ref):
    number, place_at = at_ref[3], at_ref[4]
    own, ff_own = wq_ref.shape[0], wu_ref.shape[0]
    cuts = wi_ref.shape[1] // D
    width = D // size
    vectors = vec_ref[...]
    lanes = lanes_to(vectors[:8], own, number * own)
    row = lax.broadcasted_iota(jnp.int32, lanes.shape, 0)
    first = jnp.where(row < 6, lanes, 0.0)
    inner = lanes_to(vectors[8:16], ff_own, lax.rem(number, D // ff_own) * ff_own)
    spot = lax.div(number, D // ff_own)
    for j in range(cuts):
        hit = (row == (6 + j) % 8) & (spot == j)
        if 6 + j < 8:
            first = first + jnp.where(hit, pltpu.roll(inner, 6 + j, 0), 0.0)
    second = jnp.zeros_like(first)
    for j in range(2, cuts):
        hit = (row == j - 2) & (spot == j)
        second = second + jnp.where(hit, pltpu.roll(inner, j - 2, 0), 0.0)
    wi = wi_ref[...].astype(WIDE)
    late = [wu_ref[...].astype(WIDE)] + [wi[:, j * D:(j + 1) * D] for j in range(cuts)]
    late += [first, second, wo_ref[...].astype(WIDE)]
    late_ref[...] = jnp.concatenate(late, axis=0).astype(LOW)
    cols = jnp.concatenate([ref[...].astype(WIDE) for ref in (wq_ref, wk_ref, wv_ref)], axis=0)
    for b in range(size):
        cols_ref[b] = cols[:, b * width:(b + 1) * width].astype(LOW)
    lanes = lanes_to(vectors[16:24], own, place_at * own)
    bias = jnp.concatenate(
        [lanes[i:i + 1, :width] for i in range(3)] + [jnp.zeros((1, D - 3 * width), WIDE)], axis=1)
    bias = jnp.concatenate([bias, jnp.zeros((7, D), WIDE)], axis=0)
    places = [halves(pq_ref[...].astype(WIDE)), halves(pk_ref[...].astype(WIDE)), bias]
    mixed_ref[...] = jnp.concatenate(places, axis=0).astype(LOW)


def pack_call(at, vectors, *weights):
    own, ff_own = weights[0].shape[0], weights[-1].shape[0]
    size = 4
    rows = ff_own + weights[-2].shape[1] // D * own + 16 + own
    return pl.pallas_call(
        functools.partial(pack_kernel, size),
        out_shape=[
            jax.ShapeDtypeStruct((rows, D), LOW),
            jax.ShapeDtypeStruct((size, 3 * own, D // size), LOW),
            jax.ShapeDtypeStruct((2 * own + 8, D), LOW),
        ],
        in_specs=[pl.BlockSpec(memory_space=pltpu.SMEM)]
        + [pl.BlockSpec(memory_space=pltpu.VMEM)] * (1 + len(weights)),
        compiler_params=pltpu.CompilerParams(vmem_limit_bytes=VMEM_BYTES),
        name="pack",
    )(at, vectors, *weights)


def finish_kernel(cols_ref, mixed_ref, *out_refs):
    own = out_refs[0].shape[0]
    cols = [cols_ref[b].astype(WIDE) for b in range(cols_ref.shape[0])]
    for i in range(3):
        out_refs[i][...] = jnp.concatenate([c[i * own:(i + 1) * own] for c in cols], axis=1)
    mixed = mixed_ref[...].astype(WIDE)
    for i in range(2):
        out_refs[3 + i][...] = halves(mixed[i * own:(i + 1) * own])


def finish_call(cols, mixed):
    own = cols.shape[1] // 3
    return pl.pallas_call(
        finish_kernel,
        out_shape=[jax.ShapeDtypeStruct((own, D), WIDE)] * 5,
        compiler_params=pltpu.CompilerParams(vmem_limit_bytes=VMEM_BYTES),
        name="finish",
    )(cols, mixed)


def assemble_kernel(own, size, at_ref, mine_ref, theirs_ref, w_ref, pq_ref, pk_ref, bias_ref, got):
    pages = got.shape[0]
    inner = pages // size
    width = D // size
    even = (at_ref[1] >> 1) == 0
    for z in range(pages // 2):
        mine, theirs = mine_ref[at_ref[2] ^ z].astype(WIDE), theirs_ref[at_ref[2] ^ z].astype(WIDE)
        got[2 * z] = jnp.where(even, mine, theirs)
        got[2 * z + 1] = jnp.where(even, theirs, mine)
    columns = []
    for part in range(3):
        rows = got[:, pl.ds(part * own, own)]
        cut = [rows[:, :, b * width:(b + 1) * width][:, None] for b in range(size)]
        columns.append(jnp.concatenate(cut, axis=1).reshape(D, width))
    w_ref[...] = jnp.concatenate(columns, axis=1).astype(LOW)
    for start, ref in ((3 * own, pq_ref), (4 * own, pk_ref)):
        order = [b * inner + lo for lo in range(inner) for b in range(size)]
        rows = jnp.concatenate([got[p, pl.ds(start, own)] for p in order], axis=0)
        ref[...] = rows.astype(LOW).reshape(ref.shape)
    bias_ref[...] = jnp.sum(got[:, pl.ds(5 * own, 8)], axis=0)[:1, :3 * width]


def assemble_call(at, mine, theirs, own, size):
    width = D // size
    place = (width // HD, HD, 2 * SPAN)
    return pl.pallas_call(
        functools.partial(assemble_kernel, own, size),
        out_shape=[
            jax.ShapeDtypeStruct((D, 3 * width), LOW),
            jax.ShapeDtypeStruct(place, LOW),
            jax.ShapeDtypeStruct(place, LOW),
            jax.ShapeDtypeStruct((1, 3 * width), WIDE),
        ],
        in_specs=[pl.BlockSpec(memory_space=pltpu.SMEM)] + [pl.BlockSpec(memory_space=pltpu.VMEM)] * 2,
        scratch_shapes=[pltpu.VMEM((2 * mine.shape[0],) + mine.shape[1:], WIDE)],
        compiler_params=pltpu.CompilerParams(vmem_limit_bytes=VMEM_BYTES),
        name="assemble",
    )(at, mine, theirs)


def turn(spread, left, right):
    s, c = spread[:, :SPAN], spread[:, SPAN:]
    return jnp.concatenate(
        [(s * left + c * right).astype(LOW), (c * left - s * right).astype(LOW)], axis=1)


def turn_back(gradient, left, right):
    s, c = gradient[:, :SPAN], gradient[:, SPAN:]
    return jnp.concatenate(
        [(s * left - c * right).astype(LOW), (s * right + c * left).astype(LOW)], axis=1)


def feature_pair(sines, cosines):
    sines, cosines = sines.astype(LOW), cosines.astype(LOW)
    return (jnp.concatenate([sines, cosines], axis=1), jnp.concatenate([cosines, sines], axis=1))


def attend_kernel(heads, blocks, me_ref, *refs):
    tok_refs = refs[:blocks]
    (w_ref, bias_ref, pq_ref, pk_ref, sin_ref, cos_ref, alive_ref,
     qkv_ref, soft_ref, ctx_ref) = refs[blocks:]
    me = me_ref[0]
    rows = tok_refs[0].shape[1]
    width = heads * HD
    tok = jnp.concatenate([ref[0] for ref in tok_refs], axis=0)
    sines, cosines = sin_ref[0], cos_ref[0]
    key_feats, query_feats = feature_pair(sines, cosines)
    alive = alive_ref[0] > 0
    qkv = (dot(tok, w_ref[...]) + bias_ref[...]).astype(LOW)
    qkv_ref[0] = qkv
    pieces = []
    for h in range(heads):
        q = qkv[:, h * HD:(h + 1) * HD]
        k = qkv[:, width + h * HD:width + (h + 1) * HD]
        v = qkv[:, 2 * width + h * HD:2 * width + (h + 1) * HD]
        turned_q = turn(dot(q, pq_ref[h]), cosines, sines)
        turned_k = turn(dot(k, pk_ref[h]), sines, cosines)
        raw = dot_nt(q, k) + dot_nt(turned_q, key_feats) + dot_nt(query_feats, turned_k)
        scores = jnp.where(alive, raw * SCALING, -1e30)
        lifted = jnp.exp(scores - jnp.max(scores, axis=1, keepdims=True))
        soft = (lifted / jnp.sum(lifted, axis=1, keepdims=True)).astype(LOW)
        soft_ref[0, h] = soft
        pieces.append(dot(soft, v).astype(LOW))
    ctx = jnp.concatenate(pieces, axis=1)
    for j in range(blocks):
        ctx_ref[me ^ j, 0] = ctx[j * rows:(j + 1) * rows]


def attend_call(me, toks, w_qkv, bias, place_q, place_k, sines, cosines, alive):
    blocks = len(toks)
    pages, rows, _ = toks[0].shape
    heads = place_q.shape[0]
    width = heads * HD
    count = blocks * rows
    by_page = lambda *shape: pl.BlockSpec((1,) + shape, lambda p, *_: (p,) + (0,) * len(shape))
    return pl.pallas_call(
        functools.partial(attend_kernel, heads, blocks),
        grid_spec=pltpu.PrefetchScalarGridSpec(
            num_scalar_prefetch=1,
            grid=(pages,),
            in_specs=[by_page(rows, D)] * blocks + [
                whole((D, 3 * width)), whole((1, 3 * width)),
                whole((heads, HD, 2 * SPAN)), whole((heads, HD, 2 * SPAN)),
                by_page(count, SPAN), by_page(count, SPAN), by_page(1, count)],
            out_specs=[
                by_page(count, 3 * width), by_page(heads, count, count),
                pl.BlockSpec((blocks, 1, rows, width), lambda p, *_: (0, p, 0, 0))],
        ),
        out_shape=[
            jax.ShapeDtypeStruct((pages, count, 3 * width), LOW),
            jax.ShapeDtypeStruct((pages, heads, count, count), LOW),
            jax.ShapeDtypeStruct((blocks, pages, rows, width), LOW),
        ],
        compiler_params=pltpu.CompilerParams(vmem_limit_bytes=VMEM_BYTES),
        cost_estimate=cost(20e9, 20e6),
        name="attend",
    )(me, *toks, w_qkv, bias, place_q, place_k, sines, cosines, alive)


def joined_grads(own, size, pages, d_w, d_pq, d_pk, d_bias):
    inner = pages // size
    width = D // size
    cut = d_w.reshape(pages, size, own, 3 * width)
    parts = []
    for part in range(3):
        parts.append(jnp.concatenate(
            [cut[:, b, :, part * width:(part + 1) * width] for b in range(size)], axis=2))
    for place in (d_pq, d_pk):
        place = place.reshape(D // size, 2 * SPAN)
        order = [(lo * size + b) * own for b in range(size) for lo in range(inner)]
        parts.append(jnp.concatenate([place[at:at + own][None] for at in order], axis=0))
    row = jnp.concatenate([d_bias, jnp.zeros((1, D - 3 * width), WIDE)], axis=1)
    parts.append(jnp.broadcast_to(row[None], (pages, 8, D)))
    return jnp.concatenate(parts, axis=1).astype(LOW)


def attend_back_kernel(heads, blocks, joined, me_ref, *refs):
    tok_refs = refs[:blocks]
    (w_ref, qkv_ref, soft_ref, dctx_ref, pq_ref, pk_ref, sin_ref, cos_ref,
     part_ref, *out_refs, dw_sum, dpq_sum, dpk_sum, db_sum) = refs[blocks:]
    me = me_ref[0]
    step, last = pl.program_id(0), pl.num_programs(0) - 1
    rows = tok_refs[0].shape[1]
    width = heads * HD
    sines, cosines = sin_ref[0], cos_ref[0]
    key_feats, query_feats = feature_pair(sines, cosines)
    qkv = qkv_ref[0]
    dctx = jnp.concatenate([dctx_ref[me ^ j, 0] for j in range(blocks)], axis=0)

    @pl.when(step == 0)
    def _():
        for ref in (dw_sum, dpq_sum, dpk_sum, db_sum):
            ref[...] = jnp.zeros_like(ref)

    d_q, d_k, d_v = [], [], []
    for h in range(heads):
        q = qkv[:, h * HD:(h + 1) * HD]
        k = qkv[:, width + h * HD:width + (h + 1) * HD]
        v = qkv[:, 2 * width + h * HD:2 * width + (h + 1) * HD]
        dc = dctx[:, h * HD:(h + 1) * HD]
        soft = soft_ref[0, h]
        soft_wide = soft.astype(WIDE)
        attend_grad = dot_nt(dc, v)
        row_dot = jnp.sum(soft_wide * attend_grad, axis=1, keepdims=True)
        raw_grad = (soft_wide * (attend_grad - row_dot) * SCALING).astype(LOW)
        d_v.append(dot_tn(soft, dc).astype(LOW))
        spread_q = turn_back(dot(raw_grad, key_feats), cosines, sines)
        d_q.append((dot(raw_grad, k) + dot_nt(spread_q, pq_ref[h])).astype(LOW))
        dpq_sum[h] += dot_tn(q, spread_q)
        spread_k = turn_back(dot_tn(raw_grad, query_feats), sines, cosines)
        d_k.append((dot_tn(raw_grad, q) + dot_nt(spread_k, pk_ref[h])).astype(LOW))
        dpk_sum[h] += dot_tn(k, spread_k)
    dqkv = jnp.concatenate(d_q + d_k + d_v, axis=1)
    db_sum[...] += jnp.sum(dqkv.astype(WIDE), axis=0, keepdims=True)
    tok = jnp.concatenate([ref[0] for ref in tok_refs], axis=0)
    dw_sum[...] += dot_tn(tok, dqkv)
    part = dot_nt(dqkv, w_ref[...]).astype(LOW)
    for j in range(blocks):
        part_ref[j, 0] = part[j * rows:(j + 1) * rows]

    @pl.when(step == last)
    def _():
        if joined:
            rows = joined_grads(*joined, dw_sum[...], dpq_sum[...], dpk_sum[...], db_sum[...])
            even = me_ref[1] == 0
            for z in range(rows.shape[0] // 2):
                first, second = rows[2 * z], rows[2 * z + 1]
                out_refs[0][me_ref[2] ^ z] = jnp.where(even, first, second)
                out_refs[1][me_ref[2] ^ z] = jnp.where(even, second, first)
        else:
            for ref, total in zip(out_refs, (dw_sum, dpq_sum, dpk_sum, db_sum)):
                ref[...] = total[...].astype(ref.dtype)


def attend_back_call(joined, me, toks, w_qkv, qkv, soft, dctx, place_q, place_k, sines, cosines):
    blocks, pages, rows, width = dctx.shape
    heads = place_q.shape[0]
    count = blocks * rows
    by_page = lambda *shape: pl.BlockSpec((1,) + shape, lambda p, *_: (p,) + (0,) * len(shape))
    place = (heads, HD, 2 * SPAN)
    if joined:
        own, _, owners = joined
        sums = [jax.ShapeDtypeStruct((owners // 2, 5 * own + 8, D), LOW)] * 2
    else:
        sums = [jax.ShapeDtypeStruct((D, 3 * width), LOW), jax.ShapeDtypeStruct(place, LOW),
                jax.ShapeDtypeStruct(place, LOW), jax.ShapeDtypeStruct((1, 3 * width), WIDE)]
    return pl.pallas_call(
        functools.partial(attend_back_kernel, heads, blocks, joined),
        grid_spec=pltpu.PrefetchScalarGridSpec(
            num_scalar_prefetch=1,
            grid=(pages,),
            in_specs=[by_page(rows, D)] * blocks + [
                whole((D, 3 * width)),
                by_page(count, 3 * width), by_page(heads, count, count),
                pl.BlockSpec((blocks, 1, rows, width), lambda p, *_: (0, p, 0, 0)),
                whole(place), whole(place), by_page(count, SPAN), by_page(count, SPAN)],
            out_specs=[
                pl.BlockSpec((blocks, 1, rows, D), lambda p, *_: (0, p, 0, 0)),
                *(whole(item.shape) for item in sums)],
            scratch_shapes=[
                pltpu.VMEM((D, 3 * width), WIDE), pltpu.VMEM(place, WIDE), pltpu.VMEM(place, WIDE),
                pltpu.VMEM((1, 3 * width), WIDE)],
        ),
        out_shape=[jax.ShapeDtypeStruct((blocks, pages, rows, D), LOW), *sums],
        compiler_params=pltpu.CompilerParams(vmem_limit_bytes=VMEM_BYTES),
        cost_estimate=cost(30e9, 20e6),
        name="attend_back",
    )(me, *toks, w_qkv, qkv, soft, dctx, place_q, place_k, sines, cosines)


def normed(values):
    centred = values - jnp.mean(values, axis=1, keepdims=True)
    scale = lax.rsqrt(jnp.mean(centred * centred, axis=1, keepdims=True) + 1e-05)
    return centred * scale, scale


def normed_back(gradient, unit, scale):
    mean = jnp.mean(gradient, axis=1, keepdims=True)
    along = jnp.mean(gradient * unit, axis=1, keepdims=True)
    return scale * (gradient - mean - unit * along)


def summed(values):
    return jnp.sum(values, axis=0, keepdims=True)


def second_half_kernel(cuts, split, at_ref, ctx_ref, tok_ref, cot_ref, wo_ref, vec_ref, wi_ref, *refs):
    n_grads = 4 if split else 2
    wu_ref, out_ref, pre_grad_ref, dctx_ref = refs[:4]
    grad_refs = refs[4:4 + n_grads]
    (small_ref, ctx_all, first, first_low, unit_one, scale_one, act, slope, outer, pre_two_grad,
     outer_grad, first_grad) = refs[4 + n_grads:]
    step = pl.program_id(0)
    core, x_at, y_at, z_at = at_ref[0], at_ref[1] >> 1, at_ref[1] & 1, at_ref[2]
    blocks, _, _, width = ctx_ref.shape
    count = tok_ref.shape[0]
    b_out, b_outer, gain_one, shift_one, gain_two, shift_two = (vec_ref[i:i + 1] for i in range(6))

    w_outer = wu_ref[...].reshape(D, D)

    @pl.when(step == 0)
    def _():
        small_ref[...] = jnp.zeros_like(small_ref)
        ctx = jnp.concatenate([ctx_ref[b].reshape(count, width) for b in range(blocks)], axis=1)
        ctx_all[...] = ctx
        pre = tok_ref[...].astype(WIDE) + (dot(ctx, wo_ref[...]) + b_out)
        unit, scale = normed(pre)
        unit_one[...] = unit
        scale_one[...] = jnp.broadcast_to(scale, scale_one.shape)
        value = unit * gain_one + shift_one
        first[...] = value
        first_low[...] = value.astype(LOW)

    @pl.when(step < cuts)
    def _():
        inner = dot(first_low[...], wi_ref[...]) + vec_ref[pl.ds(6 + step, 1)]
        half = 0.5 + 0.5 * lax.erf(inner * (0.5 ** 0.5))
        slope[step] = half + inner * (jnp.exp(inner * inner * -0.5) * ((0.5 / math.pi) ** 0.5))
        activated = (inner * half).astype(LOW)
        act[step] = activated
        product = dot(activated, w_outer)

        @pl.when(step == 0)
        def _():
            outer[...] = product

        @pl.when(step > 0)
        def _():
            outer[...] += product

    @pl.when(step == cuts - 1)
    def _():
        unit, scale = normed(first[...] + (outer[...] + b_outer))
        out_ref[...] = (unit * gain_two + shift_two).astype(LOW)
        cot = cot_ref[...].astype(WIDE)
        grad = normed_back(cot * gain_two, unit, scale)
        pre_two_grad[...] = grad
        low = grad.astype(LOW)
        outer_grad[...] = low
        small_ref[1:2] = summed(low.astype(WIDE))
        small_ref[4:5] = summed(cot * unit)
        small_ref[5:6] = summed(cot)

    def store_24(grad):
        cut = grad.reshape(4, 2, 2, 2, D // 32, D)
        for z in range(4):
            for x in range(2):
                for y in range(2):
                    slot = (0, y_at ^ y, x_at ^ x, z_at ^ z)
                    first, second = cut[z, x, y, 0], cut[z, x, y, 1]
                    grad_refs[2][slot] = jnp.where(core == 0, first, second).astype(LOW)
                    grad_refs[3][slot] = jnp.where(core == 0, second, first).astype(LOW)

    @pl.when((step >= cuts) & (step < 2 * cuts))
    def _():
        j = 2 * cuts - 1 - step
        low = outer_grad[...]
        d_outer = dot_tn(act[j], low).astype(LOW)
        inner_grad = (dot_nt(low, w_outer) * slope[j]).astype(LOW)
        small_ref[pl.ds(6 + j, 1)] = summed(inner_grad.astype(WIDE))
        d_inner = dot_tn(first_low[...], inner_grad)
        if split:
            cut = d_outer.reshape(2, 2, 2, D // 8, D)
            for x in range(2):
                for y in range(2):
                    slot = (x_at ^ x, y_at ^ y, 0)
                    first, second = cut[x, y, 0], cut[x, y, 1]
                    grad_refs[0][slot] = jnp.where(core == 0, first, second)
                    grad_refs[1][slot] = jnp.where(core == 0, second, first)
            store_24(d_inner)
        else:
            grad_refs[0][...] = d_outer
            grad_refs[1][0] = d_inner.astype(LOW)
        product = dot_nt(inner_grad, wi_ref[...])

        @pl.when(step == cuts)
        def _():
            first_grad[...] = pre_two_grad[...] + product

        @pl.when(step > cuts)
        def _():
            first_grad[...] += product

    @pl.when(step == 2 * cuts)
    def _():
        grad = first_grad[...]
        unit = unit_one[...]
        small_ref[2:3] = summed(grad * unit)
        small_ref[3:4] = summed(grad)
        grad = normed_back(grad * gain_one, unit, scale_one[:, :1])
        pre_grad_ref[...] = grad
        low = grad.astype(LOW)
        small_ref[0:1] = summed(low.astype(WIDE))
        dctx = dot_nt(low, wo_ref[...]).astype(LOW)
        for b in range(blocks):
            dctx_ref[b] = dctx[:, b * width:(b + 1) * width].reshape(dctx_ref.shape[1:])
        d_output = dot_tn(ctx_all[...], low)
        if split:
            store_24(d_output)
        else:
            grad_refs[1][0] = d_output.astype(LOW)


def second_half_call(split, at, ctx, tok, cot, w_output, vectors, w_inner, w_outer):
    blocks, pages, rows, width = ctx.shape
    count = pages * rows
    cuts = w_inner.shape[1] // D
    now = lambda i: jnp.where(i < cuts, i, jnp.maximum(2 * cuts - 1 - i, 0))
    late = lambda i: jnp.where(i < cuts, cuts - 1, jnp.maximum(2 * cuts - 1 - i, 0))
    last = lambda i: jnp.where(i < 2 * cuts, late(i), cuts)
    square, tall = (D, D), (count, D)
    eighth = (2, 2, 1, D // 8, D)
    slots = (1, 2, 2, 4, D // 32, D)
    if split:
        grad_specs = [pl.BlockSpec(eighth, lambda i, at: (0, 0, late(i) ^ at[2], 0, 0))] * 2
        grad_specs += [pl.BlockSpec(slots, lambda i, at: (last(i), 0, 0, 0, 0, 0))] * 2
        grads = [(2, 2, cuts, D // 8, D)] * 2 + [(cuts + 1,) + slots[1:]] * 2
    else:
        grad_specs = [
            pl.BlockSpec(square, lambda i, at: (late(i), 0)),
            pl.BlockSpec((1,) + square, lambda i, at: (last(i), 0, 0))]
        grads = [(cuts * D, D), (cuts + 1,) + square]
    return pl.pallas_call(
        functools.partial(second_half_kernel, cuts, split),
        grid_spec=pltpu.PrefetchScalarGridSpec(
            num_scalar_prefetch=1,
            grid=(2 * cuts + 1,),
            in_specs=[
                whole(ctx.shape), whole(tall), whole(tall), whole(square), whole(vectors.shape),
                pl.BlockSpec(square, lambda i, at: (0, now(i))),
                pl.BlockSpec((8, D // 8, D), lambda i, at: (now(i), 0, 0))],
            out_specs=[whole(tall), whole(tall), whole(ctx.shape), *grad_specs, whole(vectors.shape)],
            scratch_shapes=[
                pltpu.VMEM(tall, LOW), pltpu.VMEM(tall, WIDE), pltpu.VMEM(tall, LOW),
                pltpu.VMEM(tall, WIDE), pltpu.VMEM((count, 128), WIDE), pltpu.VMEM((cuts,) + tall, LOW),
                pltpu.VMEM((cuts,) + tall, WIDE), pltpu.VMEM(tall, WIDE), pltpu.VMEM(tall, WIDE),
                pltpu.VMEM(tall, LOW), pltpu.VMEM(tall, WIDE)],
        ),
        out_shape=[
            jax.ShapeDtypeStruct(tall, LOW),
            jax.ShapeDtypeStruct(tall, WIDE),
            jax.ShapeDtypeStruct(ctx.shape, LOW),
            *(jax.ShapeDtypeStruct(shape, LOW) for shape in grads),
            jax.ShapeDtypeStruct(vectors.shape, WIDE),
        ],
        compiler_params=pltpu.CompilerParams(vmem_limit_bytes=VMEM_BYTES),
        cost_estimate=cost(20e9, 30e6),
        name="second_half",
    )(at, ctx, tok, cot, w_output, vectors, w_inner, w_outer)


def swap(value, axis, size, bit):
    return lax.ppermute(value, axis, [(i, i ^ bit) for i in range(size)])


def gather_slots(value):
    near = swap(value, "pb", 4, 1)
    far = swap(value, "pb", 4, 2)
    return (value, near, far, swap(far, "pb", 4, 1))


def hop(value, devices, bits):
    return lax.ppermute(value, AXES, [(i, i ^ bits) for i in range(devices)])


def added(*terms):
    return sum(term.astype(WIDE) for term in terms)


def sum_along_z(value, devices):
    return added(value[0], *(hop(value[j], devices, j << 3) for j in (1, 2, 3)))


def tie(*values):
    return lax.optimization_barrier(values)


def transpose_roles(value, pages, size):
    inner = pages // size
    pairs = []
    for hi in range(size):
        for lo in range(inner):
            for b in range(size):
                pairs.append(((hi * inner + lo) * size + b, (b * inner + lo) * size + hi))
    return lax.ppermute(value, AXES, pairs)


def sum_slots(partial):
    got = swap(partial[1::2], "pb", 4, 1)
    total = partial[0::2].astype(WIDE) + got.astype(WIDE)
    return total[0] + swap(total[1].astype(LOW), "pb", 4, 2).astype(WIDE)


def to_halves(place):
    cut = place.reshape(place.shape[:-1] + (2, 2, FREQ))
    return jnp.swapaxes(cut, -3, -2).reshape(place.shape)


def on_device(sizes, tokens, cotangent, boxes, resolution, padding,
              query_weight, keys_weight, values_weight, output_weight, query_place, keys_place,
              inner_weight, outer_weight, query_bias, keys_bias, values_bias, output_bias,
              inner_bias, outer_bias, first_gain, first_shift, second_gain, second_shift):
    page_size, pb_size = sizes
    devices = page_size * pb_size
    inner_pages = page_size // pb_size
    pages, rows, _ = tokens.shape
    count = rows * pb_size
    heads = HEADS // pb_size
    width = heads * HD
    own = query_weight.shape[0]
    ff_own = outer_weight.shape[0]
    ff = ff_own * devices
    cuts = ff // D
    me, page = lax.axis_index("pb"), lax.axis_index("page")
    place_at = (page % inner_pages) * pb_size + me
    number = page * pb_size + me
    me_array = me.astype(jnp.int32).reshape(1)
    by_link = (page_size, pb_size, own) == (8, 4, 24)

    at = jnp.stack([number & 1, (number >> 1) & 3, number >> 3, number, place_at]).astype(jnp.int32)
    small_rows = 16
    vectors = [output_bias, outer_bias, first_gain, first_shift, second_gain, second_shift]
    if by_link:
        lines = vectors + [None] * 2 + [inner_bias] + [None] * 7 + [query_bias, keys_bias, values_bias]
        lines = [jnp.zeros((128,), WIDE) if line is None
                 else jnp.pad(line.astype(WIDE), (0, 128 - line.shape[0])) for line in lines]
        lines = jnp.concatenate(lines + [jnp.zeros((5 * 128,), WIDE)]).reshape(24, 128)
        packed, cols, mixed = pack_call(
            at, lines, query_weight, keys_weight, values_weight, query_place, keys_place,
            output_weight, inner_weight, outer_weight)
    else:
        cols = jnp.concatenate([query_weight, keys_weight, values_weight], axis=0)
        cols = cols.reshape(3 * own, pb_size, width).swapaxes(0, 1)
        bias_rows = jnp.zeros((3, width), LOW)
        bias_rows = lax.dynamic_update_slice(
            bias_rows, jnp.stack([query_bias, keys_bias, values_bias]), (0, place_at * own))
        bias_rows = jnp.pad(bias_rows.reshape(1, 3 * width), ((0, 7), (0, D - 3 * width)))
        mixed = jnp.concatenate([to_halves(query_place), to_halves(keys_place), bias_rows], axis=0)
        vectors = lax.dynamic_update_slice(jnp.zeros((6, D), LOW), jnp.stack(vectors), (0, number * own))
        b_inner = lax.dynamic_update_slice(jnp.zeros((ff,), LOW), inner_bias, (number * ff_own,))
        vectors = jnp.concatenate(
            [vectors, b_inner.reshape(cuts, D), jnp.zeros((small_rows - 6 - cuts, D), LOW)], axis=0)
        packed = jnp.concatenate(
            [outer_weight] + [inner_weight[:, j * D:(j + 1) * D] for j in range(cuts)]
            + [vectors, output_weight], axis=0)
    cols = lax.all_to_all(cols, "pb", 0, 0, tiled=True)
    cols = cols.swapaxes(0, 1).reshape(3 * own, D)
    mixed = transpose_roles(mixed, page_size, pb_size)
    mixed = jnp.concatenate([cols, mixed], axis=0)
    late = lax.all_gather(packed, AXES, axis=0)

    grid_x = (boxes[0] + boxes[2]) * 500 // resolution[0][:, None]
    grid_y = (boxes[1] + boxes[3]) * 500 // resolution[1][:, None]
    places = lax.all_gather(jnp.stack([grid_x, grid_y, padding]), "pb", axis=0)
    toks = gather_slots(tokens)

    places = jnp.stack([places[me ^ j] for j in range(pb_size)])
    places = places.transpose(1, 2, 0, 3).reshape(3, pages, count)
    rates = jnp.exp(jnp.arange(FREQ).astype(WIDE) * (-math.log(10000.0) / FREQ))
    grids = places[:2].astype(WIDE)
    angles = jnp.concatenate(
        [grids[0][..., None] * rates, grids[1][..., None] * rates], axis=-1)
    sines, cosines = jnp.sin(angles), jnp.cos(angles)
    alive = places[2][:, None, :]

    if by_link:
        mixed = jnp.stack([mixed] + [hop(mixed, devices, j << 3) for j in (1, 2, 3)])
        w_qkv, place_q, place_k, bias_qkv = assemble_call(
            at, mixed, hop(mixed, devices, 4), own, pb_size)
    else:
        mixed = lax.all_gather(mixed, "page", axis=0)
        w_qkv = mixed[:, :3 * own].reshape(page_size, 3, own, pb_size, width)
        w_qkv = w_qkv.transpose(0, 3, 2, 1, 4).reshape(D, 3 * width)
        bias_qkv = jnp.sum(mixed[:, 5 * own, :3 * width].astype(WIDE), axis=0, keepdims=True)
        mixed = mixed[:, 3 * own:5 * own].reshape(pb_size, inner_pages, 2, own, D)
        mixed = mixed.transpose(2, 1, 0, 3, 4).reshape(2, heads, HD, 2 * SPAN)
        place_q, place_k = mixed[0], mixed[1]

    qkv, soft, ctx_heads = attend_call(
        me_array, toks, w_qkv, bias_qkv, place_q, place_k, sines, cosines, alive)
    ctx = lax.all_to_all(ctx_heads, "pb", 0, 0, tiled=True)

    spot = ff_own
    w_inner = jnp.concatenate(
        [late[:, spot + j * own:spot + (j + 1) * own].reshape(D, D) for j in range(cuts)], axis=1)
    spot += cuts * own
    vectors = jnp.sum(late[:, spot:spot + small_rows].astype(WIDE), axis=0)
    w_output = late[:, spot + small_rows:].reshape(D, D)
    w_outer = late if by_link else late[:, :ff_own].reshape(8 * cuts, D // 8, D)

    tok = tokens.reshape(pages * rows, D)
    output, pre_one_grad, dctx, *grads, small = second_half_call(
        by_link, at, ctx, tok, cotangent.reshape(pages * rows, D), w_output, vectors, w_inner, w_outer)
    dctx = lax.all_to_all(dctx, "pb", 0, 0, tiled=True)

    if by_link:
        outer_kept, outer_sent, inner_kept, inner_sent = grads
        outer_sent, inner_sent = hop(outer_sent, devices, 1), hop(inner_sent, devices, 1)
        outer_far = added(outer_kept[1], outer_sent[1]).astype(LOW)
        inner_far = added(inner_kept[:, 1], inner_sent[:, 1]).astype(LOW)
        outer_kept = added(outer_kept[0], outer_sent[0]).astype(LOW)
        inner_kept = added(inner_kept[:, 0], inner_sent[:, 0]).astype(LOW)
        dctx, outer_far, inner_far, outer_kept, inner_kept = tie(
            dctx, outer_far, inner_far, outer_kept, inner_kept)
        outer_far, inner_far = hop(outer_far, devices, 4), hop(inner_far, devices, 2)
    small = lax.all_gather(small, AXES, axis=0)

    joined = (own, pb_size, page_size) if by_link else None
    me_array = jnp.stack([me, at[1] >> 1, at[2]]).astype(jnp.int32)
    partial, *sums = attend_back_call(
        joined, me_array, toks, w_qkv, qkv, soft, dctx, place_q, place_k, sines, cosines)

    if by_link:
        partial, mixed, mixed_far, outer_kept, outer_far, inner_kept, inner_far = tie(
            partial, *sums, outer_kept, outer_far, inner_kept, inner_far)
        mixed_far = hop(mixed_far, devices, 4)
        near = hop(partial[1::2], devices, 1)
        outer_sent = added(outer_kept[1], outer_far[1]).astype(LOW)
        inner_sent = added(inner_kept[:, 1], inner_far[:, 1]).astype(LOW)
        outer_sent, inner_sent = hop(outer_sent, devices, 2), hop(inner_sent, devices, 4)
        outer_kept, inner_kept = added(outer_kept[0], outer_far[0]), added(inner_kept[:, 0], inner_far[:, 0])
        mixed, mixed_far, partial, near = tie(mixed, mixed_far, partial, near)
        total = added(partial[0::2], near)
        far = hop(total[1].astype(LOW), devices, 2)
        mixed = added(mixed, mixed_far).astype(LOW)
        mixed, outer_kept, outer_sent, inner_kept, inner_sent = tie(
            mixed, outer_kept, outer_sent, inner_kept, inner_sent)
        mixed_z = [hop(mixed[j], devices, j << 3) for j in (1, 2, 3)]
        outer_sum = added(outer_kept, outer_sent).astype(LOW)
        inner_sum = added(inner_kept, inner_sent).astype(LOW).swapaxes(0, 1)
        outer_z = [hop(outer_sum[j], devices, j << 3) for j in (1, 2, 3)]
        inner_z = [hop(inner_sum[j], devices, j << 3) for j in (1, 2, 3)]
        mixed = added(mixed[0], *mixed_z).astype(LOW)
        cols, far, total = tie(
            mixed[:3 * own].reshape(3 * own, pb_size, width).swapaxes(0, 1), far, total[0])
        tokens_grad = pre_one_grad.reshape(pages, rows, D) + added(total, far)
        cols = lax.all_to_all(cols, "pb", 0, 0, tiled=True)
        mixed = transpose_roles(mixed[3 * own:], page_size, pb_size)
        cols, mixed, outer_sum, inner_sum, *got = tie(
            cols, mixed, outer_sum, inner_sum, *outer_z, *inner_z)
        d_outer = added(outer_sum[0], *got[:3])
        inner_sum = added(inner_sum[0], *got[3:])
        d_query, d_keys, d_values, d_place_q, d_place_k = finish_call(cols, mixed)
        d_inner = jnp.concatenate([inner_sum[j] for j in range(cuts)], axis=1)
        d_output = inner_sum[cuts]
    else:
        d_outer = lax.psum_scatter(
            grads[0].reshape(devices, ff_own, D), AXES, scatter_dimension=0, tiled=False).astype(WIDE)
        inner_sum = grads[1].reshape(cuts + 1, devices, own, D).swapaxes(0, 1)
        inner_sum = lax.psum_scatter(inner_sum, AXES, scatter_dimension=0, tiled=False).astype(WIDE)
        d_inner = jnp.concatenate([inner_sum[j] for j in range(cuts)], axis=1)
        d_output = inner_sum[cuts]
        d_w, d_pq, d_pk, d_bias = sums
        d_w = d_w.reshape(page_size, pb_size, own, 3, width).transpose(0, 3, 2, 1, 4)
        d_w = d_w.reshape(page_size, 3 * own, D)
        d_p = jnp.stack([d_pq, d_pk]).reshape(2, inner_pages, pb_size, own, D)
        d_p = d_p.transpose(2, 1, 0, 3, 4).reshape(page_size, 2 * own, D)
        d_bias = jnp.pad(d_bias, ((0, 7), (0, D - 3 * width))).astype(LOW)
        d_bias = jnp.broadcast_to(d_bias[None], (page_size, 8, D))
        mixed = jnp.concatenate([d_w, d_p, d_bias], axis=1)
        mixed = lax.all_to_all(mixed, "page", 0, 0, tiled=True)
        mixed = jnp.sum(mixed.astype(WIDE), axis=0).astype(LOW)
        tokens_grad = pre_one_grad.reshape(pages, rows, D) + sum_slots(partial)
        cols = mixed[:3 * own].reshape(3 * own, pb_size, width).swapaxes(0, 1)
        cols = lax.all_to_all(cols, "pb", 0, 0, tiled=True)
        d_query, d_keys, d_values = cols.swapaxes(0, 1).reshape(3, own, D).astype(WIDE)
        mixed = transpose_roles(mixed[3 * own:], page_size, pb_size)
        d_place_q, d_place_k = to_halves(mixed[:own].astype(WIDE)), to_halves(mixed[own:2 * own].astype(WIDE))
    d_bias = lax.dynamic_slice(
        mixed[2 * own, :3 * width].astype(WIDE).reshape(3, width), (0, place_at * own), (3, own))

    small = jnp.sum(small, axis=0)
    d_b_inner = lax.dynamic_slice(small[6:6 + cuts].reshape(ff), (number * ff_own,), (ff_own,))
    vectors = lax.dynamic_slice(small, (0, number * own), (6, own))
    return (
        output.reshape(pages, rows, D),
        tokens_grad,
        d_query, d_keys, d_values,
        d_output,
        d_place_q, d_place_k,
        d_inner,
        d_outer.reshape(ff_own, D),
        d_bias[0], d_bias[1], d_bias[2],
        vectors[0], d_b_inner, vectors[1], vectors[2], vectors[3], vectors[4], vectors[5],
    )


def solution(mesh):
    rows, vector = P(AXES, None), P(AXES)
    token = P("page", "pb", None)
    in_specs = (token, token, P(None, "page", "pb"), P(None, "page"), P("page", "pb"))
    in_specs = in_specs + (rows,) * 8 + (vector,) * 10
    out_specs = (token, token) + (rows,) * 8 + (vector,) * 10
    sizes = (mesh.shape["page"], mesh.shape["pb"])
    return jax.shard_map(
        functools.partial(on_device, sizes), mesh=mesh, in_specs=in_specs, out_specs=out_specs,
        check_vma=False)
```

```python
import functools
import math

import jax
import jax.numpy as jnp
from jax import lax
from jax.experimental import pallas as pl
from jax.experimental.pallas import tpu as pltpu
from jax.sharding import PartitionSpec as P

HEADS = 12
HD = 64
FREQ = 192
D = HEADS * HD
SPAN = 2 * FREQ
SCALING = (3.0 * HD) ** (-0.5)
LOW = jnp.bfloat16
WIDE = jnp.float32
AXES = ("page", "pb")
VMEM_BYTES = 56 * 1024 * 1024


def dot(a, b):
    return jnp.dot(a, b, preferred_element_type=WIDE)


def dot_nt(a, b):
    return lax.dot_general(a, b, (((1,), (1,)), ((), ())), preferred_element_type=WIDE)


def dot_tn(a, b):
    return lax.dot_general(a, b, (((0,), (0,)), ((), ())), preferred_element_type=WIDE)


def whole(shape):
    return pl.BlockSpec(shape, lambda i, *_: (0,) * len(shape))


def cost(flops, bytes_accessed):
    return pl.CostEstimate(flops=int(flops), bytes_accessed=int(bytes_accessed), transcendentals=0)


def lanes_to(rows, length, start):
    lane = lax.broadcasted_iota(jnp.int32, rows.shape, 1)
    rows = jnp.where(lane < length, rows, 0.0)
    padded = jnp.concatenate([rows, jnp.zeros((rows.shape[0], D - rows.shape[1]), WIDE)], axis=1)
    return pltpu.roll(padded, start, 1)


def halves(place):
    cut = [place[:, i * FREQ:(i + 1) * FREQ] for i in (0, 2, 1, 3)]
    return jnp.concatenate(cut, axis=1)


def pack_kernel(size, at_ref, vec_ref, wq_ref, wk_ref, wv_ref, pq_ref, pk_ref, wo_ref, wi_ref, wu_ref,
                late_ref, cols_ref, mixed_ref):
    number, place_at = at_ref[3], at_ref[4]
    own, ff_own = wq_ref.shape[0], wu_ref.shape[0]
    cuts = wi_ref.shape[1] // D
    width = D // size
    vectors = vec_ref[...]
    lanes = lanes_to(vectors[:8], own, number * own)
    row = lax.broadcasted_iota(jnp.int32, lanes.shape, 0)
    first = jnp.where(row < 6, lanes, 0.0)
    inner = lanes_to(vectors[8:16], ff_own, lax.rem(number, D // ff_own) * ff_own)
    spot = lax.div(number, D // ff_own)
    for j in range(cuts):
        hit = (row == (6 + j) % 8) & (spot == j)
        if 6 + j < 8:
            first = first + jnp.where(hit, pltpu.roll(inner, 6 + j, 0), 0.0)
    second = jnp.zeros_like(first)
    for j in range(2, cuts):
        hit = (row == j - 2) & (spot == j)
        second = second + jnp.where(hit, pltpu.roll(inner, j - 2, 0), 0.0)
    wi = wi_ref[...].astype(WIDE)
    late = [wu_ref[...].astype(WIDE)] + [wi[:, j * D:(j + 1) * D] for j in range(cuts)]
    late += [first, second, wo_ref[...].astype(WIDE)]
    late_ref[...] = jnp.concatenate(late, axis=0).astype(LOW)
    cols = jnp.concatenate([ref[...].astype(WIDE) for ref in (wq_ref, wk_ref, wv_ref)], axis=0)
    for b in range(size):
        cols_ref[b] = cols[:, b * width:(b + 1) * width].astype(LOW)
    lanes = lanes_to(vectors[16:24], own, place_at * own)
    bias = jnp.concatenate(
        [lanes[i:i + 1, :width] for i in range(3)] + [jnp.zeros((1, D - 3 * width), WIDE)], axis=1)
    bias = jnp.concatenate([bias, jnp.zeros((7, D), WIDE)], axis=0)
    places = [halves(pq_ref[...].astype(WIDE)), halves(pk_ref[...].astype(WIDE)), bias]
    mixed_ref[...] = jnp.concatenate(places, axis=0).astype(LOW)


def pack_call(at, vectors, *weights):
    own, ff_own = weights[0].shape[0], weights[-1].shape[0]
    size = 4
    rows = ff_own + weights[-2].shape[1] // D * own + 16 + own
    return pl.pallas_call(
        functools.partial(pack_kernel, size),
        out_shape=[
            jax.ShapeDtypeStruct((rows, D), LOW),
            jax.ShapeDtypeStruct((size, 3 * own, D // size), LOW),
            jax.ShapeDtypeStruct((2 * own + 8, D), LOW),
        ],
        in_specs=[pl.BlockSpec(memory_space=pltpu.SMEM)]
        + [pl.BlockSpec(memory_space=pltpu.VMEM)] * (1 + len(weights)),
        compiler_params=pltpu.CompilerParams(vmem_limit_bytes=VMEM_BYTES),
        name="pack",
    )(at, vectors, *weights)


def finish_kernel(at_ref, cols_ref, mixed_ref, *out_refs):
    *grad_refs, lines_ref = out_refs
    number, place_at = at_ref[3], at_ref[4]
    own = grad_refs[0].shape[0]
    size, _, width = cols_ref.shape
    cols = [cols_ref[lax.rem(number, size) ^ b].astype(WIDE) for b in range(size)]
    for i in range(3):
        grad_refs[i][...] = jnp.concatenate([c[i * own:(i + 1) * own] for c in cols], axis=1)
    mixed = mixed_ref[...].astype(WIDE)
    for i in range(2):
        grad_refs[3 + i][...] = halves(mixed[i * own:(i + 1) * own])
    total = sum(c[3 * own:] for c in cols)
    quarters = [total[16 * i:16 * (i + 1)] for i in range(size)]
    rows = sum(jnp.where(lax.div(number, 8) == i, part, 0.0) for i, part in enumerate(quarters))
    rows = pltpu.roll(rows, lax.rem(width - lax.rem(number, 8) * own, width), 1)
    inner = sum(jnp.where(lax.div(lax.rem(number, 8), 2) == i, part, 0.0) for i, part in enumerate(quarters))
    inner = sum(jnp.where(lax.div(number, 8) == j, inner[6 + j:7 + j], 0.0) for j in range(4))
    inner = pltpu.roll(jnp.broadcast_to(inner, (8, width)), lax.rem(number, 2) * (width // 2), 1)
    bias = mixed[2 * own + 8:2 * own + 16]
    bias = jnp.concatenate([bias[2:3, i * width:(i + 1) * width] for i in range(3)] + [bias[:5, :width]], axis=0)
    bias = pltpu.roll(bias, lax.rem(width - place_at * own, width), 1)
    lines_ref[...] = jnp.concatenate([rows[:8, :128], inner[:, :128], bias[:, :128]], axis=0)


def finish_call(at, cols, mixed):
    own = (mixed.shape[0] - 16) // 2
    return pl.pallas_call(
        finish_kernel,
        out_shape=[jax.ShapeDtypeStruct((own, D), WIDE)] * 5 + [jax.ShapeDtypeStruct((24, 128), WIDE)],
        in_specs=[pl.BlockSpec(memory_space=pltpu.SMEM)] + [pl.BlockSpec(memory_space=pltpu.VMEM)] * 2,
        compiler_params=pltpu.CompilerParams(vmem_limit_bytes=VMEM_BYTES),
        name="finish",
    )(at, cols, mixed)


def assemble_kernel(own, size, at_ref, mine_ref, theirs_ref, w_ref, pq_ref, pk_ref, bias_ref, got):
    pages = got.shape[0]
    inner = pages // size
    width = D // size
    even = (at_ref[1] >> 1) == 0
    for z in range(pages // 2):
        mine, theirs = mine_ref[at_ref[2] ^ z].astype(WIDE), theirs_ref[at_ref[2] ^ z].astype(WIDE)
        got[2 * z] = jnp.where(even, mine, theirs)
        got[2 * z + 1] = jnp.where(even, theirs, mine)
    columns = []
    for part in range(3):
        rows = got[:, pl.ds(part * own, own)]
        cut = [rows[:, :, b * width:(b + 1) * width][:, None] for b in range(size)]
        columns.append(jnp.concatenate(cut, axis=1).reshape(D, width))
    w_ref[...] = jnp.concatenate(columns, axis=1).astype(LOW)
    for start, ref in ((3 * own, pq_ref), (4 * own, pk_ref)):
        order = [b * inner + lo for lo in range(inner) for b in range(size)]
        rows = jnp.concatenate([got[p, pl.ds(start, own)] for p in order], axis=0)
        ref[...] = rows.astype(LOW).reshape(ref.shape)
    bias_ref[...] = jnp.sum(got[:, pl.ds(5 * own, 8)], axis=0)[:1, :3 * width]


def assemble_call(at, mine, theirs, own, size):
    width = D // size
    place = (width // HD, HD, 2 * SPAN)
    return pl.pallas_call(
        functools.partial(assemble_kernel, own, size),
        out_shape=[
            jax.ShapeDtypeStruct((D, 3 * width), LOW),
            jax.ShapeDtypeStruct(place, LOW),
            jax.ShapeDtypeStruct(place, LOW),
            jax.ShapeDtypeStruct((1, 3 * width), WIDE),
        ],
        in_specs=[pl.BlockSpec(memory_space=pltpu.SMEM)] + [pl.BlockSpec(memory_space=pltpu.VMEM)] * 2,
        scratch_shapes=[pltpu.VMEM((2 * mine.shape[0],) + mine.shape[1:], WIDE)],
        compiler_params=pltpu.CompilerParams(vmem_limit_bytes=VMEM_BYTES),
        name="assemble",
    )(at, mine, theirs)


def fold(rows):
    half = rows.shape[0] // 2
    return jnp.concatenate([rows[:half], rows[half:]], axis=1)


def unfold(rows):
    half = rows.shape[1] // 2
    return jnp.concatenate([rows[:, :half], rows[:, half:]], axis=0)


def turn(spread, left, right):
    s, c = spread[:, :SPAN], spread[:, SPAN:]
    return jnp.concatenate(
        [(s * left + c * right).astype(LOW), (c * left - s * right).astype(LOW)], axis=1)


def turn_back(gradient, left, right):
    s, c = gradient[:, :SPAN], gradient[:, SPAN:]
    return jnp.concatenate(
        [(s * left - c * right).astype(LOW), (s * right + c * left).astype(LOW)], axis=1)


def feature_pair(sines, cosines):
    sines, cosines = sines.astype(LOW), cosines.astype(LOW)
    return (jnp.concatenate([sines, cosines], axis=1), jnp.concatenate([cosines, sines], axis=1))


def attend_kernel(heads, blocks, me_ref, *refs):
    tok_refs = refs[:blocks]
    (w_ref, bias_ref, pq_ref, pk_ref, sin_ref, cos_ref, alive_ref,
     qkv_ref, soft_ref, share_ref, ctx_ref) = refs[blocks:]
    me = me_ref[0]
    rows = tok_refs[0].shape[1]
    width = heads * HD
    tok = jnp.concatenate([ref[0] for ref in tok_refs], axis=0)
    sines, cosines = sin_ref[0], cos_ref[0]
    key_feats, query_feats = feature_pair(sines, cosines)
    count = tok.shape[0]
    mask = jnp.broadcast_to(jnp.where(alive_ref[0] > 0, 0.0, -1e30), (128, count)).T[:, :HD]
    lane = lax.broadcasted_iota(jnp.int32, (count, HD), 1)
    mask = jnp.where(lane == 0, mask, 0.0).astype(LOW)
    ones = jnp.where(lane == 0, 1.0, 0.0).astype(LOW)
    qkv = (dot(tok, w_ref[...]) + bias_ref[...]).astype(LOW)
    qkv_ref[0] = qkv
    pieces = []
    for h in range(heads):
        q = qkv[:, h * HD:(h + 1) * HD]
        k = qkv[:, width + h * HD:width + (h + 1) * HD]
        v = qkv[:, 2 * width + h * HD:2 * width + (h + 1) * HD]
        turned_q = turn(dot(q, pq_ref[h]), cosines, sines)
        turned_k = turn(dot(k, pk_ref[h]), sines, cosines)
        raw = dot_nt(jnp.concatenate([turned_q, query_feats, q, ones], axis=1),
                     jnp.concatenate([key_feats, turned_k, k, mask], axis=1))
        lifted = jnp.exp2((raw - jnp.max(raw, axis=1, keepdims=True)) * (SCALING * math.log2(math.e)))
        share = 1.0 / jnp.sum(lifted, axis=1, keepdims=True)
        share_ref[0, :, h:h + 1] = share
        lifted = lifted.astype(LOW)
        soft_ref[0, h] = lifted
        pieces.append((dot(lifted, v) * share).astype(LOW))
    ctx = jnp.concatenate(pieces, axis=1)
    for j in range(blocks):
        ctx_ref[me ^ j, 0] = fold(ctx[j * rows:(j + 1) * rows])


def attend_call(me, toks, w_qkv, bias, place_q, place_k, sines, cosines, alive):
    blocks = len(toks)
    pages, rows, _ = toks[0].shape
    heads = place_q.shape[0]
    width = heads * HD
    count = blocks * rows
    by_page = lambda *shape: pl.BlockSpec((1,) + shape, lambda p, *_: (p,) + (0,) * len(shape))
    return pl.pallas_call(
        functools.partial(attend_kernel, heads, blocks),
        grid_spec=pltpu.PrefetchScalarGridSpec(
            num_scalar_prefetch=1,
            grid=(pages,),
            in_specs=[by_page(rows, D)] * blocks + [
                whole((D, 3 * width)), whole((1, 3 * width)),
                whole((heads, HD, 2 * SPAN)), whole((heads, HD, 2 * SPAN)),
                by_page(count, SPAN), by_page(count, SPAN), by_page(1, count)],
            out_specs=[
                by_page(count, 3 * width), by_page(heads, count, count), by_page(count, heads),
                pl.BlockSpec((blocks, 1, rows // 2, 2 * width), lambda p, *_: (0, p, 0, 0))],
        ),
        out_shape=[
            jax.ShapeDtypeStruct((pages, count, 3 * width), LOW),
            jax.ShapeDtypeStruct((pages, heads, count, count), LOW),
            jax.ShapeDtypeStruct((pages, count, heads), WIDE),
            jax.ShapeDtypeStruct((blocks, pages, rows // 2, 2 * width), LOW),
        ],
        compiler_params=pltpu.CompilerParams(vmem_limit_bytes=VMEM_BYTES),
        cost_estimate=cost(20e9, 20e6),
        name="attend",
    )(me, *toks, w_qkv, bias, place_q, place_k, sines, cosines, alive)


def joined_grads(own, size, pages, small, d_w, d_pq, d_pk, d_bias):
    inner = pages // size
    width = D // size
    cut = d_w.reshape(pages, size, own, 3 * width)
    parts = []
    for part in range(3):
        parts.append(jnp.concatenate(
            [cut[:, b, :, part * width:(part + 1) * width] for b in range(size)], axis=2))
    for place in (d_pq, d_pk):
        place = place.reshape(D // size, 2 * SPAN)
        order = [(lo * size + b) * own for b in range(size) for lo in range(inner)]
        parts.append(jnp.concatenate([place[at:at + own][None] for at in order], axis=0))
    row = jnp.concatenate([d_bias, jnp.zeros((1, D - 3 * width), WIDE)], axis=1)
    at = lax.broadcasted_iota(jnp.int32, small.shape, 0)
    rows = jnp.where(at == 10, row, jnp.where(at < 10, small, 0.0))
    parts.append(jnp.broadcast_to(rows[None], (pages,) + rows.shape))
    return jnp.concatenate(parts, axis=1).astype(LOW)


def attend_back_kernel(heads, blocks, joined, me_ref, *refs):
    tok_refs = refs[:blocks]
    (w_ref, small_ref, qkv_ref, soft_ref, share_ref, ctx_ref, dctx_ref, pq_ref, pk_ref, sin_ref, cos_ref,
     kept_ref, sent_ref, *out_refs, dw_sum, dpq_sum, dpk_sum, db_sum) = refs[blocks:]
    me = me_ref[0]
    step, last = pl.program_id(0), pl.num_programs(0) - 1
    rows = tok_refs[0].shape[1]
    width = heads * HD
    sines, cosines = sin_ref[0], cos_ref[0]
    key_feats, query_feats = feature_pair(sines, cosines)
    qkv = qkv_ref[0]
    dctx = jnp.concatenate([unfold(dctx_ref[me ^ j, 0]) for j in range(blocks)], axis=0)
    ctx = jnp.concatenate([unfold(ctx_ref[me ^ j, 0]) for j in range(blocks)], axis=0)
    along = dctx.astype(WIDE) * ctx.astype(WIDE)

    @pl.when(step == 0)
    def _():
        for ref in (dw_sum, dpq_sum, dpk_sum, db_sum):
            ref[...] = jnp.zeros_like(ref)

    d_q, d_k, d_v = [], [], []
    for h in range(heads):
        q = qkv[:, h * HD:(h + 1) * HD]
        k = qkv[:, width + h * HD:width + (h + 1) * HD]
        v = qkv[:, 2 * width + h * HD:2 * width + (h + 1) * HD]
        dc = dctx[:, h * HD:(h + 1) * HD]
        share = share_ref[0, :, h:h + 1]
        lifted = soft_ref[0, h]
        row_dot = jnp.sum(along[:, h * HD:(h + 1) * HD], axis=1, keepdims=True)
        raw_grad = ((dot_nt(dc, v) - row_dot) * (share * SCALING) * lifted.astype(WIDE)).astype(LOW)
        d_v.append(dot_tn(lifted, (dc.astype(WIDE) * share).astype(LOW)).astype(LOW))
        turned = dot(raw_grad, jnp.concatenate([key_feats, k], axis=1))
        spread_q = turn_back(turned[:, :2 * SPAN], cosines, sines)
        d_q.append((turned[:, 2 * SPAN:] + dot_nt(spread_q, pq_ref[h])).astype(LOW))
        dpq_sum[h] += dot_tn(q, spread_q)
        turned = dot_tn(raw_grad, jnp.concatenate([query_feats, q], axis=1))
        spread_k = turn_back(turned[:, :2 * SPAN], sines, cosines)
        d_k.append((turned[:, 2 * SPAN:] + dot_nt(spread_k, pk_ref[h])).astype(LOW))
        dpk_sum[h] += dot_tn(k, spread_k)
    dqkv = jnp.concatenate(d_q + d_k + d_v, axis=1)
    db_sum[...] += jnp.sum(dqkv.astype(WIDE), axis=0, keepdims=True)
    tok = jnp.concatenate([ref[0] for ref in tok_refs], axis=0)
    dw_sum[...] += dot_tn(tok, dqkv)
    part = dot_nt(dqkv, w_ref[...]).astype(LOW)
    for j in range(blocks):
        (sent_ref if j % 2 else kept_ref)[j // 2, 0] = part[j * rows:(j + 1) * rows]

    @pl.when(step == last)
    def _():
        if joined:
            rows = joined_grads(*joined, small_ref[...], dw_sum[...], dpq_sum[...], dpk_sum[...], db_sum[...])
            even = me_ref[1] == 0
            for z in range(rows.shape[0] // 2):
                first, second = rows[2 * z], rows[2 * z + 1]
                out_refs[0][me_ref[2] ^ z] = jnp.where(even, first, second)
                out_refs[1][me_ref[2] ^ z] = jnp.where(even, second, first)
        else:
            for ref, total in zip(out_refs, (dw_sum, dpq_sum, dpk_sum, db_sum)):
                ref[...] = total[...].astype(ref.dtype)


def attend_back_call(joined, me, toks, w_qkv, small, qkv, soft, share, ctx, dctx, place_q, place_k, sines, cosines):
    blocks, pages, rows, width = dctx.shape
    rows, width = 2 * rows, width // 2
    heads = place_q.shape[0]
    count = blocks * rows
    by_page = lambda *shape: pl.BlockSpec((1,) + shape, lambda p, *_: (p,) + (0,) * len(shape))
    place = (heads, HD, 2 * SPAN)
    if joined:
        own, _, owners = joined
        sums = [jax.ShapeDtypeStruct((owners // 2, 5 * own + 16, D), LOW)] * 2
    else:
        sums = [jax.ShapeDtypeStruct((D, 3 * width), LOW), jax.ShapeDtypeStruct(place, LOW),
                jax.ShapeDtypeStruct(place, LOW), jax.ShapeDtypeStruct((1, 3 * width), WIDE)]
    return pl.pallas_call(
        functools.partial(attend_back_kernel, heads, blocks, joined),
        grid_spec=pltpu.PrefetchScalarGridSpec(
            num_scalar_prefetch=1,
            grid=(pages,),
            in_specs=[by_page(rows, D)] * blocks + [
                whole((D, 3 * width)), whole(small.shape),
                by_page(count, 3 * width), by_page(heads, count, count), by_page(count, heads),
                pl.BlockSpec((blocks, 1, rows // 2, 2 * width), lambda p, *_: (0, p, 0, 0)),
                pl.BlockSpec((blocks, 1, rows // 2, 2 * width), lambda p, *_: (0, p, 0, 0)),
                whole(place), whole(place), by_page(count, SPAN), by_page(count, SPAN)],
            out_specs=[
                *[pl.BlockSpec((blocks // 2, 1, rows, D), lambda p, *_: (0, p, 0, 0))] * 2,
                *(whole(item.shape) for item in sums)],
            scratch_shapes=[
                pltpu.VMEM((D, 3 * width), WIDE), pltpu.VMEM(place, WIDE), pltpu.VMEM(place, WIDE),
                pltpu.VMEM((1, 3 * width), WIDE)],
        ),
        out_shape=[*[jax.ShapeDtypeStruct((blocks // 2, pages, rows, D), LOW)] * 2, *sums],
        compiler_params=pltpu.CompilerParams(vmem_limit_bytes=VMEM_BYTES),
        cost_estimate=cost(30e9, 20e6),
        name="attend_back",
    )(me, *toks, w_qkv, small, qkv, soft, share, ctx, dctx, place_q, place_k, sines, cosines)


def normed(values):
    centred = values - jnp.mean(values, axis=1, keepdims=True)
    scale = lax.rsqrt(jnp.mean(centred * centred, axis=1, keepdims=True) + 1e-05)
    return centred * scale, scale


def normed_back(gradient, unit, scale):
    mean = jnp.mean(gradient, axis=1, keepdims=True)
    along = jnp.mean(gradient * unit, axis=1, keepdims=True)
    return scale * (gradient - mean - unit * along)


def summed(values):
    return jnp.sum(values, axis=0, keepdims=True)


def second_half_kernel(cuts, split, at_ref, ctx_ref, tok_ref, cot_ref, wo_ref, vec_ref, wi_ref, *refs):
    n_grads = 4 if split else 2
    wu_ref, out_ref, pre_grad_ref, dctx_ref = refs[:4]
    grad_refs = refs[4:4 + n_grads]
    (small_ref, ctx_all, first, first_low, unit_one, scale_one, act, slope, outer, pre_two_grad,
     outer_grad, first_grad) = refs[4 + n_grads:]
    step = pl.program_id(0)
    core, x_at, y_at, z_at = at_ref[0], at_ref[1] >> 1, at_ref[1] & 1, at_ref[2]
    blocks, pages, rows, width = ctx_ref.shape
    rows, width = 2 * rows, width // 2
    count = tok_ref.shape[0]
    b_out, b_outer, gain_one, shift_one, gain_two, shift_two = (vec_ref[i:i + 1] for i in range(6))

    w_outer = wu_ref[...].reshape(D, D)

    @pl.when(step == 0)
    def _():
        small_ref[...] = jnp.zeros_like(small_ref)
        ctx = jnp.concatenate(
            [jnp.concatenate([unfold(ctx_ref[b, p]) for b in range(blocks)], axis=1)
             for p in range(pages)], axis=0)
        ctx_all[...] = ctx
        pre = tok_ref[...].astype(WIDE) + (dot(ctx, wo_ref[...]) + b_out)
        unit, scale = normed(pre)
        unit_one[...] = unit
        scale_one[...] = jnp.broadcast_to(scale, scale_one.shape)
        value = unit * gain_one + shift_one
        first[...] = value
        first_low[...] = value.astype(LOW)

    @pl.when(step < cuts)
    def _():
        inner = dot(first_low[...], wi_ref[...]) + vec_ref[pl.ds(6 + step, 1)]
        half = 0.5 + 0.5 * lax.erf(inner * (0.5 ** 0.5))
        slope[step] = half + inner * (jnp.exp(inner * inner * -0.5) * ((0.5 / math.pi) ** 0.5))
        activated = (inner * half).astype(LOW)
        act[step] = activated
        product = dot(activated, w_outer)

        @pl.when(step == 0)
        def _():
            outer[...] = product

        @pl.when(step > 0)
        def _():
            outer[...] += product

    @pl.when(step == cuts - 1)
    def _():
        unit, scale = normed(first[...] + (outer[...] + b_outer))
        out_ref[...] = (unit * gain_two + shift_two).astype(LOW)
        cot = cot_ref[...].astype(WIDE)
        grad = normed_back(cot * gain_two, unit, scale)
        pre_two_grad[...] = grad
        low = grad.astype(LOW)
        outer_grad[...] = low
        small_ref[1:2] = summed(low.astype(WIDE))
        small_ref[4:5] = summed(cot * unit)
        small_ref[5:6] = summed(cot)

    def store_24(grad):
        cut = grad.reshape(4, 2, 2, 2, D // 32, D)
        for z in range(4):
            for x in range(2):
                for y in range(2):
                    slot = (0, x_at ^ x, y_at ^ y, z_at ^ z)
                    first, second = cut[z, x, y, 0], cut[z, x, y, 1]
                    grad_refs[2][slot] = jnp.where(core == 0, first, second).astype(LOW)
                    grad_refs[3][slot] = jnp.where(core == 0, second, first).astype(LOW)

    @pl.when((step >= cuts) & (step < 2 * cuts))
    def _():
        j = 2 * cuts - 1 - step
        low = outer_grad[...]
        d_outer = dot_tn(act[j], low).astype(LOW)
        inner_grad = (dot_nt(low, w_outer) * slope[j]).astype(LOW)
        small_ref[pl.ds(6 + j, 1)] = summed(inner_grad.astype(WIDE))
        d_inner = dot_tn(first_low[...], inner_grad)
        if split:
            cut = d_outer.reshape(2, 2, 2, D // 8, D)
            for x in range(2):
                for y in range(2):
                    slot = (0, x_at ^ x, y_at ^ y)
                    first, second = cut[x, y, 0], cut[x, y, 1]
                    grad_refs[0][slot] = jnp.where(core == 0, first, second)
                    grad_refs[1][slot] = jnp.where(core == 0, second, first)
            store_24(d_inner)
        else:
            grad_refs[0][...] = d_outer
            grad_refs[1][0] = d_inner.astype(LOW)
        product = dot_nt(inner_grad, wi_ref[...])

        @pl.when(step == cuts)
        def _():
            first_grad[...] = pre_two_grad[...] + product

        @pl.when(step > cuts)
        def _():
            first_grad[...] += product

    @pl.when(step == 2 * cuts)
    def _():
        grad = first_grad[...]
        unit = unit_one[...]
        small_ref[2:3] = summed(grad * unit)
        small_ref[3:4] = summed(grad)
        grad = normed_back(grad * gain_one, unit, scale_one[:, :1])
        pre_grad_ref[...] = grad
        low = grad.astype(LOW)
        small_ref[0:1] = summed(low.astype(WIDE))
        dctx = dot_nt(low, wo_ref[...]).astype(LOW)
        for b in range(blocks):
            for p in range(pages):
                dctx_ref[b, p] = fold(dctx[p * rows:(p + 1) * rows, b * width:(b + 1) * width])
        d_output = dot_tn(ctx_all[...], low)
        if split:
            store_24(d_output)
        else:
            grad_refs[1][0] = d_output.astype(LOW)


def second_half_call(split, at, ctx, tok, cot, w_output, vectors, w_inner, w_outer):
    blocks, pages, rows, width = ctx.shape
    count = 2 * pages * rows
    cuts = w_inner.shape[1] // D
    now = lambda i: jnp.where(i < cuts, i, jnp.maximum(2 * cuts - 1 - i, 0))
    late = lambda i: jnp.where(i < cuts, cuts - 1, jnp.maximum(2 * cuts - 1 - i, 0))
    last = lambda i: jnp.where(i < 2 * cuts, late(i), cuts)
    square, tall = (D, D), (count, D)
    eighth = (1, 2, 2, D // 8, D)
    slots = (1, 2, 2, 4, D // 32, D)
    if split:
        grad_specs = [pl.BlockSpec(eighth, lambda i, at: (late(i), 0, 0, 0, 0))] * 2
        grad_specs += [pl.BlockSpec(slots, lambda i, at: (last(i), 0, 0, 0, 0, 0))] * 2
        grads = [(cuts, 2, 2, D // 8, D)] * 2 + [(cuts + 1,) + slots[1:]] * 2
    else:
        grad_specs = [
            pl.BlockSpec(square, lambda i, at: (late(i), 0)),
            pl.BlockSpec((1,) + square, lambda i, at: (last(i), 0, 0))]
        grads = [(cuts * D, D), (cuts + 1,) + square]
    return pl.pallas_call(
        functools.partial(second_half_kernel, cuts, split),
        grid_spec=pltpu.PrefetchScalarGridSpec(
            num_scalar_prefetch=1,
            grid=(2 * cuts + 1,),
            in_specs=[
                whole(ctx.shape), whole(tall), whole(tall), whole(square), whole(vectors.shape),
                pl.BlockSpec(square, lambda i, at: (0, now(i))),
                pl.BlockSpec((8, D // 8, D), lambda i, at: (now(i), 0, 0))],
            out_specs=[whole(tall), whole(tall), whole(ctx.shape), *grad_specs, whole(vectors.shape)],
            scratch_shapes=[
                pltpu.VMEM(tall, LOW), pltpu.VMEM(tall, WIDE), pltpu.VMEM(tall, LOW),
                pltpu.VMEM(tall, WIDE), pltpu.VMEM((count, 128), WIDE), pltpu.VMEM((cuts,) + tall, LOW),
                pltpu.VMEM((cuts,) + tall, WIDE), pltpu.VMEM(tall, WIDE), pltpu.VMEM(tall, WIDE),
                pltpu.VMEM(tall, LOW), pltpu.VMEM(tall, WIDE)],
        ),
        out_shape=[
            jax.ShapeDtypeStruct(tall, LOW),
            jax.ShapeDtypeStruct(tall, WIDE),
            jax.ShapeDtypeStruct(ctx.shape, LOW),
            *(jax.ShapeDtypeStruct(shape, LOW) for shape in grads),
            jax.ShapeDtypeStruct(vectors.shape, WIDE),
        ],
        compiler_params=pltpu.CompilerParams(vmem_limit_bytes=VMEM_BYTES),
        cost_estimate=cost(20e9, 30e6),
        name="second_half",
    )(at, ctx, tok, cot, w_output, vectors, w_inner, w_outer)


def swap(value, axis, size, bit):
    return lax.ppermute(value, axis, [(i, i ^ bit) for i in range(size)])


def gather_slots(value):
    near = swap(value, "pb", 4, 1)
    far = swap(value, "pb", 4, 2)
    return (value, near, far, swap(far, "pb", 4, 1))


def hop(value, devices, bits):
    return lax.ppermute(value, AXES, [(i, i ^ bits) for i in range(devices)])


def added(*terms):
    return sum(term.astype(WIDE) for term in terms)


def sum_along_z(value, devices):
    return added(value[0], *(hop(value[j], devices, j << 3) for j in (1, 2, 3)))


def exchange_along_z(value, devices):
    lines = [[i + 8 * z for z in range(4)] for i in range(8)]
    return lax.all_to_all(value, AXES, 0, 0, tiled=True, axis_index_groups=lines)


def tie(*values):
    return lax.optimization_barrier(values)


def transpose_roles(value, pages, size):
    inner = pages // size
    pairs = []
    for hi in range(size):
        for lo in range(inner):
            for b in range(size):
                pairs.append(((hi * inner + lo) * size + b, (b * inner + lo) * size + hi))
    return lax.ppermute(value, AXES, pairs)


def sum_slots(kept, sent):
    total = added(kept, swap(sent, "pb", 4, 1))
    return total[0] + swap(total[1].astype(LOW), "pb", 4, 2).astype(WIDE)


def to_halves(place):
    cut = place.reshape(place.shape[:-1] + (2, 2, FREQ))
    return jnp.swapaxes(cut, -3, -2).reshape(place.shape)


def on_device(sizes, tokens, cotangent, boxes, resolution, padding,
              query_weight, keys_weight, values_weight, output_weight, query_place, keys_place,
              inner_weight, outer_weight, query_bias, keys_bias, values_bias, output_bias,
              inner_bias, outer_bias, first_gain, first_shift, second_gain, second_shift):
    page_size, pb_size = sizes
    devices = page_size * pb_size
    inner_pages = page_size // pb_size
    pages, rows, _ = tokens.shape
    count = rows * pb_size
    heads = HEADS // pb_size
    width = heads * HD
    own = query_weight.shape[0]
    ff_own = outer_weight.shape[0]
    ff = ff_own * devices
    cuts = ff // D
    me, page = lax.axis_index("pb"), lax.axis_index("page")
    place_at = (page % inner_pages) * pb_size + me
    number = page * pb_size + me
    me_array = me.astype(jnp.int32).reshape(1)
    by_link = (page_size, pb_size, own) == (8, 4, 24)

    at = jnp.stack([number & 1, (number >> 1) & 3, number >> 3, number, place_at]).astype(jnp.int32)
    small_rows = 16
    vectors = [output_bias, outer_bias, first_gain, first_shift, second_gain, second_shift]
    if by_link:
        lines = list(enumerate(vectors)) + [(8, inner_bias), (16, query_bias), (17, keys_bias), (18, values_bias)]
        lines = added(*(jnp.pad(line.astype(WIDE), (128 * i, 128 * (24 - i) - line.shape[0]))
                        for i, line in lines)).reshape(24, 128)
        packed, cols, mixed = pack_call(
            at, lines, query_weight, keys_weight, values_weight, query_place, keys_place,
            output_weight, inner_weight, outer_weight)
    else:
        cols = jnp.concatenate([query_weight, keys_weight, values_weight], axis=0)
        cols = cols.reshape(3 * own, pb_size, width).swapaxes(0, 1)
        bias_rows = jnp.zeros((3, width), LOW)
        bias_rows = lax.dynamic_update_slice(
            bias_rows, jnp.stack([query_bias, keys_bias, values_bias]), (0, place_at * own))
        bias_rows = jnp.pad(bias_rows.reshape(1, 3 * width), ((0, 7), (0, D - 3 * width)))
        mixed = jnp.concatenate([to_halves(query_place), to_halves(keys_place), bias_rows], axis=0)
        vectors = lax.dynamic_update_slice(jnp.zeros((6, D), LOW), jnp.stack(vectors), (0, number * own))
        b_inner = lax.dynamic_update_slice(jnp.zeros((ff,), LOW), inner_bias, (number * ff_own,))
        vectors = jnp.concatenate(
            [vectors, b_inner.reshape(cuts, D), jnp.zeros((small_rows - 6 - cuts, D), LOW)], axis=0)
        packed = jnp.concatenate(
            [outer_weight] + [inner_weight[:, j * D:(j + 1) * D] for j in range(cuts)]
            + [vectors, output_weight], axis=0)
    cols = lax.all_to_all(cols, "pb", 0, 0, tiled=True)
    cols = cols.swapaxes(0, 1).reshape(3 * own, D)
    mixed = transpose_roles(mixed, page_size, pb_size)
    mixed = jnp.concatenate([cols, mixed], axis=0)
    late = lax.all_gather(packed, AXES, axis=0)

    grid_x = (boxes[0] + boxes[2]) * 500 // resolution[0][:, None]
    grid_y = (boxes[1] + boxes[3]) * 500 // resolution[1][:, None]
    places = lax.all_gather(jnp.stack([grid_x, grid_y, padding]), "pb", axis=0)
    toks = gather_slots(tokens)

    places = jnp.stack([places[me ^ j] for j in range(pb_size)])
    places = places.transpose(1, 2, 0, 3).reshape(3, pages, count)
    rates = jnp.exp(jnp.arange(FREQ).astype(WIDE) * (-math.log(10000.0) / FREQ))
    grids = places[:2].astype(WIDE)
    angles = jnp.concatenate(
        [grids[0][..., None] * rates, grids[1][..., None] * rates], axis=-1)
    sines, cosines = jnp.sin(angles), jnp.cos(angles)
    alive = places[2][:, None, :]

    if by_link:
        mixed = jnp.stack([mixed] + [hop(mixed, devices, j << 3) for j in (1, 2, 3)])
        w_qkv, place_q, place_k, bias_qkv = assemble_call(
            at, mixed, hop(mixed, devices, 4), own, pb_size)
    else:
        mixed = lax.all_gather(mixed, "page", axis=0)
        w_qkv = mixed[:, :3 * own].reshape(page_size, 3, own, pb_size, width)
        w_qkv = w_qkv.transpose(0, 3, 2, 1, 4).reshape(D, 3 * width)
        bias_qkv = jnp.sum(mixed[:, 5 * own, :3 * width].astype(WIDE), axis=0, keepdims=True)
        mixed = mixed[:, 3 * own:5 * own].reshape(pb_size, inner_pages, 2, own, D)
        mixed = mixed.transpose(2, 1, 0, 3, 4).reshape(2, heads, HD, 2 * SPAN)
        place_q, place_k = mixed[0], mixed[1]

    qkv, soft, share, ctx_heads = attend_call(
        me_array, toks, w_qkv, bias_qkv, place_q, place_k, sines, cosines, alive)
    ctx = lax.all_to_all(ctx_heads, "pb", 0, 0, tiled=True)

    spot = ff_own
    w_inner = jnp.concatenate(
        [late[:, spot + j * own:spot + (j + 1) * own].reshape(D, D) for j in range(cuts)], axis=1)
    spot += cuts * own
    vectors = jnp.sum(late[:, spot:spot + small_rows].astype(WIDE), axis=0)
    w_output = late[:, spot + small_rows:].reshape(D, D)
    w_outer = late if by_link else late[:, :ff_own].reshape(8 * cuts, D // 8, D)

    tok = tokens.reshape(pages * rows, D)
    output, pre_one_grad, dctx, *grads, small = second_half_call(
        by_link, at, ctx, tok, cotangent.reshape(pages * rows, D), w_output, vectors, w_inner, w_outer)
    dctx = lax.all_to_all(dctx, "pb", 0, 0, tiled=True)

    if by_link:
        outer_kept, outer_sent, inner_kept, inner_sent = grads
        outer_core, inner_core = hop(outer_sent, devices, 1), hop(inner_sent, devices, 1)
        outer_sum = added(outer_kept, outer_core).astype(LOW)
        inner_far = added(inner_kept[:, 1], inner_core[:, 1]).astype(LOW)
        dctx, outer_sum, inner_far = tie(dctx, outer_sum, inner_far)
        outer_got, inner_far = exchange_along_z(outer_sum, devices), hop(inner_far, devices, 4)

    joined = (own, pb_size, page_size) if by_link else None
    me_array = jnp.stack([me, at[1] >> 1, at[2]]).astype(jnp.int32)
    kept, sent, *sums = attend_back_call(
        joined, me_array, toks, w_qkv, small, qkv, soft, share, ctx_heads, dctx, place_q, place_k, sines, cosines)

    if by_link:
        kept, sent, mixed, mixed_far, inner_far = tie(kept, sent, *sums, inner_far)
        mixed_far, sent = hop(mixed_far, devices, 4), hop(sent, devices, 1)
        inner_sent = added(inner_kept[:, 0, 1], inner_core[:, 0, 1], inner_far[:, 1]).astype(LOW)
        inner_sent = hop(inner_sent, devices, 2)
        inner_sum = added(inner_kept[:, 0, 0], inner_core[:, 0, 0], inner_far[:, 0])
        mixed, mixed_far, kept, sent, inner_sum, inner_sent, outer_got = tie(
            mixed, mixed_far, kept, sent, inner_sum, inner_sent, outer_got)
        mixed = added(mixed, mixed_far).astype(LOW)
        inner_sum = added(inner_sum, inner_sent).astype(LOW).swapaxes(0, 1).reshape(4, (cuts + 1) * own, D)
        mixed = jnp.concatenate([mixed, inner_sum], axis=1)
        mixed_z = [hop(mixed[j], devices, j << 3) for j in (1, 2, 3)]
        outer_sent = hop(added(*(outer_got[z, 1] for z in range(4))).astype(LOW), devices, 4)
        far = hop(added(kept[1], sent[1]).astype(LOW), devices, 2)
        outer_sum = added(*(outer_got[z, 0] for z in range(4)))
        mixed, kept, sent, far, outer_sum, outer_sent, *mixed_z = tie(
            mixed, kept, sent, far, outer_sum, outer_sent, *mixed_z)
        rest = 5 * own + 16
        inner_sum = added(mixed[0, rest:], *(got[rest:] for got in mixed_z)).reshape(cuts + 1, own, D)
        mixed = added(mixed[0, :rest], *(got[:rest] for got in mixed_z)).astype(LOW)
        small = mixed[5 * own:].reshape(16, pb_size, width).swapaxes(0, 1).reshape(1, 16 * pb_size, width)
        cols = mixed[:3 * own].reshape(3 * own, pb_size, width).swapaxes(0, 1)
        cols = jnp.concatenate([cols, jnp.broadcast_to(small, (pb_size,) + small.shape[1:])], axis=1)
        cols = jnp.stack([cols[me]] + [swap(cols[me ^ j], "pb", pb_size, j) for j in (1, 2, 3)])
        mixed = transpose_roles(mixed[3 * own:5 * own + 16], page_size, pb_size)
        outer_sum = added(outer_sum, outer_sent)
        outer_sent = hop(outer_sum[1].astype(LOW), devices, 2)
        tokens_grad = pre_one_grad.reshape(pages, rows, D) + added(kept[0], sent[0], far)
        d_outer = added(outer_sum[0], outer_sent)
        d_query, d_keys, d_values, d_place_q, d_place_k, lines = finish_call(at, cols, mixed)
        vectors = [lines[i, :own] for i in range(6)]
        d_b_inner = lines[8, :ff_own]
        d_bias = [lines[16 + i, :own] for i in range(3)]
        d_inner = jnp.concatenate([inner_sum[j] for j in range(cuts)], axis=1)
        d_output = inner_sum[cuts]
    else:
        d_outer = lax.psum_scatter(
            grads[0].reshape(devices, ff_own, D), AXES, scatter_dimension=0, tiled=False).astype(WIDE)
        inner_sum = grads[1].reshape(cuts + 1, devices, own, D).swapaxes(0, 1)
        inner_sum = lax.psum_scatter(inner_sum, AXES, scatter_dimension=0, tiled=False).astype(WIDE)
        d_inner = jnp.concatenate([inner_sum[j] for j in range(cuts)], axis=1)
        d_output = inner_sum[cuts]
        d_w, d_pq, d_pk, d_bias = sums
        d_w = d_w.reshape(page_size, pb_size, own, 3, width).transpose(0, 3, 2, 1, 4)
        d_w = d_w.reshape(page_size, 3 * own, D)
        d_p = jnp.stack([d_pq, d_pk]).reshape(2, inner_pages, pb_size, own, D)
        d_p = d_p.transpose(2, 1, 0, 3, 4).reshape(page_size, 2 * own, D)
        d_bias = jnp.pad(d_bias, ((0, 7), (0, D - 3 * width))).astype(LOW)
        d_bias = jnp.broadcast_to(d_bias[None], (page_size, 8, D))
        mixed = jnp.concatenate([d_w, d_p, d_bias], axis=1)
        mixed = lax.all_to_all(mixed, "page", 0, 0, tiled=True)
        mixed = jnp.sum(mixed.astype(WIDE), axis=0).astype(LOW)
        tokens_grad = pre_one_grad.reshape(pages, rows, D) + sum_slots(kept, sent)
        cols = mixed[:3 * own].reshape(3 * own, pb_size, width).swapaxes(0, 1)
        cols = lax.all_to_all(cols, "pb", 0, 0, tiled=True)
        d_query, d_keys, d_values = cols.swapaxes(0, 1).reshape(3, own, D).astype(WIDE)
        mixed = transpose_roles(mixed[3 * own:], page_size, pb_size)
        d_place_q, d_place_k = to_halves(mixed[:own].astype(WIDE)), to_halves(mixed[own:2 * own].astype(WIDE))
        d_bias = lax.dynamic_slice(
            mixed[2 * own, :3 * width].astype(WIDE).reshape(3, width), (0, place_at * own), (3, own))
        small = jnp.sum(lax.all_gather(small, AXES, axis=0), axis=0)
        d_b_inner = lax.dynamic_slice(small[6:6 + cuts].reshape(ff), (number * ff_own,), (ff_own,))
        vectors = lax.dynamic_slice(small, (0, number * own), (6, own))

    return (
        output.reshape(pages, rows, D),
        tokens_grad,
        d_query, d_keys, d_values,
        d_output,
        d_place_q, d_place_k,
        d_inner,
        d_outer.reshape(ff_own, D),
        d_bias[0], d_bias[1], d_bias[2],
        vectors[0], d_b_inner, vectors[1], vectors[2], vectors[3], vectors[4], vectors[5],
    )


def solution(mesh):
    rows, vector = P(AXES, None), P(AXES)
    token = P("page", "pb", None)
    in_specs = (token, token, P(None, "page", "pb"), P(None, "page"), P("page", "pb"))
    in_specs = in_specs + (rows,) * 8 + (vector,) * 10
    out_specs = (token, token) + (rows,) * 8 + (vector,) * 10
    sizes = (mesh.shape["page"], mesh.shape["pb"])
    return jax.shard_map(
        functools.partial(on_device, sizes), mesh=mesh, in_specs=in_specs, out_specs=out_specs,
        check_vma=False)
```

```python
import functools
import math

import jax
import jax.numpy as jnp
from jax import lax
from jax.experimental import pallas as pl
from jax.experimental.pallas import tpu as pltpu
from jax.sharding import PartitionSpec as P

HEADS = 12
HD = 64
FREQ = 192
D = HEADS * HD
SPAN = 2 * FREQ
SCALING = (3.0 * HD) ** (-0.5)
LOW = jnp.bfloat16
WIDE = jnp.float32
AXES = ("page", "pb")
VMEM_BYTES = 56 * 1024 * 1024


def dot(a, b):
    return jnp.dot(a, b, preferred_element_type=WIDE)


def dot_nt(a, b):
    return lax.dot_general(a, b, (((1,), (1,)), ((), ())), preferred_element_type=WIDE)


def dot_tn(a, b):
    return lax.dot_general(a, b, (((0,), (0,)), ((), ())), preferred_element_type=WIDE)


def whole(shape):
    return pl.BlockSpec(shape, lambda i, *_: (0,) * len(shape))


def cost(flops, bytes_accessed):
    return pl.CostEstimate(flops=int(flops), bytes_accessed=int(bytes_accessed), transcendentals=0)


def lanes_to(rows, length, start):
    lane = lax.broadcasted_iota(jnp.int32, rows.shape, 1)
    rows = jnp.where(lane < length, rows, 0.0)
    padded = jnp.concatenate([rows, jnp.zeros((rows.shape[0], D - rows.shape[1]), WIDE)], axis=1)
    return pltpu.roll(padded, start, 1)


def halves(place):
    cut = [place[:, i * FREQ:(i + 1) * FREQ] for i in (0, 2, 1, 3)]
    return jnp.concatenate(cut, axis=1)


def pack_kernel(size, at_ref, vec_ref, wq_ref, wk_ref, wv_ref, pq_ref, pk_ref, wo_ref, wi_ref, wu_ref,
                late_ref, cols_ref, mixed_ref):
    number, place_at = at_ref[3], at_ref[4]
    own, ff_own = wq_ref.shape[0], wu_ref.shape[0]
    cuts = wi_ref.shape[1] // D
    width = D // size
    vectors = vec_ref[...]
    lanes = lanes_to(vectors[:8], own, number * own)
    row = lax.broadcasted_iota(jnp.int32, lanes.shape, 0)
    first = jnp.where(row < 6, lanes, 0.0)
    inner = lanes_to(vectors[8:16], ff_own, lax.rem(number, D // ff_own) * ff_own)
    spot = lax.div(number, D // ff_own)
    for j in range(cuts):
        hit = (row == (6 + j) % 8) & (spot == j)
        if 6 + j < 8:
            first = first + jnp.where(hit, pltpu.roll(inner, 6 + j, 0), 0.0)
    second = jnp.zeros_like(first)
    for j in range(2, cuts):
        hit = (row == j - 2) & (spot == j)
        second = second + jnp.where(hit, pltpu.roll(inner, j - 2, 0), 0.0)
    wi = wi_ref[...].astype(WIDE)
    late = [wu_ref[...].astype(WIDE)] + [wi[:, j * D:(j + 1) * D] for j in range(cuts)]
    late += [first, second, wo_ref[...].astype(WIDE)]
    late_ref[...] = jnp.concatenate(late, axis=0).astype(LOW)
    cols = jnp.concatenate([ref[...].astype(WIDE) for ref in (wq_ref, wk_ref, wv_ref)], axis=0)
    for b in range(size):
        cols_ref[b] = cols[:, b * width:(b + 1) * width].astype(LOW)
    lanes = lanes_to(vectors[16:24], own, place_at * own)
    bias = jnp.concatenate(
        [lanes[i:i + 1, :width] for i in range(3)] + [jnp.zeros((1, D - 3 * width), WIDE)], axis=1)
    bias = jnp.concatenate([bias, jnp.zeros((7, D), WIDE)], axis=0)
    places = [halves(pq_ref[...].astype(WIDE)), halves(pk_ref[...].astype(WIDE)), bias]
    mixed_ref[...] = jnp.concatenate(places, axis=0).astype(LOW)


def pack_call(at, vectors, *weights):
    own, ff_own = weights[0].shape[0], weights[-1].shape[0]
    size = 4
    rows = ff_own + weights[-2].shape[1] // D * own + 16 + own
    return pl.pallas_call(
        functools.partial(pack_kernel, size),
        out_shape=[
            jax.ShapeDtypeStruct((rows, D), LOW),
            jax.ShapeDtypeStruct((size, 3 * own, D // size), LOW),
            jax.ShapeDtypeStruct((2 * own + 8, D), LOW),
        ],
        in_specs=[pl.BlockSpec(memory_space=pltpu.SMEM)]
        + [pl.BlockSpec(memory_space=pltpu.VMEM)] * (1 + len(weights)),
        compiler_params=pltpu.CompilerParams(vmem_limit_bytes=VMEM_BYTES),
        name="pack",
    )(at, vectors, *weights)


def finish_kernel(at_ref, cols_ref, mixed_ref, *out_refs):
    *grad_refs, lines_ref = out_refs
    number, place_at = at_ref[3], at_ref[4]
    own = grad_refs[0].shape[0]
    size, _, width = cols_ref.shape
    cols = [cols_ref[lax.rem(number, size) ^ b].astype(WIDE) for b in range(size)]
    for i in range(3):
        grad_refs[i][...] = jnp.concatenate([c[i * own:(i + 1) * own] for c in cols], axis=1)
    mixed = mixed_ref[...].astype(WIDE)
    for i in range(2):
        grad_refs[3 + i][...] = halves(mixed[i * own:(i + 1) * own])
    total = sum(c[3 * own:] for c in cols)
    quarters = [total[16 * i:16 * (i + 1)] for i in range(size)]
    rows = sum(jnp.where(lax.div(number, 8) == i, part, 0.0) for i, part in enumerate(quarters))
    rows = pltpu.roll(rows, lax.rem(width - lax.rem(number, 8) * own, width), 1)
    inner = sum(jnp.where(lax.div(lax.rem(number, 8), 2) == i, part, 0.0) for i, part in enumerate(quarters))
    inner = sum(jnp.where(lax.div(number, 8) == j, inner[6 + j:7 + j], 0.0) for j in range(4))
    inner = pltpu.roll(jnp.broadcast_to(inner, (8, width)), lax.rem(number, 2) * (width // 2), 1)
    bias = mixed[2 * own + 8:2 * own + 16]
    bias = jnp.concatenate([bias[2:3, i * width:(i + 1) * width] for i in range(3)] + [bias[:5, :width]], axis=0)
    bias = pltpu.roll(bias, lax.rem(width - place_at * own, width), 1)
    lines_ref[...] = jnp.concatenate([rows[:8, :128], inner[:, :128], bias[:, :128]], axis=0)


def finish_call(at, cols, mixed):
    own = (mixed.shape[0] - 16) // 2
    return pl.pallas_call(
        finish_kernel,
        out_shape=[jax.ShapeDtypeStruct((own, D), WIDE)] * 5 + [jax.ShapeDtypeStruct((24, 128), WIDE)],
        in_specs=[pl.BlockSpec(memory_space=pltpu.SMEM)] + [pl.BlockSpec(memory_space=pltpu.VMEM)] * 2,
        compiler_params=pltpu.CompilerParams(vmem_limit_bytes=20 * 1024 * 1024),
        name="finish",
    )(at, cols, mixed)


def assemble_kernel(own, size, at_ref, mine_ref, theirs_ref, w_ref, pq_ref, pk_ref, bias_ref, got):
    pages = got.shape[0]
    inner = pages // size
    width = D // size
    even = (at_ref[1] >> 1) == 0
    for z in range(pages // 2):
        mine, theirs = mine_ref[at_ref[2] ^ z].astype(WIDE), theirs_ref[at_ref[2] ^ z].astype(WIDE)
        got[2 * z] = jnp.where(even, mine, theirs)
        got[2 * z + 1] = jnp.where(even, theirs, mine)
    columns = []
    for part in range(3):
        rows = got[:, pl.ds(part * own, own)]
        cut = [rows[:, :, b * width:(b + 1) * width][:, None] for b in range(size)]
        columns.append(jnp.concatenate(cut, axis=1).reshape(D, width))
    w_ref[...] = jnp.concatenate(columns, axis=1).astype(LOW)
    for start, ref in ((3 * own, pq_ref), (4 * own, pk_ref)):
        order = [b * inner + lo for lo in range(inner) for b in range(size)]
        rows = jnp.concatenate([got[p, pl.ds(start, own)] for p in order], axis=0)
        ref[...] = rows.astype(LOW).reshape(ref.shape)
    bias_ref[...] = jnp.sum(got[:, pl.ds(5 * own, 8)], axis=0)[:1, :3 * width]


def assemble_call(at, mine, theirs, own, size):
    width = D // size
    place = (width // HD, HD, 2 * SPAN)
    return pl.pallas_call(
        functools.partial(assemble_kernel, own, size),
        out_shape=[
            jax.ShapeDtypeStruct((D, 3 * width), LOW),
            jax.ShapeDtypeStruct(place, LOW),
            jax.ShapeDtypeStruct(place, LOW),
            jax.ShapeDtypeStruct((1, 3 * width), WIDE),
        ],
        in_specs=[pl.BlockSpec(memory_space=pltpu.SMEM)] + [pl.BlockSpec(memory_space=pltpu.VMEM)] * 2,
        scratch_shapes=[pltpu.VMEM((2 * mine.shape[0],) + mine.shape[1:], WIDE)],
        compiler_params=pltpu.CompilerParams(vmem_limit_bytes=VMEM_BYTES),
        name="assemble",
    )(at, mine, theirs)


def fold(rows):
    half = rows.shape[0] // 2
    return jnp.concatenate([rows[:half], rows[half:]], axis=1)


def unfold(rows):
    half = rows.shape[1] // 2
    return jnp.concatenate([rows[:, :half], rows[:, half:]], axis=0)


def turn(spread, left, right):
    s, c = spread[:, :SPAN], spread[:, SPAN:]
    return jnp.concatenate(
        [(s * left + c * right).astype(LOW), (c * left - s * right).astype(LOW)], axis=1)


def turn_back(gradient, left, right):
    s, c = gradient[:, :SPAN], gradient[:, SPAN:]
    return jnp.concatenate(
        [(s * left - c * right).astype(LOW), (s * right + c * left).astype(LOW)], axis=1)


def feature_pair(sines, cosines):
    sines, cosines = sines.astype(LOW), cosines.astype(LOW)
    return (jnp.concatenate([sines, cosines], axis=1), jnp.concatenate([cosines, sines], axis=1))


def attend_kernel(heads, blocks, me_ref, *refs):
    tok_refs = refs[:blocks]
    (w_ref, bias_ref, pq_ref, pk_ref, sin_ref, cos_ref, alive_ref,
     qkv_ref, soft_ref, share_ref, ctx_ref) = refs[blocks:]
    rows = tok_refs[0].shape[1]
    width = heads * HD
    tok = jnp.concatenate([ref[0] for ref in tok_refs], axis=0)
    sines, cosines = sin_ref[0], cos_ref[0]
    key_feats, query_feats = feature_pair(sines, cosines)
    count = tok.shape[0]
    mask = jnp.broadcast_to(jnp.where(alive_ref[0] > 0, 0.0, -1e30), (128, count)).T[:, :HD]
    lane = lax.broadcasted_iota(jnp.int32, (count, HD), 1)
    mask = jnp.where(lane == 0, mask, 0.0).astype(LOW)
    ones = jnp.where(lane == 0, 1.0, 0.0).astype(LOW)
    qkv = (dot(tok, w_ref[...]) + bias_ref[...]).astype(LOW)
    qkv_ref[0] = qkv
    pieces = []
    for h in range(heads):
        q = qkv[:, h * HD:(h + 1) * HD]
        k = qkv[:, width + h * HD:width + (h + 1) * HD]
        v = qkv[:, 2 * width + h * HD:2 * width + (h + 1) * HD]
        turned_q = turn(dot(q, pq_ref[h]), cosines, sines)
        turned_k = turn(dot(k, pk_ref[h]), sines, cosines)
        raw = dot_nt(jnp.concatenate([turned_q, query_feats, q, ones], axis=1),
                     jnp.concatenate([key_feats, turned_k, k, mask], axis=1))
        lifted = jnp.exp2((raw - jnp.max(raw, axis=1, keepdims=True)) * (SCALING * math.log2(math.e)))
        share = 1.0 / jnp.sum(lifted, axis=1, keepdims=True)
        share_ref[0, :, h:h + 1] = share
        lifted = lifted.astype(LOW)
        soft_ref[0, h] = lifted
        pieces.append((dot(lifted, v) * share).astype(LOW))
    ctx = jnp.concatenate(pieces, axis=1)
    for j in range(blocks):
        ctx_ref[j, 0] = fold(ctx[j * rows:(j + 1) * rows])


def attend_call(me, toks, w_qkv, bias, place_q, place_k, sines, cosines, alive):
    blocks = len(toks)
    pages, rows, _ = toks[0].shape
    heads = place_q.shape[0]
    width = heads * HD
    count = blocks * rows
    by_page = lambda *shape: pl.BlockSpec((1,) + shape, lambda p, *_: (p,) + (0,) * len(shape))
    return pl.pallas_call(
        functools.partial(attend_kernel, heads, blocks),
        grid_spec=pltpu.PrefetchScalarGridSpec(
            num_scalar_prefetch=1,
            grid=(pages,),
            in_specs=[by_page(rows, D)] * blocks + [
                whole((D, 3 * width)), whole((1, 3 * width)),
                whole((heads, HD, 2 * SPAN)), whole((heads, HD, 2 * SPAN)),
                by_page(count, SPAN), by_page(count, SPAN), by_page(1, count)],
            out_specs=[
                by_page(count, 3 * width), by_page(heads, count, count), by_page(count, heads),
                pl.BlockSpec((blocks, 1, rows // 2, 2 * width), lambda p, *_: (0, p, 0, 0))],
        ),
        out_shape=[
            jax.ShapeDtypeStruct((pages, count, 3 * width), LOW),
            jax.ShapeDtypeStruct((pages, heads, count, count), LOW),
            jax.ShapeDtypeStruct((pages, count, heads), WIDE),
            jax.ShapeDtypeStruct((blocks, pages, rows // 2, 2 * width), LOW),
        ],
        compiler_params=pltpu.CompilerParams(vmem_limit_bytes=VMEM_BYTES),
        cost_estimate=cost(20e9, 20e6),
        name="attend",
    )(me, *toks, w_qkv, bias, place_q, place_k, sines, cosines, alive)


def joined_grads(own, size, pages, small, d_w, d_pq, d_pk, d_bias):
    inner = pages // size
    width = D // size
    cut = d_w.reshape(pages, size, own, 3 * width)
    parts = []
    for part in range(3):
        parts.append(jnp.concatenate(
            [cut[:, b, :, part * width:(part + 1) * width] for b in range(size)], axis=2))
    for place in (d_pq, d_pk):
        place = place.reshape(D // size, 2 * SPAN)
        order = [(lo * size + b) * own for b in range(size) for lo in range(inner)]
        parts.append(jnp.concatenate([place[at:at + own][None] for at in order], axis=0))
    row = jnp.concatenate([d_bias, jnp.zeros((1, D - 3 * width), WIDE)], axis=1)
    at = lax.broadcasted_iota(jnp.int32, small.shape, 0)
    rows = jnp.where(at == 10, row, jnp.where(at < 10, small, 0.0))
    parts.append(jnp.broadcast_to(rows[None], (pages,) + rows.shape))
    return jnp.concatenate(parts, axis=1).astype(LOW)


def attend_back_kernel(heads, blocks, joined, me_ref, *refs):
    tok_refs = refs[:blocks]
    (w_ref, small_ref, qkv_ref, soft_ref, share_ref, ctx_ref, dctx_ref, pq_ref, pk_ref, sin_ref, cos_ref,
     kept_ref, sent_ref, *out_refs, dw_sum, dpq_sum, dpk_sum, db_sum) = refs[blocks:]
    step, last = pl.program_id(0), pl.num_programs(0) - 1
    rows = tok_refs[0].shape[1]
    width = heads * HD
    sines, cosines = sin_ref[0], cos_ref[0]
    key_feats, query_feats = feature_pair(sines, cosines)
    qkv = qkv_ref[0]
    dctx = jnp.concatenate([unfold(dctx_ref[me_ref[0] ^ j, 0]) for j in range(blocks)], axis=0)
    ctx = jnp.concatenate([unfold(ctx_ref[j, 0]) for j in range(blocks)], axis=0)
    along = dctx.astype(WIDE) * ctx.astype(WIDE)

    @pl.when(step == 0)
    def _():
        for ref in (dw_sum, dpq_sum, dpk_sum, db_sum):
            ref[...] = jnp.zeros_like(ref)

    d_q, d_k, d_v = [], [], []
    for h in range(heads):
        q = qkv[:, h * HD:(h + 1) * HD]
        k = qkv[:, width + h * HD:width + (h + 1) * HD]
        v = qkv[:, 2 * width + h * HD:2 * width + (h + 1) * HD]
        dc = dctx[:, h * HD:(h + 1) * HD]
        share = share_ref[0, :, h:h + 1]
        lifted = soft_ref[0, h]
        row_dot = jnp.sum(along[:, h * HD:(h + 1) * HD], axis=1, keepdims=True)
        raw_grad = ((dot_nt(dc, v) - row_dot) * (share * SCALING) * lifted.astype(WIDE)).astype(LOW)
        d_v.append(dot_tn(lifted, (dc.astype(WIDE) * share).astype(LOW)).astype(LOW))
        turned = dot(raw_grad, jnp.concatenate([key_feats, k], axis=1))
        spread_q = turn_back(turned[:, :2 * SPAN], cosines, sines)
        d_q.append((turned[:, 2 * SPAN:] + dot_nt(spread_q, pq_ref[h])).astype(LOW))
        dpq_sum[h] += dot_tn(q, spread_q)
        turned = dot_tn(raw_grad, jnp.concatenate([query_feats, q], axis=1))
        spread_k = turn_back(turned[:, :2 * SPAN], sines, cosines)
        d_k.append((turned[:, 2 * SPAN:] + dot_nt(spread_k, pk_ref[h])).astype(LOW))
        dpk_sum[h] += dot_tn(k, spread_k)
    dqkv = jnp.concatenate(d_q + d_k + d_v, axis=1)
    db_sum[...] += jnp.sum(dqkv.astype(WIDE), axis=0, keepdims=True)
    tok = jnp.concatenate([ref[0] for ref in tok_refs], axis=0)
    dw_sum[...] += dot_tn(tok, dqkv)
    part = dot_nt(dqkv, w_ref[...]).astype(LOW)
    for j in range(blocks):
        (sent_ref if j % 2 else kept_ref)[j // 2, 0] = part[j * rows:(j + 1) * rows]

    @pl.when(step == last)
    def _():
        if joined:
            rows = joined_grads(*joined, small_ref[...], dw_sum[...], dpq_sum[...], dpk_sum[...], db_sum[...])
            even = me_ref[1] == 0
            for z in range(rows.shape[0] // 2):
                first, second = rows[2 * z], rows[2 * z + 1]
                out_refs[0][me_ref[2] ^ z] = jnp.where(even, first, second)
                out_refs[1][me_ref[2] ^ z] = jnp.where(even, second, first)
        else:
            for ref, total in zip(out_refs, (dw_sum, dpq_sum, dpk_sum, db_sum)):
                ref[...] = total[...].astype(ref.dtype)


def attend_back_call(joined, me, toks, w_qkv, small, qkv, soft, share, ctx, dctx, place_q, place_k, sines, cosines):
    blocks, pages, rows, width = dctx.shape
    rows, width = 2 * rows, width // 2
    heads = place_q.shape[0]
    count = blocks * rows
    by_page = lambda *shape: pl.BlockSpec((1,) + shape, lambda p, *_: (p,) + (0,) * len(shape))
    place = (heads, HD, 2 * SPAN)
    if joined:
        own, _, owners = joined
        sums = [jax.ShapeDtypeStruct((owners // 2, 5 * own + 16, D), LOW)] * 2
    else:
        sums = [jax.ShapeDtypeStruct((D, 3 * width), LOW), jax.ShapeDtypeStruct(place, LOW),
                jax.ShapeDtypeStruct(place, LOW), jax.ShapeDtypeStruct((1, 3 * width), WIDE)]
    return pl.pallas_call(
        functools.partial(attend_back_kernel, heads, blocks, joined),
        grid_spec=pltpu.PrefetchScalarGridSpec(
            num_scalar_prefetch=1,
            grid=(pages,),
            in_specs=[by_page(rows, D)] * blocks + [
                whole((D, 3 * width)), whole(small.shape),
                by_page(count, 3 * width), by_page(heads, count, count), by_page(count, heads),
                pl.BlockSpec((blocks, 1, rows // 2, 2 * width), lambda p, *_: (0, p, 0, 0)),
                pl.BlockSpec((blocks, 1, rows // 2, 2 * width), lambda p, *_: (0, p, 0, 0)),
                whole(place), whole(place), by_page(count, SPAN), by_page(count, SPAN)],
            out_specs=[
                *[pl.BlockSpec((blocks // 2, 1, rows, D), lambda p, *_: (0, p, 0, 0))] * 2,
                *(whole(item.shape) for item in sums)],
            scratch_shapes=[
                pltpu.VMEM((D, 3 * width), WIDE), pltpu.VMEM(place, WIDE), pltpu.VMEM(place, WIDE),
                pltpu.VMEM((1, 3 * width), WIDE)],
        ),
        out_shape=[*[jax.ShapeDtypeStruct((blocks // 2, pages, rows, D), LOW)] * 2, *sums],
        compiler_params=pltpu.CompilerParams(vmem_limit_bytes=VMEM_BYTES),
        cost_estimate=cost(30e9, 20e6),
        name="attend_back",
    )(me, *toks, w_qkv, small, qkv, soft, share, ctx, dctx, place_q, place_k, sines, cosines)


def normed(values):
    centred = values - jnp.mean(values, axis=1, keepdims=True)
    scale = lax.rsqrt(jnp.mean(centred * centred, axis=1, keepdims=True) + 1e-05)
    return centred * scale, scale


def normed_back(gradient, unit, scale):
    mean = jnp.mean(gradient, axis=1, keepdims=True)
    along = jnp.mean(gradient * unit, axis=1, keepdims=True)
    return scale * (gradient - mean - unit * along)


def summed(values):
    return jnp.sum(values, axis=0, keepdims=True)


def second_half_kernel(cuts, split, at_ref, ctx_ref, tok_ref, cot_ref, wo_ref, vec_ref, wi_ref, *refs):
    n_grads = 4 if split else 2
    wu_ref, out_ref, pre_grad_ref, dctx_ref = refs[:4]
    grad_refs = refs[4:4 + n_grads]
    (small_ref, ctx_all, first, first_low, unit_one, scale_one, act, slope, outer, pre_two_grad,
     outer_grad, first_grad) = refs[4 + n_grads:]
    step = pl.program_id(0)
    core, x_at, y_at, z_at = at_ref[0], at_ref[1] >> 1, at_ref[1] & 1, at_ref[2]
    here = lax.rem(at_ref[3], ctx_ref.shape[0])
    blocks, pages, rows, width = ctx_ref.shape
    rows, width = 2 * rows, width // 2
    count = tok_ref.shape[0]
    b_out, b_outer, gain_one, shift_one, gain_two, shift_two = (vec_ref[i:i + 1] for i in range(6))

    w_outer = wu_ref[...].reshape(D, D)

    @pl.when(step == 0)
    def _():
        small_ref[...] = jnp.zeros_like(small_ref)
        ctx = jnp.concatenate(
            [jnp.concatenate([unfold(ctx_ref[here ^ b, p]) for b in range(blocks)], axis=1)
             for p in range(pages)], axis=0)
        ctx_all[...] = ctx
        pre = tok_ref[...].astype(WIDE) + (dot(ctx, wo_ref[...]) + b_out)
        unit, scale = normed(pre)
        unit_one[...] = unit
        scale_one[...] = jnp.broadcast_to(scale, scale_one.shape)
        value = unit * gain_one + shift_one
        first[...] = value
        first_low[...] = value.astype(LOW)

    @pl.when(step < cuts)
    def _():
        inner = dot(first_low[...], wi_ref[0]) + vec_ref[pl.ds(6 + step, 1)]
        half = 0.5 + 0.5 * lax.erf(inner * (0.5 ** 0.5))
        slope[step] = half + inner * (jnp.exp(inner * inner * -0.5) * ((0.5 / math.pi) ** 0.5))
        activated = (inner * half).astype(LOW)
        act[step] = activated
        product = dot(activated, w_outer)

        @pl.when(step == 0)
        def _():
            outer[...] = product

        @pl.when(step > 0)
        def _():
            outer[...] += product

    @pl.when(step == cuts - 1)
    def _():
        unit, scale = normed(first[...] + (outer[...] + b_outer))
        out_ref[...] = (unit * gain_two + shift_two).astype(LOW)
        cot = cot_ref[...].astype(WIDE)
        grad = normed_back(cot * gain_two, unit, scale)
        pre_two_grad[...] = grad
        low = grad.astype(LOW)
        outer_grad[...] = low
        small_ref[1:2] = summed(low.astype(WIDE))
        small_ref[4:5] = summed(cot * unit)
        small_ref[5:6] = summed(cot)

    def store_24(grad):
        cut = grad.reshape(4, 2, 2, 2, D // 32, D)
        for z in range(4):
            for x in range(2):
                for y in range(2):
                    slot = (0, x_at ^ x, y_at ^ y, z_at ^ z)
                    first, second = cut[z, x, y, 0], cut[z, x, y, 1]
                    grad_refs[2][slot] = jnp.where(core == 0, first, second).astype(LOW)
                    grad_refs[3][slot] = jnp.where(core == 0, second, first).astype(LOW)

    @pl.when((step >= cuts) & (step < 2 * cuts))
    def _():
        j = 2 * cuts - 1 - step
        low = outer_grad[...]
        d_outer = dot_tn(act[j], low).astype(LOW)
        inner_grad = (dot_nt(low, w_outer) * slope[j]).astype(LOW)
        small_ref[pl.ds(6 + j, 1)] = summed(inner_grad.astype(WIDE))
        d_inner = dot_tn(first_low[...], inner_grad)
        if split:
            cut = d_outer.reshape(2, 2, 2, D // 8, D)
            for x in range(2):
                for y in range(2):
                    slot = (0, x_at ^ x, y_at ^ y)
                    first, second = cut[x, y, 0], cut[x, y, 1]
                    grad_refs[0][slot] = jnp.where(core == 0, first, second)
                    grad_refs[1][slot] = jnp.where(core == 0, second, first)
            store_24(d_inner)
        else:
            grad_refs[0][...] = d_outer
            grad_refs[1][0] = d_inner.astype(LOW)
        product = dot_nt(inner_grad, wi_ref[0])

        @pl.when(step == cuts)
        def _():
            first_grad[...] = pre_two_grad[...] + product

        @pl.when(step > cuts)
        def _():
            first_grad[...] += product

    @pl.when(step == 2 * cuts)
    def _():
        grad = first_grad[...]
        unit = unit_one[...]
        small_ref[2:3] = summed(grad * unit)
        small_ref[3:4] = summed(grad)
        grad = normed_back(grad * gain_one, unit, scale_one[:, :1])
        pre_grad_ref[...] = grad
        low = grad.astype(LOW)
        small_ref[0:1] = summed(low.astype(WIDE))
        dctx = dot_nt(low, wo_ref[...]).astype(LOW)
        for b in range(blocks):
            for p in range(pages):
                dctx_ref[b, p] = fold(dctx[p * rows:(p + 1) * rows, b * width:(b + 1) * width])
        d_output = dot_tn(ctx_all[...], low)
        if split:
            store_24(d_output)
        else:
            grad_refs[1][0] = d_output.astype(LOW)


def second_half_call(split, at, ctx, tok, cot, w_output, vectors, w_inner, w_outer):
    blocks, pages, rows, width = ctx.shape
    count = 2 * pages * rows
    cuts = w_inner.shape[0]
    now = lambda i: jnp.where(i < cuts, i, jnp.maximum(2 * cuts - 1 - i, 0))
    late = lambda i: jnp.where(i < cuts, cuts - 1, jnp.maximum(2 * cuts - 1 - i, 0))
    last = lambda i: jnp.where(i < 2 * cuts, late(i), cuts)
    square, tall = (D, D), (count, D)
    eighth = (1, 2, 2, D // 8, D)
    slots = (1, 2, 2, 4, D // 32, D)
    if split:
        grad_specs = [pl.BlockSpec(eighth, lambda i, at: (late(i) ^ at[2], 0, 0, 0, 0))] * 2
        grad_specs += [pl.BlockSpec(slots, lambda i, at: (last(i), 0, 0, 0, 0, 0))] * 2
        grads = [(cuts, 2, 2, D // 8, D)] * 2 + [(cuts + 1,) + slots[1:]] * 2
    else:
        grad_specs = [
            pl.BlockSpec(square, lambda i, at: (late(i), 0)),
            pl.BlockSpec((1,) + square, lambda i, at: (last(i), 0, 0))]
        grads = [(cuts * D, D), (cuts + 1,) + square]
    return pl.pallas_call(
        functools.partial(second_half_kernel, cuts, split),
        grid_spec=pltpu.PrefetchScalarGridSpec(
            num_scalar_prefetch=1,
            grid=(2 * cuts + 1,),
            in_specs=[
                whole(ctx.shape), whole(tall), whole(tall), whole(square), whole(vectors.shape),
                pl.BlockSpec((1,) + square, lambda i, at: (now(i), 0, 0)),
                pl.BlockSpec((8, D // 8, D), lambda i, at: (now(i), 0, 0))],
            out_specs=[whole(tall), whole(tall), whole(ctx.shape), *grad_specs, whole(vectors.shape)],
            scratch_shapes=[
                pltpu.VMEM(tall, LOW), pltpu.VMEM(tall, WIDE), pltpu.VMEM(tall, LOW),
                pltpu.VMEM(tall, WIDE), pltpu.VMEM((count, 128), WIDE), pltpu.VMEM((cuts,) + tall, LOW),
                pltpu.VMEM((cuts,) + tall, WIDE), pltpu.VMEM(tall, WIDE), pltpu.VMEM(tall, WIDE),
                pltpu.VMEM(tall, LOW), pltpu.VMEM(tall, WIDE)],
        ),
        out_shape=[
            jax.ShapeDtypeStruct(tall, LOW),
            jax.ShapeDtypeStruct(tall, WIDE),
            jax.ShapeDtypeStruct(ctx.shape, LOW),
            *(jax.ShapeDtypeStruct(shape, LOW) for shape in grads),
            jax.ShapeDtypeStruct(vectors.shape, WIDE),
        ],
        compiler_params=pltpu.CompilerParams(vmem_limit_bytes=44 * 1024 * 1024),
        cost_estimate=cost(20e9, 30e6),
        name="second_half",
    )(at, ctx, tok, cot, w_output, vectors, w_inner, w_outer)


def swap(value, axis, size, bit):
    return lax.ppermute(value, axis, [(i, i ^ bit) for i in range(size)])


def exchange_slots(value):
    return jnp.stack([value[0]] + [swap(value[j], "pb", 4, j) for j in (1, 2, 3)])


def gather_slots(value):
    near = swap(value, "pb", 4, 1)
    far = swap(value, "pb", 4, 2)
    return (value, near, far, swap(far, "pb", 4, 1))


def hop(value, devices, bits):
    return lax.ppermute(value, AXES, [(i, i ^ bits) for i in range(devices)])


def added(*terms):
    return sum(term.astype(WIDE) for term in terms)


def sum_along_z(value, devices):
    return added(value[0], *(hop(value[j], devices, j << 3) for j in (1, 2, 3)))


def tie(*values):
    return lax.optimization_barrier(values)


def transpose_roles(value, pages, size):
    inner = pages // size
    pairs = []
    for hi in range(size):
        for lo in range(inner):
            for b in range(size):
                pairs.append(((hi * inner + lo) * size + b, (b * inner + lo) * size + hi))
    return lax.ppermute(value, AXES, pairs)


def sum_slots(kept, sent):
    total = added(kept, swap(sent, "pb", 4, 1))
    return total[0] + swap(total[1].astype(LOW), "pb", 4, 2).astype(WIDE)


def to_halves(place):
    cut = place.reshape(place.shape[:-1] + (2, 2, FREQ))
    return jnp.swapaxes(cut, -3, -2).reshape(place.shape)


def on_device(sizes, tokens, cotangent, boxes, resolution, padding,
              query_weight, keys_weight, values_weight, output_weight, query_place, keys_place,
              inner_weight, outer_weight, query_bias, keys_bias, values_bias, output_bias,
              inner_bias, outer_bias, first_gain, first_shift, second_gain, second_shift):
    page_size, pb_size = sizes
    devices = page_size * pb_size
    inner_pages = page_size // pb_size
    pages, rows, _ = tokens.shape
    count = rows * pb_size
    heads = HEADS // pb_size
    width = heads * HD
    own = query_weight.shape[0]
    ff_own = outer_weight.shape[0]
    ff = ff_own * devices
    cuts = ff // D
    me, page = lax.axis_index("pb"), lax.axis_index("page")
    place_at = (page % inner_pages) * pb_size + me
    number = page * pb_size + me
    me_array = me.astype(jnp.int32).reshape(1)
    by_link = (page_size, pb_size, own) == (8, 4, 24)

    at = jnp.stack([number & 1, (number >> 1) & 3, number >> 3, number, place_at]).astype(jnp.int32)
    small_rows = 16
    vectors = [output_bias, outer_bias, first_gain, first_shift, second_gain, second_shift]
    if by_link:
        lines = list(enumerate(vectors)) + [(8, inner_bias), (16, query_bias), (17, keys_bias), (18, values_bias)]
        lines = added(*(jnp.pad(line.astype(WIDE), (128 * i, 128 * (24 - i) - line.shape[0]))
                        for i, line in lines)).reshape(24, 128)
        packed, cols, mixed = pack_call(
            at, lines, query_weight, keys_weight, values_weight, query_place, keys_place,
            output_weight, inner_weight, outer_weight)
    else:
        cols = jnp.concatenate([query_weight, keys_weight, values_weight], axis=0)
        cols = cols.reshape(3 * own, pb_size, width).swapaxes(0, 1)
        bias_rows = jnp.zeros((3, width), LOW)
        bias_rows = lax.dynamic_update_slice(
            bias_rows, jnp.stack([query_bias, keys_bias, values_bias]), (0, place_at * own))
        bias_rows = jnp.pad(bias_rows.reshape(1, 3 * width), ((0, 7), (0, D - 3 * width)))
        mixed = jnp.concatenate([to_halves(query_place), to_halves(keys_place), bias_rows], axis=0)
        vectors = lax.dynamic_update_slice(jnp.zeros((6, D), LOW), jnp.stack(vectors), (0, number * own))
        b_inner = lax.dynamic_update_slice(jnp.zeros((ff,), LOW), inner_bias, (number * ff_own,))
        vectors = jnp.concatenate(
            [vectors, b_inner.reshape(cuts, D), jnp.zeros((small_rows - 6 - cuts, D), LOW)], axis=0)
        packed = jnp.concatenate(
            [outer_weight] + [inner_weight[:, j * D:(j + 1) * D] for j in range(cuts)]
            + [vectors, output_weight], axis=0)
    cols = lax.all_to_all(cols, "pb", 0, 0, tiled=True)
    cols = cols.swapaxes(0, 1).reshape(3 * own, D)
    mixed = transpose_roles(mixed, page_size, pb_size)
    mixed = jnp.concatenate([cols, mixed], axis=0)
    late = lax.all_gather(packed, AXES, axis=0)

    grid_x = (boxes[0] + boxes[2]) * 500 // resolution[0][:, None]
    grid_y = (boxes[1] + boxes[3]) * 500 // resolution[1][:, None]
    places = lax.all_gather(jnp.stack([grid_x, grid_y, padding]), "pb", axis=0)
    toks = gather_slots(tokens)

    places = jnp.stack([places[me ^ j] for j in range(pb_size)])
    places = places.transpose(1, 2, 0, 3).reshape(3, pages, count)
    rates = jnp.exp(jnp.arange(FREQ).astype(WIDE) * (-math.log(10000.0) / FREQ))
    grids = places[:2].astype(WIDE)
    angles = jnp.concatenate(
        [grids[0][..., None] * rates, grids[1][..., None] * rates], axis=-1)
    sines, cosines = jnp.sin(angles), jnp.cos(angles)
    alive = places[2][:, None, :]

    if by_link:
        mixed = jnp.stack([mixed] + [hop(mixed, devices, j << 3) for j in (1, 2, 3)])
        w_qkv, place_q, place_k, bias_qkv = assemble_call(
            at, mixed, hop(mixed, devices, 4), own, pb_size)
    else:
        mixed = lax.all_gather(mixed, "page", axis=0)
        w_qkv = mixed[:, :3 * own].reshape(page_size, 3, own, pb_size, width)
        w_qkv = w_qkv.transpose(0, 3, 2, 1, 4).reshape(D, 3 * width)
        bias_qkv = jnp.sum(mixed[:, 5 * own, :3 * width].astype(WIDE), axis=0, keepdims=True)
        mixed = mixed[:, 3 * own:5 * own].reshape(pb_size, inner_pages, 2, own, D)
        mixed = mixed.transpose(2, 1, 0, 3, 4).reshape(2, heads, HD, 2 * SPAN)
        place_q, place_k = mixed[0], mixed[1]

    qkv, soft, share, ctx_heads = attend_call(
        me_array, toks, w_qkv, bias_qkv, place_q, place_k, sines, cosines, alive)
    ctx = exchange_slots(ctx_heads)

    spot = ff_own
    w_inner = late[:, spot:spot + cuts * own].reshape(devices, cuts, own, D)
    w_inner = w_inner.swapaxes(0, 1).reshape(cuts, D, D)
    spot += cuts * own
    vectors = jnp.sum(late[:, spot:spot + small_rows].astype(WIDE), axis=0)
    w_output = late[:, spot + small_rows:].reshape(D, D)
    w_outer = late if by_link else late[:, :ff_own].reshape(8 * cuts, D // 8, D)

    tok = tokens.reshape(pages * rows, D)
    output, pre_one_grad, dctx, *grads, small = second_half_call(
        by_link, at, ctx, tok, cotangent.reshape(pages * rows, D), w_output, vectors, w_inner, w_outer)
    dctx = lax.all_to_all(dctx, "pb", 0, 0, tiled=True)

    if by_link:
        outer_kept, outer_sent, inner_kept, inner_sent = grads
        outer_core, inner_core = hop(outer_sent, devices, 1), hop(inner_sent, devices, 1)
        outer_sum = added(outer_kept, outer_core).astype(LOW)
        inner_far = added(inner_kept[:, 1], inner_core[:, 1]).astype(LOW)
        outer_got = [outer_sum[0]] + [hop(outer_sum[j], devices, j << 3) for j in (1, 2, 3)]
        dctx, outer_got[0], far = tie(dctx, outer_got[0], inner_far)
        inner_far = hop(inner_far, devices, 4)

    joined = (own, pb_size, page_size) if by_link else None
    me_array = jnp.stack([me, at[1] >> 1, at[2]]).astype(jnp.int32)
    kept, sent, *sums = attend_back_call(
        joined, me_array, toks, w_qkv, small, qkv, soft, share, ctx_heads, dctx, place_q, place_k, sines, cosines)

    if by_link:
        kept, sent, mixed, mixed_far, inner_far = tie(kept, sent, *sums, inner_far)
        mixed_far, sent = hop(mixed_far, devices, 4), hop(sent, devices, 1)
        inner_sent = added(inner_kept[:, 0, 1], inner_core[:, 0, 1], inner_far[:, 1]).astype(LOW)
        inner_sent = hop(inner_sent, devices, 2)
        inner_sum = added(inner_kept[:, 0, 0], inner_core[:, 0, 0], inner_far[:, 0])
        mixed, mixed_far, kept, sent, inner_sum, inner_sent, *outer_got = tie(
            mixed, mixed_far, kept, sent, inner_sum, inner_sent, *outer_got)
        mixed = added(mixed, mixed_far).astype(LOW)
        inner_sum = added(inner_sum, inner_sent).astype(LOW).swapaxes(0, 1).reshape(4, (cuts + 1) * own, D)
        mixed = jnp.concatenate([mixed, inner_sum], axis=1)
        mixed_z = [hop(mixed[j], devices, j << 3) for j in (1, 2, 3)]
        outer_sent = hop(added(*(got[1] for got in outer_got)).astype(LOW), devices, 4)
        far = hop(added(kept[1], sent[1]).astype(LOW), devices, 2)
        outer_sum = added(*(got[0] for got in outer_got))
        mixed, kept, sent, far, outer_sum, outer_sent, *mixed_z = tie(
            mixed, kept, sent, far, outer_sum, outer_sent, *mixed_z)
        rest = 5 * own + 16
        inner_sum = added(mixed[0, rest:], *(got[rest:] for got in mixed_z)).reshape(cuts + 1, own, D)
        mixed = added(mixed[0, :rest], *(got[:rest] for got in mixed_z)).astype(LOW)
        small = mixed[5 * own:].reshape(16, pb_size, width).swapaxes(0, 1).reshape(1, 16 * pb_size, width)
        cols = mixed[:3 * own].reshape(3 * own, pb_size, width).swapaxes(0, 1)
        cols = jnp.concatenate([cols, jnp.broadcast_to(small, (pb_size,) + small.shape[1:])], axis=1)
        cols = jnp.stack([cols[me]] + [swap(cols[me ^ j], "pb", pb_size, j) for j in (1, 2, 3)])
        mixed = transpose_roles(mixed[3 * own:5 * own + 16], page_size, pb_size)
        outer_sum = added(outer_sum, outer_sent)
        outer_sent = hop(outer_sum[1].astype(LOW), devices, 2)
        tokens_grad = pre_one_grad.reshape(pages, rows, D) + added(kept[0], sent[0], far)
        d_outer = added(outer_sum[0], outer_sent)
        d_query, d_keys, d_values, d_place_q, d_place_k, lines = finish_call(at, cols, mixed)
        vectors = [lines[i, :own] for i in range(6)]
        d_b_inner = lines[8, :ff_own]
        d_bias = [lines[16 + i, :own] for i in range(3)]
        d_inner = jnp.concatenate([inner_sum[j] for j in range(cuts)], axis=1)
        d_output = inner_sum[cuts]
    else:
        d_outer = lax.psum_scatter(
            grads[0].reshape(devices, ff_own, D), AXES, scatter_dimension=0, tiled=False).astype(WIDE)
        inner_sum = grads[1].reshape(cuts + 1, devices, own, D).swapaxes(0, 1)
        inner_sum = lax.psum_scatter(inner_sum, AXES, scatter_dimension=0, tiled=False).astype(WIDE)
        d_inner = jnp.concatenate([inner_sum[j] for j in range(cuts)], axis=1)
        d_output = inner_sum[cuts]
        d_w, d_pq, d_pk, d_bias = sums
        d_w = d_w.reshape(page_size, pb_size, own, 3, width).transpose(0, 3, 2, 1, 4)
        d_w = d_w.reshape(page_size, 3 * own, D)
        d_p = jnp.stack([d_pq, d_pk]).reshape(2, inner_pages, pb_size, own, D)
        d_p = d_p.transpose(2, 1, 0, 3, 4).reshape(page_size, 2 * own, D)
        d_bias = jnp.pad(d_bias, ((0, 7), (0, D - 3 * width))).astype(LOW)
        d_bias = jnp.broadcast_to(d_bias[None], (page_size, 8, D))
        mixed = jnp.concatenate([d_w, d_p, d_bias], axis=1)
        mixed = lax.all_to_all(mixed, "page", 0, 0, tiled=True)
        mixed = jnp.sum(mixed.astype(WIDE), axis=0).astype(LOW)
        tokens_grad = pre_one_grad.reshape(pages, rows, D) + sum_slots(kept, sent)
        cols = mixed[:3 * own].reshape(3 * own, pb_size, width).swapaxes(0, 1)
        cols = lax.all_to_all(cols, "pb", 0, 0, tiled=True)
        d_query, d_keys, d_values = cols.swapaxes(0, 1).reshape(3, own, D).astype(WIDE)
        mixed = transpose_roles(mixed[3 * own:], page_size, pb_size)
        d_place_q, d_place_k = to_halves(mixed[:own].astype(WIDE)), to_halves(mixed[own:2 * own].astype(WIDE))
        d_bias = lax.dynamic_slice(
            mixed[2 * own, :3 * width].astype(WIDE).reshape(3, width), (0, place_at * own), (3, own))
        small = jnp.sum(lax.all_gather(small, AXES, axis=0), axis=0)
        d_b_inner = lax.dynamic_slice(small[6:6 + cuts].reshape(ff), (number * ff_own,), (ff_own,))
        vectors = lax.dynamic_slice(small, (0, number * own), (6, own))

    return (
        output.reshape(pages, rows, D),
        tokens_grad,
        d_query, d_keys, d_values,
        d_output,
        d_place_q, d_place_k,
        d_inner,
        d_outer.reshape(ff_own, D),
        d_bias[0], d_bias[1], d_bias[2],
        vectors[0], d_b_inner, vectors[1], vectors[2], vectors[3], vectors[4], vectors[5],
    )


def solution(mesh):
    rows, vector = P(AXES, None), P(AXES)
    token = P("page", "pb", None)
    in_specs = (token, token, P(None, "page", "pb"), P(None, "page"), P("page", "pb"))
    in_specs = in_specs + (rows,) * 8 + (vector,) * 10
    out_specs = (token, token) + (rows,) * 8 + (vector,) * 10
    sizes = (mesh.shape["page"], mesh.shape["pb"])
    return jax.shard_map(
        functools.partial(on_device, sizes), mesh=mesh, in_specs=in_specs, out_specs=out_specs,
        check_vma=False)
```

```python
import functools
import math

import jax
import jax.numpy as jnp
from jax import lax
from jax.experimental import pallas as pl
from jax.experimental.pallas import tpu as pltpu
from jax.sharding import PartitionSpec as P

HEADS = 12
HD = 64
FREQ = 192
D = HEADS * HD
SPAN = 2 * FREQ
SCALING = (3.0 * HD) ** (-0.5)
LOW = jnp.bfloat16
WIDE = jnp.float32
AXES = ("page", "pb")
VMEM_BYTES = 56 * 1024 * 1024


def dot(a, b):
    return jnp.dot(a, b, preferred_element_type=WIDE)


def dot_nt(a, b):
    return lax.dot_general(a, b, (((1,), (1,)), ((), ())), preferred_element_type=WIDE)


def dot_tn(a, b):
    return lax.dot_general(a, b, (((0,), (0,)), ((), ())), preferred_element_type=WIDE)


def whole(shape):
    return pl.BlockSpec(shape, lambda i, *_: (0,) * len(shape))


def cost(flops, bytes_accessed):
    return pl.CostEstimate(flops=int(flops), bytes_accessed=int(bytes_accessed), transcendentals=0)


def lanes_to(rows, length, start):
    lane = lax.broadcasted_iota(jnp.int32, rows.shape, 1)
    rows = jnp.where(lane < length, rows, 0.0)
    padded = jnp.concatenate([rows, jnp.zeros((rows.shape[0], D - rows.shape[1]), WIDE)], axis=1)
    return pltpu.roll(padded, start, 1)


def halves(place):
    cut = [place[:, i * FREQ:(i + 1) * FREQ] for i in (0, 2, 1, 3)]
    return jnp.concatenate(cut, axis=1)


def pack_kernel(size, at_ref, vec_ref, wq_ref, wk_ref, wv_ref, pq_ref, pk_ref, wo_ref, wi_ref, wu_ref,
                late_ref, cols_ref, mixed_ref):
    number, place_at = at_ref[3], at_ref[4]
    own, ff_own = wq_ref.shape[0], wu_ref.shape[0]
    cuts = wi_ref.shape[1] // D
    width = D // size
    vectors = vec_ref[...]
    lanes = lanes_to(vectors[:8], own, number * own)
    row = lax.broadcasted_iota(jnp.int32, lanes.shape, 0)
    first = jnp.where(row < 6, lanes, 0.0)
    inner = lanes_to(vectors[8:16], ff_own, lax.rem(number, D // ff_own) * ff_own)
    spot = lax.div(number, D // ff_own)
    for j in range(cuts):
        hit = (row == (6 + j) % 8) & (spot == j)
        if 6 + j < 8:
            first = first + jnp.where(hit, pltpu.roll(inner, 6 + j, 0), 0.0)
    second = jnp.zeros_like(first)
    for j in range(2, cuts):
        hit = (row == j - 2) & (spot == j)
        second = second + jnp.where(hit, pltpu.roll(inner, j - 2, 0), 0.0)
    wi = wi_ref[...].astype(WIDE)
    late = [wu_ref[...].astype(WIDE)] + [wi[:, j * D:(j + 1) * D] for j in range(cuts)]
    late += [first, second, wo_ref[...].astype(WIDE)]
    late_ref[...] = jnp.concatenate(late, axis=0).astype(LOW)
    cols = jnp.concatenate([ref[...].astype(WIDE) for ref in (wq_ref, wk_ref, wv_ref)], axis=0)
    for b in range(size):
        cols_ref[b] = cols[:, b * width:(b + 1) * width].astype(LOW)
    lanes = lanes_to(vectors[16:24], own, place_at * own)
    bias = jnp.concatenate(
        [lanes[i:i + 1, :width] for i in range(3)] + [jnp.zeros((1, D - 3 * width), WIDE)], axis=1)
    bias = jnp.concatenate([bias, jnp.zeros((7, D), WIDE)], axis=0)
    places = [halves(pq_ref[...].astype(WIDE)), halves(pk_ref[...].astype(WIDE)), bias]
    mixed_ref[...] = jnp.concatenate(places, axis=0).astype(LOW)


def pack_call(at, vectors, *weights):
    own, ff_own = weights[0].shape[0], weights[-1].shape[0]
    size = 4
    rows = ff_own + weights[-2].shape[1] // D * own + 16 + own
    return pl.pallas_call(
        functools.partial(pack_kernel, size),
        out_shape=[
            jax.ShapeDtypeStruct((rows, D), LOW),
            jax.ShapeDtypeStruct((size, 3 * own, D // size), LOW),
            jax.ShapeDtypeStruct((2 * own + 8, D), LOW),
        ],
        in_specs=[pl.BlockSpec(memory_space=pltpu.SMEM)]
        + [pl.BlockSpec(memory_space=pltpu.VMEM)] * (1 + len(weights)),
        compiler_params=pltpu.CompilerParams(vmem_limit_bytes=VMEM_BYTES),
        name="pack",
    )(at, vectors, *weights)


def finish_kernel(at_ref, cols_ref, mixed_ref, *out_refs):
    grad_refs, line_refs = out_refs[:5], out_refs[5:]
    number, place_at = at_ref[3], at_ref[4]
    own = grad_refs[0].shape[0]
    size, _, width = cols_ref.shape
    cols = [cols_ref[lax.rem(number, size) ^ b].astype(WIDE) for b in range(size)]
    for i in range(3):
        grad_refs[i][...] = jnp.concatenate([c[i * own:(i + 1) * own] for c in cols], axis=1)
    mixed = mixed_ref[...].astype(WIDE)
    for i in range(2):
        grad_refs[3 + i][...] = halves(mixed[i * own:(i + 1) * own])
    total = sum(c[3 * own:] for c in cols)
    quarters = [total[16 * i:16 * (i + 1)] for i in range(size)]
    rows = sum(jnp.where(lax.div(number, 8) == i, part, 0.0) for i, part in enumerate(quarters))
    rows = pltpu.roll(rows, lax.rem(width - lax.rem(number, 8) * own, width), 1)
    inner = sum(jnp.where(lax.div(lax.rem(number, 8), 2) == i, part, 0.0) for i, part in enumerate(quarters))
    inner = sum(jnp.where(lax.div(number, 8) == j, inner[6 + j:7 + j], 0.0) for j in range(4))
    inner = pltpu.roll(jnp.broadcast_to(inner, (8, width)), lax.rem(number, 2) * (width // 2), 1)
    bias = mixed[2 * own + 8:2 * own + 16]
    bias = jnp.concatenate([bias[2:3, i * width:(i + 1) * width] for i in range(3)] + [bias[:5, :width]], axis=0)
    bias = pltpu.roll(bias, lax.rem(width - place_at * own, width), 1)
    for i, ref in enumerate(line_refs):
        source, row = (rows, i) if i < 6 else (inner, 0) if i == 6 else (bias, i - 7)
        ref[...] = source[row:row + 1, :ref.shape[1]]


def finish_call(at, cols, mixed, ff_own):
    own = (mixed.shape[0] - 16) // 2
    return pl.pallas_call(
        finish_kernel,
        out_shape=[jax.ShapeDtypeStruct((own, D), WIDE)] * 5
        + [jax.ShapeDtypeStruct((1, ff_own if i == 6 else own), WIDE) for i in range(10)],
        in_specs=[pl.BlockSpec(memory_space=pltpu.SMEM)] + [pl.BlockSpec(memory_space=pltpu.VMEM)] * 2,
        compiler_params=pltpu.CompilerParams(vmem_limit_bytes=20 * 1024 * 1024),
        name="finish",
    )(at, cols, mixed)


def assemble_kernel(own, size, at_ref, mine_ref, theirs_ref, w_ref, pq_ref, pk_ref, bias_ref, got):
    pages = got.shape[0]
    inner = pages // size
    width = D // size
    even = (at_ref[1] >> 1) == 0
    for z in range(pages // 2):
        mine, theirs = mine_ref[at_ref[2] ^ z].astype(WIDE), theirs_ref[at_ref[2] ^ z].astype(WIDE)
        got[2 * z] = jnp.where(even, mine, theirs)
        got[2 * z + 1] = jnp.where(even, theirs, mine)
    columns = []
    for part in range(3):
        rows = got[:, pl.ds(part * own, own)]
        cut = [rows[:, :, b * width:(b + 1) * width][:, None] for b in range(size)]
        columns.append(jnp.concatenate(cut, axis=1).reshape(D, width))
    w_ref[...] = jnp.concatenate(columns, axis=1).astype(LOW)
    for start, ref in ((3 * own, pq_ref), (4 * own, pk_ref)):
        order = [b * inner + lo for lo in range(inner) for b in range(size)]
        rows = jnp.concatenate([got[p, pl.ds(start, own)] for p in order], axis=0)
        ref[...] = rows.astype(LOW).reshape(ref.shape)
    bias_ref[...] = jnp.sum(got[:, pl.ds(5 * own, 8)], axis=0)[:1, :3 * width]


def assemble_call(at, mine, theirs, own, size):
    width = D // size
    place = (width // HD, HD, 2 * SPAN)
    return pl.pallas_call(
        functools.partial(assemble_kernel, own, size),
        out_shape=[
            jax.ShapeDtypeStruct((D, 3 * width), LOW),
            jax.ShapeDtypeStruct(place, LOW),
            jax.ShapeDtypeStruct(place, LOW),
            jax.ShapeDtypeStruct((1, 3 * width), WIDE),
        ],
        in_specs=[pl.BlockSpec(memory_space=pltpu.SMEM)] + [pl.BlockSpec(memory_space=pltpu.VMEM)] * 2,
        scratch_shapes=[pltpu.VMEM((2 * mine.shape[0],) + mine.shape[1:], WIDE)],
        compiler_params=pltpu.CompilerParams(vmem_limit_bytes=VMEM_BYTES),
        name="assemble",
    )(at, mine, theirs)


def fold(rows):
    half = rows.shape[0] // 2
    return jnp.concatenate([rows[:half], rows[half:]], axis=1)


def unfold(rows):
    half = rows.shape[1] // 2
    return jnp.concatenate([rows[:, :half], rows[:, half:]], axis=0)


def turn(spread, left, right):
    s, c = spread[:, :SPAN], spread[:, SPAN:]
    return jnp.concatenate(
        [(s * left + c * right).astype(LOW), (c * left - s * right).astype(LOW)], axis=1)


def turn_back(gradient, left, right):
    s, c = gradient[:, :SPAN], gradient[:, SPAN:]
    return jnp.concatenate(
        [(s * left - c * right).astype(LOW), (s * right + c * left).astype(LOW)], axis=1)


def feature_pair(sines, cosines):
    sines, cosines = sines.astype(LOW), cosines.astype(LOW)
    return (jnp.concatenate([sines, cosines], axis=1), jnp.concatenate([cosines, sines], axis=1))


def attend_kernel(heads, blocks, me_ref, *refs):
    tok_refs = refs[:blocks]
    (w_ref, bias_ref, pq_ref, pk_ref, sin_ref, cos_ref, alive_ref,
     qkv_ref, soft_ref, share_ref, ctx_ref) = refs[blocks:]
    rows = tok_refs[0].shape[1]
    width = heads * HD
    tok = jnp.concatenate([ref[0] for ref in tok_refs], axis=0)
    sines, cosines = sin_ref[0], cos_ref[0]
    key_feats, query_feats = feature_pair(sines, cosines)
    count = tok.shape[0]
    mask = jnp.broadcast_to(jnp.where(alive_ref[0] > 0, 0.0, -1e30), (128, count)).T[:, :HD]
    lane = lax.broadcasted_iota(jnp.int32, (count, HD), 1)
    mask = jnp.where(lane == 0, mask, 0.0).astype(LOW)
    ones = jnp.where(lane == 0, 1.0, 0.0).astype(LOW)
    qkv = (dot(tok, w_ref[...]) + bias_ref[...]).astype(LOW)
    qkv_ref[0] = qkv
    pieces = []
    for h in range(heads):
        q = qkv[:, h * HD:(h + 1) * HD]
        k = qkv[:, width + h * HD:width + (h + 1) * HD]
        v = qkv[:, 2 * width + h * HD:2 * width + (h + 1) * HD]
        turned_q = turn(dot(q, pq_ref[h]), cosines, sines)
        turned_k = turn(dot(k, pk_ref[h]), sines, cosines)
        raw = dot_nt(jnp.concatenate([turned_q, query_feats, q, ones], axis=1),
                     jnp.concatenate([key_feats, turned_k, k, mask], axis=1))
        lifted = jnp.exp2((raw - jnp.max(raw, axis=1, keepdims=True)) * (SCALING * math.log2(math.e)))
        share = 1.0 / jnp.sum(lifted, axis=1, keepdims=True)
        share_ref[0, :, h:h + 1] = share
        lifted = lifted.astype(LOW)
        soft_ref[0, h] = lifted
        pieces.append((dot(lifted, v) * share).astype(LOW))
    ctx = jnp.concatenate(pieces, axis=1)
    for j in range(blocks):
        ctx_ref[j, 0] = fold(ctx[j * rows:(j + 1) * rows])


def attend_call(me, toks, w_qkv, bias, place_q, place_k, sines, cosines, alive):
    blocks = len(toks)
    pages, rows, _ = toks[0].shape
    heads = place_q.shape[0]
    width = heads * HD
    count = blocks * rows
    by_page = lambda *shape: pl.BlockSpec((1,) + shape, lambda p, *_: (p,) + (0,) * len(shape))
    return pl.pallas_call(
        functools.partial(attend_kernel, heads, blocks),
        grid_spec=pltpu.PrefetchScalarGridSpec(
            num_scalar_prefetch=1,
            grid=(pages,),
            in_specs=[by_page(rows, D)] * blocks + [
                whole((D, 3 * width)), whole((1, 3 * width)),
                whole((heads, HD, 2 * SPAN)), whole((heads, HD, 2 * SPAN)),
                by_page(count, SPAN), by_page(count, SPAN), by_page(1, count)],
            out_specs=[
                by_page(count, 3 * width), by_page(heads, count, count), by_page(count, heads),
                pl.BlockSpec((blocks, 1, rows // 2, 2 * width), lambda p, *_: (0, p, 0, 0))],
        ),
        out_shape=[
            jax.ShapeDtypeStruct((pages, count, 3 * width), LOW),
            jax.ShapeDtypeStruct((pages, heads, count, count), LOW),
            jax.ShapeDtypeStruct((pages, count, heads), WIDE),
            jax.ShapeDtypeStruct((blocks, pages, rows // 2, 2 * width), LOW),
        ],
        compiler_params=pltpu.CompilerParams(vmem_limit_bytes=VMEM_BYTES),
        cost_estimate=cost(20e9, 20e6),
        name="attend",
    )(me, *toks, w_qkv, bias, place_q, place_k, sines, cosines, alive)


def joined_grads(own, size, pages, small, d_w, d_pq, d_pk, d_bias):
    inner = pages // size
    width = D // size
    cut = d_w.reshape(pages, size, own, 3 * width)
    parts = []
    for part in range(3):
        parts.append(jnp.concatenate(
            [cut[:, b, :, part * width:(part + 1) * width] for b in range(size)], axis=2))
    for place in (d_pq, d_pk):
        place = place.reshape(D // size, 2 * SPAN)
        order = [(lo * size + b) * own for b in range(size) for lo in range(inner)]
        parts.append(jnp.concatenate([place[at:at + own][None] for at in order], axis=0))
    row = jnp.concatenate([d_bias, jnp.zeros((1, D - 3 * width), WIDE)], axis=1)
    at = lax.broadcasted_iota(jnp.int32, small.shape, 0)
    rows = jnp.where(at == 10, row, jnp.where(at < 10, small, 0.0))
    parts.append(jnp.broadcast_to(rows[None], (pages,) + rows.shape))
    return jnp.concatenate(parts, axis=1).astype(LOW)


def attend_back_kernel(heads, blocks, joined, me_ref, *refs):
    tok_refs = refs[:blocks]
    (w_ref, small_ref, qkv_ref, soft_ref, share_ref, ctx_ref, dctx_ref, pq_ref, pk_ref, sin_ref, cos_ref,
     kept_ref, sent_ref, *out_refs, dw_sum, dpq_sum, dpk_sum, db_sum) = refs[blocks:]
    step, last = pl.program_id(0), pl.num_programs(0) - 1
    rows = tok_refs[0].shape[1]
    width = heads * HD
    sines, cosines = sin_ref[0], cos_ref[0]
    key_feats, query_feats = feature_pair(sines, cosines)
    qkv = qkv_ref[0]
    dctx = jnp.concatenate([unfold(dctx_ref[me_ref[0] ^ j, 0]) for j in range(blocks)], axis=0)
    ctx = jnp.concatenate([unfold(ctx_ref[j, 0]) for j in range(blocks)], axis=0)
    along = dctx.astype(WIDE) * ctx.astype(WIDE)

    @pl.when(step == 0)
    def _():
        for ref in (dw_sum, dpq_sum, dpk_sum, db_sum):
            ref[...] = jnp.zeros_like(ref)

    d_q, d_k, d_v = [], [], []
    for h in range(heads):
        q = qkv[:, h * HD:(h + 1) * HD]
        k = qkv[:, width + h * HD:width + (h + 1) * HD]
        v = qkv[:, 2 * width + h * HD:2 * width + (h + 1) * HD]
        dc = dctx[:, h * HD:(h + 1) * HD]
        share = share_ref[0, :, h:h + 1]
        lifted = soft_ref[0, h]
        row_dot = jnp.sum(along[:, h * HD:(h + 1) * HD], axis=1, keepdims=True)
        raw_grad = ((dot_nt(dc, v) - row_dot) * (share * SCALING) * lifted.astype(WIDE)).astype(LOW)
        d_v.append(dot_tn(lifted, (dc.astype(WIDE) * share).astype(LOW)).astype(LOW))
        turned = dot(raw_grad, jnp.concatenate([key_feats, k], axis=1))
        spread_q = turn_back(turned[:, :2 * SPAN], cosines, sines)
        d_q.append((turned[:, 2 * SPAN:] + dot_nt(spread_q, pq_ref[h])).astype(LOW))
        dpq_sum[h] += dot_tn(q, spread_q)
        turned = dot_tn(raw_grad, jnp.concatenate([query_feats, q], axis=1))
        spread_k = turn_back(turned[:, :2 * SPAN], sines, cosines)
        d_k.append((turned[:, 2 * SPAN:] + dot_nt(spread_k, pk_ref[h])).astype(LOW))
        dpk_sum[h] += dot_tn(k, spread_k)
    dqkv = jnp.concatenate(d_q + d_k + d_v, axis=1)
    db_sum[...] += jnp.sum(dqkv.astype(WIDE), axis=0, keepdims=True)
    tok = jnp.concatenate([ref[0] for ref in tok_refs], axis=0)
    dw_sum[...] += dot_tn(tok, dqkv)
    part = dot_nt(dqkv, w_ref[...]).astype(LOW)
    for j in range(blocks):
        (sent_ref if j % 2 else kept_ref)[j // 2, 0] = part[j * rows:(j + 1) * rows]

    @pl.when(step == last)
    def _():
        if joined:
            rows = joined_grads(*joined, small_ref[...], dw_sum[...], dpq_sum[...], dpk_sum[...], db_sum[...])
            even = me_ref[1] == 0
            for z in range(rows.shape[0] // 2):
                first, second = rows[2 * z], rows[2 * z + 1]
                out_refs[0][me_ref[2] ^ z] = jnp.where(even, first, second)
                out_refs[1][me_ref[2] ^ z] = jnp.where(even, second, first)
        else:
            for ref, total in zip(out_refs, (dw_sum, dpq_sum, dpk_sum, db_sum)):
                ref[...] = total[...].astype(ref.dtype)


def attend_back_call(joined, me, toks, w_qkv, small, qkv, soft, share, ctx, dctx, place_q, place_k, sines, cosines):
    blocks, pages, rows, width = dctx.shape
    rows, width = 2 * rows, width // 2
    heads = place_q.shape[0]
    count = blocks * rows
    by_page = lambda *shape: pl.BlockSpec((1,) + shape, lambda p, *_: (p,) + (0,) * len(shape))
    place = (heads, HD, 2 * SPAN)
    if joined:
        own, _, owners = joined
        sums = [jax.ShapeDtypeStruct((owners // 2, 5 * own + 16, D), LOW)] * 2
    else:
        sums = [jax.ShapeDtypeStruct((D, 3 * width), LOW), jax.ShapeDtypeStruct(place, LOW),
                jax.ShapeDtypeStruct(place, LOW), jax.ShapeDtypeStruct((1, 3 * width), WIDE)]
    return pl.pallas_call(
        functools.partial(attend_back_kernel, heads, blocks, joined),
        grid_spec=pltpu.PrefetchScalarGridSpec(
            num_scalar_prefetch=1,
            grid=(pages,),
            in_specs=[by_page(rows, D)] * blocks + [
                whole((D, 3 * width)), whole(small.shape),
                by_page(count, 3 * width), by_page(heads, count, count), by_page(count, heads),
                pl.BlockSpec((blocks, 1, rows // 2, 2 * width), lambda p, *_: (0, p, 0, 0)),
                pl.BlockSpec((blocks, 1, rows // 2, 2 * width), lambda p, *_: (0, p, 0, 0)),
                whole(place), whole(place), by_page(count, SPAN), by_page(count, SPAN)],
            out_specs=[
                *[pl.BlockSpec((blocks // 2, 1, rows, D), lambda p, *_: (0, p, 0, 0))] * 2,
                *(whole(item.shape) for item in sums)],
            scratch_shapes=[
                pltpu.VMEM((D, 3 * width), WIDE), pltpu.VMEM(place, WIDE), pltpu.VMEM(place, WIDE),
                pltpu.VMEM((1, 3 * width), WIDE)],
        ),
        out_shape=[*[jax.ShapeDtypeStruct((blocks // 2, pages, rows, D), LOW)] * 2, *sums],
        compiler_params=pltpu.CompilerParams(vmem_limit_bytes=VMEM_BYTES),
        cost_estimate=cost(30e9, 20e6),
        name="attend_back",
    )(me, *toks, w_qkv, small, qkv, soft, share, ctx, dctx, place_q, place_k, sines, cosines)


def normed(values):
    centred = values - jnp.mean(values, axis=1, keepdims=True)
    scale = lax.rsqrt(jnp.mean(centred * centred, axis=1, keepdims=True) + 1e-05)
    return centred * scale, scale


def normed_back(gradient, unit, scale):
    mean = jnp.mean(gradient, axis=1, keepdims=True)
    along = jnp.mean(gradient * unit, axis=1, keepdims=True)
    return scale * (gradient - mean - unit * along)


def summed(values):
    return jnp.sum(values, axis=0, keepdims=True)


def second_half_kernel(cuts, split, at_ref, ctx_ref, tok_ref, cot_ref, wo_ref, vec_ref, wi_ref, *refs):
    n_grads = 4 if split else 2
    wu_ref, out_ref, pre_grad_ref, dctx_ref = refs[:4]
    grad_refs = refs[4:4 + n_grads]
    (small_ref, ctx_all, first, first_low, unit_one, scale_one, act, slope, outer, pre_two_grad,
     outer_grad, first_grad) = refs[4 + n_grads:]
    step = pl.program_id(0)
    core, x_at, y_at = at_ref[0], at_ref[1] >> 1, at_ref[1] & 1
    here = lax.rem(at_ref[3], ctx_ref.shape[0])
    blocks, pages, rows, width = ctx_ref.shape
    rows, width = 2 * rows, width // 2
    count = tok_ref.shape[0]
    b_out, b_outer, gain_one, shift_one, gain_two, shift_two = (vec_ref[i:i + 1] for i in range(6))

    w_outer = wu_ref[...].reshape(D, D)

    @pl.when(step == 0)
    def _():
        small_ref[...] = jnp.zeros_like(small_ref)
        ctx = jnp.concatenate(
            [jnp.concatenate([unfold(ctx_ref[here ^ b, p]) for b in range(blocks)], axis=1)
             for p in range(pages)], axis=0)
        ctx_all[...] = ctx
        pre = tok_ref[...].astype(WIDE) + (dot(ctx, wo_ref[...]) + b_out)
        unit, scale = normed(pre)
        unit_one[...] = unit
        scale_one[...] = jnp.broadcast_to(scale, scale_one.shape)
        value = unit * gain_one + shift_one
        first[...] = value
        first_low[...] = value.astype(LOW)

    @pl.when(step < cuts)
    def _():
        inner = dot(first_low[...], wi_ref[0]) + vec_ref[pl.ds(6 + step, 1)]
        half = 0.5 + 0.5 * lax.erf(inner * (0.5 ** 0.5))
        slope[step] = half + inner * (jnp.exp(inner * inner * -0.5) * ((0.5 / math.pi) ** 0.5))
        activated = (inner * half).astype(LOW)
        act[step] = activated
        product = dot(activated, w_outer)

        @pl.when(step == 0)
        def _():
            outer[...] = product

        @pl.when(step > 0)
        def _():
            outer[...] += product

    @pl.when(step == cuts - 1)
    def _():
        unit, scale = normed(first[...] + (outer[...] + b_outer))
        out_ref[...] = (unit * gain_two + shift_two).astype(LOW)
        cot = cot_ref[...].astype(WIDE)
        grad = normed_back(cot * gain_two, unit, scale)
        pre_two_grad[...] = grad
        low = grad.astype(LOW)
        outer_grad[...] = low
        small_ref[1:2] = summed(low.astype(WIDE))
        small_ref[4:5] = summed(cot * unit)
        small_ref[5:6] = summed(cot)

    def store_24(grad):
        cut = grad.reshape(4, 2, 2, 2, D // 32, D)
        for z in range(4):
            for x in range(2):
                for y in range(2):
                    slot = (0, x_at ^ x, y_at ^ y, z)
                    first, second = cut[z, x, y, 0], cut[z, x, y, 1]
                    grad_refs[2][slot] = jnp.where(core == 0, first, second).astype(LOW)
                    grad_refs[3][slot] = jnp.where(core == 0, second, first).astype(LOW)

    @pl.when((step >= cuts) & (step < 2 * cuts))
    def _():
        j = 2 * cuts - 1 - step
        low = outer_grad[...]
        d_outer = dot_tn(act[j], low).astype(LOW)
        inner_grad = (dot_nt(low, w_outer) * slope[j]).astype(LOW)
        small_ref[pl.ds(6 + j, 1)] = summed(inner_grad.astype(WIDE))
        d_inner = dot_tn(first_low[...], inner_grad)
        if split:
            cut = d_outer.reshape(2, 2, 2, D // 8, D)
            for x in range(2):
                for y in range(2):
                    slot = (0, x_at ^ x, y_at ^ y)
                    first, second = cut[x, y, 0], cut[x, y, 1]
                    grad_refs[0][slot] = jnp.where(core == 0, first, second)
                    grad_refs[1][slot] = jnp.where(core == 0, second, first)
            store_24(d_inner)
        else:
            grad_refs[0][...] = d_outer
            grad_refs[1][0] = d_inner.astype(LOW)
        product = dot_nt(inner_grad, wi_ref[0])

        @pl.when(step == cuts)
        def _():
            first_grad[...] = pre_two_grad[...] + product

        @pl.when(step > cuts)
        def _():
            first_grad[...] += product

    @pl.when(step == 2 * cuts)
    def _():
        grad = first_grad[...]
        unit = unit_one[...]
        small_ref[2:3] = summed(grad * unit)
        small_ref[3:4] = summed(grad)
        grad = normed_back(grad * gain_one, unit, scale_one[:, :1])
        pre_grad_ref[...] = grad
        low = grad.astype(LOW)
        small_ref[0:1] = summed(low.astype(WIDE))
        dctx = dot_nt(low, wo_ref[...]).astype(LOW)
        for b in range(blocks):
            for p in range(pages):
                dctx_ref[b, p] = fold(dctx[p * rows:(p + 1) * rows, b * width:(b + 1) * width])
        d_output = dot_tn(ctx_all[...], low)
        if split:
            store_24(d_output)
        else:
            grad_refs[1][0] = d_output.astype(LOW)


def second_half_call(split, at, ctx, tok, cot, w_output, vectors, w_inner, w_outer):
    blocks, pages, rows, width = ctx.shape
    count = 2 * pages * rows
    cuts = w_inner.shape[0]
    now = lambda i: jnp.where(i < cuts, i, jnp.maximum(2 * cuts - 1 - i, 0))
    late = lambda i: jnp.where(i < cuts, cuts - 1, jnp.maximum(2 * cuts - 1 - i, 0))
    last = lambda i: jnp.where(i < 2 * cuts, late(i), cuts)
    square, tall = (D, D), (count, D)
    eighth = (1, 2, 2, D // 8, D)
    slots = (1, 2, 2, 4, D // 32, D)
    if split:
        grad_specs = [pl.BlockSpec(eighth, lambda i, at: (late(i) ^ at[2], 0, 0, 0, 0))] * 2
        grad_specs += [pl.BlockSpec(slots, lambda i, at: (last(i), 0, 0, 0, 0, 0))] * 2
        grads = [(cuts, 2, 2, D // 8, D)] * 2 + [(cuts + 1,) + slots[1:]] * 2
    else:
        grad_specs = [
            pl.BlockSpec(square, lambda i, at: (late(i), 0)),
            pl.BlockSpec((1,) + square, lambda i, at: (last(i), 0, 0))]
        grads = [(cuts * D, D), (cuts + 1,) + square]
    return pl.pallas_call(
        functools.partial(second_half_kernel, cuts, split),
        grid_spec=pltpu.PrefetchScalarGridSpec(
            num_scalar_prefetch=1,
            grid=(2 * cuts + 1,),
            in_specs=[
                whole(ctx.shape), whole(tall), whole(tall), whole(square), whole(vectors.shape),
                pl.BlockSpec((1,) + square, lambda i, at: (now(i), 0, 0)),
                pl.BlockSpec((8, D // 8, D), lambda i, at: (now(i), 0, 0))],
            out_specs=[whole(tall), whole(tall), whole(ctx.shape), *grad_specs, whole(vectors.shape)],
            scratch_shapes=[
                pltpu.VMEM(tall, LOW), pltpu.VMEM(tall, WIDE), pltpu.VMEM(tall, LOW),
                pltpu.VMEM(tall, WIDE), pltpu.VMEM((count, 128), WIDE), pltpu.VMEM((cuts,) + tall, LOW),
                pltpu.VMEM((cuts,) + tall, WIDE), pltpu.VMEM(tall, WIDE), pltpu.VMEM(tall, WIDE),
                pltpu.VMEM(tall, LOW), pltpu.VMEM(tall, WIDE)],
        ),
        out_shape=[
            jax.ShapeDtypeStruct(tall, LOW),
            jax.ShapeDtypeStruct(tall, WIDE),
            jax.ShapeDtypeStruct(ctx.shape, LOW),
            *(jax.ShapeDtypeStruct(shape, LOW) for shape in grads),
            jax.ShapeDtypeStruct(vectors.shape, WIDE),
        ],
        compiler_params=pltpu.CompilerParams(vmem_limit_bytes=44 * 1024 * 1024),
        cost_estimate=cost(20e9, 30e6),
        name="second_half",
    )(at, ctx, tok, cot, w_output, vectors, w_inner, w_outer)


def swap(value, axis, size, bit):
    return lax.ppermute(value, axis, [(i, i ^ bit) for i in range(size)])


def exchange_slots(value):
    return jnp.stack([value[0]] + [swap(value[j], "pb", 4, j) for j in (1, 2, 3)])


def gather_slots(value):
    near = swap(value, "pb", 4, 1)
    far = swap(value, "pb", 4, 2)
    return (value, near, far, swap(far, "pb", 4, 1))


def hop(value, devices, bits):
    return lax.ppermute(value, AXES, [(i, i ^ bits) for i in range(devices)])


def added(*terms):
    return sum(term.astype(WIDE) for term in terms)


def sum_along_z(value, devices):
    return added(value[0], *(hop(value[j], devices, j << 3) for j in (1, 2, 3)))


def exchange_along_z(value, devices):
    lines = [[i + 8 * z for z in range(4)] for i in range(8)]
    return lax.all_to_all(value, AXES, 0, 0, tiled=True, axis_index_groups=lines)


def tie(*values):
    return lax.optimization_barrier(values)


def transpose_roles(value, pages, size):
    inner = pages // size
    pairs = []
    for hi in range(size):
        for lo in range(inner):
            for b in range(size):
                pairs.append(((hi * inner + lo) * size + b, (b * inner + lo) * size + hi))
    return lax.ppermute(value, AXES, pairs)


def sum_slots(kept, sent):
    total = added(kept, swap(sent, "pb", 4, 1))
    return total[0] + swap(total[1].astype(LOW), "pb", 4, 2).astype(WIDE)


def to_halves(place):
    cut = place.reshape(place.shape[:-1] + (2, 2, FREQ))
    return jnp.swapaxes(cut, -3, -2).reshape(place.shape)


def on_device(sizes, tokens, cotangent, boxes, resolution, padding,
              query_weight, keys_weight, values_weight, output_weight, query_place, keys_place,
              inner_weight, outer_weight, query_bias, keys_bias, values_bias, output_bias,
              inner_bias, outer_bias, first_gain, first_shift, second_gain, second_shift):
    page_size, pb_size = sizes
    devices = page_size * pb_size
    inner_pages = page_size // pb_size
    pages, rows, _ = tokens.shape
    count = rows * pb_size
    heads = HEADS // pb_size
    width = heads * HD
    own = query_weight.shape[0]
    ff_own = outer_weight.shape[0]
    ff = ff_own * devices
    cuts = ff // D
    me, page = lax.axis_index("pb"), lax.axis_index("page")
    place_at = (page % inner_pages) * pb_size + me
    number = page * pb_size + me
    me_array = me.astype(jnp.int32).reshape(1)
    by_link = (page_size, pb_size, own) == (8, 4, 24)

    at = jnp.stack([number & 1, (number >> 1) & 3, number >> 3, number, place_at]).astype(jnp.int32)
    small_rows = 16
    vectors = [output_bias, outer_bias, first_gain, first_shift, second_gain, second_shift]
    if by_link:
        lines = list(enumerate(vectors)) + [(8, inner_bias), (16, query_bias), (17, keys_bias), (18, values_bias)]
        lines = added(*(jnp.pad(line.astype(WIDE), (128 * i, 128 * (24 - i) - line.shape[0]))
                        for i, line in lines)).reshape(24, 128)
        packed, cols, mixed = pack_call(
            at, lines, query_weight, keys_weight, values_weight, query_place, keys_place,
            output_weight, inner_weight, outer_weight)
    else:
        cols = jnp.concatenate([query_weight, keys_weight, values_weight], axis=0)
        cols = cols.reshape(3 * own, pb_size, width).swapaxes(0, 1)
        bias_rows = jnp.zeros((3, width), LOW)
        bias_rows = lax.dynamic_update_slice(
            bias_rows, jnp.stack([query_bias, keys_bias, values_bias]), (0, place_at * own))
        bias_rows = jnp.pad(bias_rows.reshape(1, 3 * width), ((0, 7), (0, D - 3 * width)))
        mixed = jnp.concatenate([to_halves(query_place), to_halves(keys_place), bias_rows], axis=0)
        vectors = lax.dynamic_update_slice(jnp.zeros((6, D), LOW), jnp.stack(vectors), (0, number * own))
        b_inner = lax.dynamic_update_slice(jnp.zeros((ff,), LOW), inner_bias, (number * ff_own,))
        vectors = jnp.concatenate(
            [vectors, b_inner.reshape(cuts, D), jnp.zeros((small_rows - 6 - cuts, D), LOW)], axis=0)
        packed = jnp.concatenate(
            [outer_weight] + [inner_weight[:, j * D:(j + 1) * D] for j in range(cuts)]
            + [vectors, output_weight], axis=0)
    cols = lax.all_to_all(cols, "pb", 0, 0, tiled=True)
    cols = cols.swapaxes(0, 1).reshape(3 * own, D)
    mixed = transpose_roles(mixed, page_size, pb_size)
    mixed = jnp.concatenate([cols, mixed], axis=0)
    late = lax.all_gather(packed, AXES, axis=0)

    grid_x = (boxes[0] + boxes[2]) * 500 // resolution[0][:, None]
    grid_y = (boxes[1] + boxes[3]) * 500 // resolution[1][:, None]
    places = lax.all_gather(jnp.stack([grid_x, grid_y, padding]), "pb", axis=0)
    toks = gather_slots(tokens)

    places = jnp.stack([places[me ^ j] for j in range(pb_size)])
    places = places.transpose(1, 2, 0, 3).reshape(3, pages, count)
    rates = jnp.exp(jnp.arange(FREQ).astype(WIDE) * (-math.log(10000.0) / FREQ))
    grids = places[:2].astype(WIDE)
    angles = jnp.concatenate(
        [grids[0][..., None] * rates, grids[1][..., None] * rates], axis=-1)
    sines, cosines = jnp.sin(angles), jnp.cos(angles)
    alive = places[2][:, None, :]

    if by_link:
        mixed = jnp.stack([mixed] + [hop(mixed, devices, j << 3) for j in (1, 2, 3)])
        w_qkv, place_q, place_k, bias_qkv = assemble_call(
            at, mixed, hop(mixed, devices, 4), own, pb_size)
    else:
        mixed = lax.all_gather(mixed, "page", axis=0)
        w_qkv = mixed[:, :3 * own].reshape(page_size, 3, own, pb_size, width)
        w_qkv = w_qkv.transpose(0, 3, 2, 1, 4).reshape(D, 3 * width)
        bias_qkv = jnp.sum(mixed[:, 5 * own, :3 * width].astype(WIDE), axis=0, keepdims=True)
        mixed = mixed[:, 3 * own:5 * own].reshape(pb_size, inner_pages, 2, own, D)
        mixed = mixed.transpose(2, 1, 0, 3, 4).reshape(2, heads, HD, 2 * SPAN)
        place_q, place_k = mixed[0], mixed[1]

    qkv, soft, share, ctx_heads = attend_call(
        me_array, toks, w_qkv, bias_qkv, place_q, place_k, sines, cosines, alive)
    ctx = exchange_slots(ctx_heads)

    spot = ff_own
    w_inner = jnp.stack(
        [late[:, spot + j * own:spot + (j + 1) * own].reshape(D, D) for j in range(cuts)])
    spot += cuts * own
    vectors = jnp.sum(late[:, spot:spot + small_rows].astype(WIDE), axis=0)
    w_output = late[:, spot + small_rows:].reshape(D, D)
    w_outer = late if by_link else late[:, :ff_own].reshape(8 * cuts, D // 8, D)

    tok = tokens.reshape(pages * rows, D)
    output, pre_one_grad, dctx, *grads, small = second_half_call(
        by_link, at, ctx, tok, cotangent.reshape(pages * rows, D), w_output, vectors, w_inner, w_outer)
    dctx = lax.all_to_all(dctx, "pb", 0, 0, tiled=True)

    if by_link:
        outer_kept, outer_sent, inner_kept, inner_sent = grads
        outer_core, inner_core = hop(outer_sent, devices, 1), hop(inner_sent, devices, 1)
        outer_sum = added(outer_kept, outer_core).astype(LOW)
        inner_far = added(inner_kept[:, 1], inner_core[:, 1]).astype(LOW)
        outer_got = [outer_sum[0]] + [hop(outer_sum[j], devices, j << 3) for j in (1, 2, 3)]
        dctx, outer_got[0], far = tie(dctx, outer_got[0], inner_far)
        inner_far = hop(inner_far, devices, 4)

    joined = (own, pb_size, page_size) if by_link else None
    me_array = jnp.stack([me, at[1] >> 1, at[2]]).astype(jnp.int32)
    kept, sent, *sums = attend_back_call(
        joined, me_array, toks, w_qkv, small, qkv, soft, share, ctx_heads, dctx, place_q, place_k, sines, cosines)

    if by_link:
        kept, sent, mixed, mixed_far, inner_far = tie(kept, sent, *sums, inner_far)
        mixed_far, sent = hop(mixed_far, devices, 4), hop(sent, devices, 1)
        inner_sent = added(inner_kept[:, 0, 1], inner_core[:, 0, 1], inner_far[:, 1]).astype(LOW)
        inner_sent = hop(inner_sent, devices, 2)
        inner_sum = added(inner_kept[:, 0, 0], inner_core[:, 0, 0], inner_far[:, 0])
        mixed, mixed_far, kept, sent, inner_sum, inner_sent, *outer_got = tie(
            mixed, mixed_far, kept, sent, inner_sum, inner_sent, *outer_got)
        mixed = added(mixed, mixed_far).astype(LOW)
        inner_sum = added(inner_sum, inner_sent).astype(LOW).swapaxes(0, 1).reshape(4, (cuts + 1) * own, D)
        inner_sum = exchange_along_z(inner_sum, devices)
        mixed_z = [hop(mixed[j], devices, j << 3) for j in (1, 2, 3)]
        outer_sent = hop(added(*(got[1] for got in outer_got)).astype(LOW), devices, 4)
        far = hop(added(kept[1], sent[1]).astype(LOW), devices, 2)
        outer_sum = added(*(got[0] for got in outer_got))
        mixed, kept, sent, far, outer_sum, outer_sent, *mixed_z = tie(
            mixed, kept, sent, far, outer_sum, outer_sent, *mixed_z)
        mixed = added(mixed[0], *mixed_z).astype(LOW)
        small = mixed[5 * own:].reshape(16, pb_size, width).swapaxes(0, 1).reshape(1, 16 * pb_size, width)
        cols = mixed[:3 * own].reshape(3 * own, pb_size, width).swapaxes(0, 1)
        cols = jnp.concatenate([cols, jnp.broadcast_to(small, (pb_size,) + small.shape[1:])], axis=1)
        cols = jnp.stack([cols[me]] + [swap(cols[me ^ j], "pb", pb_size, j) for j in (1, 2, 3)])
        mixed = transpose_roles(mixed[3 * own:5 * own + 16], page_size, pb_size)
        outer_sum = added(outer_sum, outer_sent)
        outer_sent = hop(outer_sum[1].astype(LOW), devices, 2)
        tokens_grad = pre_one_grad.reshape(pages, rows, D) + added(kept[0], sent[0], far)
        d_outer = added(outer_sum[0], outer_sent)
        d_query, d_keys, d_values, d_place_q, d_place_k, *lines = finish_call(at, cols, mixed, ff_own)
        lines = [line.reshape(-1) for line in lines]
        vectors, d_b_inner, d_bias = lines[:6], lines[6], lines[7:]
        tokens_grad, d_outer, inner_sum = tie(tokens_grad, d_outer, inner_sum)
        inner_sum = added(*(inner_sum[z] for z in range(4))).reshape(cuts + 1, own, D)
        d_inner = jnp.concatenate([inner_sum[j] for j in range(cuts)], axis=1)
        d_output = inner_sum[cuts]
    else:
        d_outer = lax.psum_scatter(
            grads[0].reshape(devices, ff_own, D), AXES, scatter_dimension=0, tiled=False).astype(WIDE)
        inner_sum = grads[1].reshape(cuts + 1, devices, own, D).swapaxes(0, 1)
        inner_sum = lax.psum_scatter(inner_sum, AXES, scatter_dimension=0, tiled=False).astype(WIDE)
        d_inner = jnp.concatenate([inner_sum[j] for j in range(cuts)], axis=1)
        d_output = inner_sum[cuts]
        d_w, d_pq, d_pk, d_bias = sums
        d_w = d_w.reshape(page_size, pb_size, own, 3, width).transpose(0, 3, 2, 1, 4)
        d_w = d_w.reshape(page_size, 3 * own, D)
        d_p = jnp.stack([d_pq, d_pk]).reshape(2, inner_pages, pb_size, own, D)
        d_p = d_p.transpose(2, 1, 0, 3, 4).reshape(page_size, 2 * own, D)
        d_bias = jnp.pad(d_bias, ((0, 7), (0, D - 3 * width))).astype(LOW)
        d_bias = jnp.broadcast_to(d_bias[None], (page_size, 8, D))
        mixed = jnp.concatenate([d_w, d_p, d_bias], axis=1)
        mixed = lax.all_to_all(mixed, "page", 0, 0, tiled=True)
        mixed = jnp.sum(mixed.astype(WIDE), axis=0).astype(LOW)
        tokens_grad = pre_one_grad.reshape(pages, rows, D) + sum_slots(kept, sent)
        cols = mixed[:3 * own].reshape(3 * own, pb_size, width).swapaxes(0, 1)
        cols = lax.all_to_all(cols, "pb", 0, 0, tiled=True)
        d_query, d_keys, d_values = cols.swapaxes(0, 1).reshape(3, own, D).astype(WIDE)
        mixed = transpose_roles(mixed[3 * own:], page_size, pb_size)
        d_place_q, d_place_k = to_halves(mixed[:own].astype(WIDE)), to_halves(mixed[own:2 * own].astype(WIDE))
        d_bias = lax.dynamic_slice(
            mixed[2 * own, :3 * width].astype(WIDE).reshape(3, width), (0, place_at * own), (3, own))
        small = jnp.sum(lax.all_gather(small, AXES, axis=0), axis=0)
        d_b_inner = lax.dynamic_slice(small[6:6 + cuts].reshape(ff), (number * ff_own,), (ff_own,))
        vectors = lax.dynamic_slice(small, (0, number * own), (6, own))

    return (
        output.reshape(pages, rows, D),
        tokens_grad,
        d_query, d_keys, d_values,
        d_output,
        d_place_q, d_place_k,
        d_inner,
        d_outer.reshape(ff_own, D),
        d_bias[0], d_bias[1], d_bias[2],
        vectors[0], d_b_inner, vectors[1], vectors[2], vectors[3], vectors[4], vectors[5],
    )


def solution(mesh):
    rows, vector = P(AXES, None), P(AXES)
    token = P("page", "pb", None)
    in_specs = (token, token, P(None, "page", "pb"), P(None, "page"), P("page", "pb"))
    in_specs = in_specs + (rows,) * 8 + (vector,) * 10
    out_specs = (token, token) + (rows,) * 8 + (vector,) * 10
    sizes = (mesh.shape["page"], mesh.shape["pb"])
    return jax.shard_map(
        functools.partial(on_device, sizes), mesh=mesh, in_specs=in_specs, out_specs=out_specs,
        check_vma=False)
```

```python
import functools
import math

import jax
import jax.numpy as jnp
from jax import lax
from jax.experimental import pallas as pl
from jax.experimental.pallas import tpu as pltpu
from jax.sharding import PartitionSpec as P

HEADS = 12
HD = 64
FREQ = 192
D = HEADS * HD
SPAN = 2 * FREQ
SCALING = (3.0 * HD) ** (-0.5)
LOW = jnp.bfloat16
WIDE = jnp.float32
AXES = ("page", "pb")
VMEM_BYTES = 56 * 1024 * 1024


def dot(a, b):
    return jnp.dot(a, b, preferred_element_type=WIDE)


def dot_nt(a, b):
    return lax.dot_general(a, b, (((1,), (1,)), ((), ())), preferred_element_type=WIDE)


def dot_tn(a, b):
    return lax.dot_general(a, b, (((0,), (0,)), ((), ())), preferred_element_type=WIDE)


def whole(shape):
    return pl.BlockSpec(shape, lambda i, *_: (0,) * len(shape))


def cost(flops, bytes_accessed):
    return pl.CostEstimate(flops=int(flops), bytes_accessed=int(bytes_accessed), transcendentals=0)


def lanes_to(rows, length, start):
    lane = lax.broadcasted_iota(jnp.int32, rows.shape, 1)
    rows = jnp.where(lane < length, rows, 0.0)
    padded = jnp.concatenate([rows, jnp.zeros((rows.shape[0], D - rows.shape[1]), WIDE)], axis=1)
    return pltpu.roll(padded, start, 1)


def halves(place):
    cut = [place[:, i * FREQ:(i + 1) * FREQ] for i in (0, 2, 1, 3)]
    return jnp.concatenate(cut, axis=1)


def pack_kernel(size, at_ref, vec_ref, wq_ref, wk_ref, wv_ref, pq_ref, pk_ref, wo_ref, wi_ref, wu_ref,
                late_ref, cols_ref, mixed_ref):
    number, place_at = at_ref[3], at_ref[4]
    own, ff_own = wq_ref.shape[0], wu_ref.shape[0]
    cuts = wi_ref.shape[1] // D
    width = D // size
    vectors = vec_ref[...]
    lanes = lanes_to(vectors[:8], own, number * own)
    row = lax.broadcasted_iota(jnp.int32, lanes.shape, 0)
    first = jnp.where(row < 6, lanes, 0.0)
    inner = lanes_to(vectors[8:16], ff_own, lax.rem(number, D // ff_own) * ff_own)
    spot = lax.div(number, D // ff_own)
    for j in range(cuts):
        hit = (row == (6 + j) % 8) & (spot == j)
        if 6 + j < 8:
            first = first + jnp.where(hit, pltpu.roll(inner, 6 + j, 0), 0.0)
    second = jnp.zeros_like(first)
    for j in range(2, cuts):
        hit = (row == j - 2) & (spot == j)
        second = second + jnp.where(hit, pltpu.roll(inner, j - 2, 0), 0.0)
    wi = wi_ref[...].astype(WIDE)
    late = [wu_ref[...].astype(WIDE)] + [wi[:, j * D:(j + 1) * D] for j in range(cuts)]
    late += [first, second, wo_ref[...].astype(WIDE)]
    late_ref[...] = jnp.concatenate(late, axis=0).astype(LOW)
    cols = jnp.concatenate([ref[...].astype(WIDE) for ref in (wq_ref, wk_ref, wv_ref)], axis=0)
    for b in range(size):
        cols_ref[b] = cols[:, b * width:(b + 1) * width].astype(LOW)
    lanes = lanes_to(vectors[16:24], own, place_at * own)
    bias = jnp.concatenate(
        [lanes[i:i + 1, :width] for i in range(3)] + [jnp.zeros((1, D - 3 * width), WIDE)], axis=1)
    bias = jnp.concatenate([bias, jnp.zeros((7, D), WIDE)], axis=0)
    places = [halves(pq_ref[...].astype(WIDE)), halves(pk_ref[...].astype(WIDE)), bias]
    mixed_ref[...] = jnp.concatenate(places, axis=0).astype(LOW)


def pack_call(at, vectors, *weights):
    own, ff_own = weights[0].shape[0], weights[-1].shape[0]
    size = 4
    rows = ff_own + weights[-2].shape[1] // D * own + 16 + own
    return pl.pallas_call(
        functools.partial(pack_kernel, size),
        out_shape=[
            jax.ShapeDtypeStruct((rows, D), LOW),
            jax.ShapeDtypeStruct((size, 3 * own, D // size), LOW),
            jax.ShapeDtypeStruct((2 * own + 8, D), LOW),
        ],
        in_specs=[pl.BlockSpec(memory_space=pltpu.SMEM)]
        + [pl.BlockSpec(memory_space=pltpu.VMEM)] * (1 + len(weights)),
        compiler_params=pltpu.CompilerParams(vmem_limit_bytes=VMEM_BYTES),
        name="pack",
    )(at, vectors, *weights)


def finish_kernel(at_ref, cols_ref, mixed_ref, *out_refs):
    grad_refs, line_refs = out_refs[:5], out_refs[5:]
    number, place_at = at_ref[3], at_ref[4]
    own = grad_refs[0].shape[0]
    size, _, width = cols_ref.shape
    cols = [cols_ref[lax.rem(number, size) ^ b].astype(WIDE) for b in range(size)]
    for i in range(3):
        grad_refs[i][...] = jnp.concatenate([c[i * own:(i + 1) * own] for c in cols], axis=1)
    mixed = mixed_ref[...].astype(WIDE)
    for i in range(2):
        grad_refs[3 + i][...] = halves(mixed[i * own:(i + 1) * own])
    total = sum(c[3 * own:] for c in cols)
    quarters = [total[16 * i:16 * (i + 1)] for i in range(size)]
    rows = sum(jnp.where(lax.div(number, 8) == i, part, 0.0) for i, part in enumerate(quarters))
    rows = pltpu.roll(rows, lax.rem(width - lax.rem(number, 8) * own, width), 1)
    inner = sum(jnp.where(lax.div(lax.rem(number, 8), 2) == i, part, 0.0) for i, part in enumerate(quarters))
    inner = sum(jnp.where(lax.div(number, 8) == j, inner[6 + j:7 + j], 0.0) for j in range(4))
    inner = pltpu.roll(jnp.broadcast_to(inner, (8, width)), lax.rem(number, 2) * (width // 2), 1)
    bias = mixed[2 * own + 8:2 * own + 16]
    bias = jnp.concatenate([bias[2:3, i * width:(i + 1) * width] for i in range(3)] + [bias[:5, :width]], axis=0)
    bias = pltpu.roll(bias, lax.rem(width - place_at * own, width), 1)
    for i, ref in enumerate(line_refs):
        source, row = (rows, i) if i < 6 else (inner, 0) if i == 6 else (bias, i - 7)
        ref[...] = source[row:row + 1, :ref.shape[1]]


def finish_call(at, cols, mixed, ff_own):
    own = (mixed.shape[0] - 16) // 2
    return pl.pallas_call(
        finish_kernel,
        out_shape=[jax.ShapeDtypeStruct((own, D), WIDE)] * 5
        + [jax.ShapeDtypeStruct((1, ff_own if i == 6 else own), WIDE) for i in range(10)],
        in_specs=[pl.BlockSpec(memory_space=pltpu.SMEM)] + [pl.BlockSpec(memory_space=pltpu.VMEM)] * 2,
        compiler_params=pltpu.CompilerParams(vmem_limit_bytes=20 * 1024 * 1024),
        name="finish",
    )(at, cols, mixed)


def assemble_kernel(own, size, at_ref, mine_ref, theirs_ref, w_ref, pq_ref, pk_ref, bias_ref, got):
    pages = got.shape[0]
    inner = pages // size
    width = D // size
    even = (at_ref[1] >> 1) == 0
    for z in range(pages // 2):
        mine, theirs = mine_ref[at_ref[2] ^ z].astype(WIDE), theirs_ref[at_ref[2] ^ z].astype(WIDE)
        got[2 * z] = jnp.where(even, mine, theirs)
        got[2 * z + 1] = jnp.where(even, theirs, mine)
    columns = []
    for part in range(3):
        rows = got[:, pl.ds(part * own, own)]
        cut = [rows[:, :, b * width:(b + 1) * width][:, None] for b in range(size)]
        columns.append(jnp.concatenate(cut, axis=1).reshape(D, width))
    w_ref[...] = jnp.concatenate(columns, axis=1).astype(LOW)
    for start, ref in ((3 * own, pq_ref), (4 * own, pk_ref)):
        order = [b * inner + lo for lo in range(inner) for b in range(size)]
        rows = jnp.concatenate([got[p, pl.ds(start, own)] for p in order], axis=0)
        ref[...] = rows.astype(LOW).reshape(ref.shape)
    bias_ref[...] = jnp.sum(got[:, pl.ds(5 * own, 8)], axis=0)[:1, :3 * width]


def assemble_call(at, mine, theirs, own, size):
    width = D // size
    place = (width // HD, HD, 2 * SPAN)
    return pl.pallas_call(
        functools.partial(assemble_kernel, own, size),
        out_shape=[
            jax.ShapeDtypeStruct((D, 3 * width), LOW),
            jax.ShapeDtypeStruct(place, LOW),
            jax.ShapeDtypeStruct(place, LOW),
            jax.ShapeDtypeStruct((1, 3 * width), WIDE),
        ],
        in_specs=[pl.BlockSpec(memory_space=pltpu.SMEM)] + [pl.BlockSpec(memory_space=pltpu.VMEM)] * 2,
        scratch_shapes=[pltpu.VMEM((2 * mine.shape[0],) + mine.shape[1:], WIDE)],
        compiler_params=pltpu.CompilerParams(vmem_limit_bytes=VMEM_BYTES),
        name="assemble",
    )(at, mine, theirs)


def fold(rows):
    half = rows.shape[0] // 2
    return jnp.concatenate([rows[:half], rows[half:]], axis=1)


def unfold(rows):
    half = rows.shape[1] // 2
    return jnp.concatenate([rows[:, :half], rows[:, half:]], axis=0)


def turn(spread, left, right):
    s, c = spread[:, :SPAN], spread[:, SPAN:]
    return jnp.concatenate(
        [(s * left + c * right).astype(LOW), (c * left - s * right).astype(LOW)], axis=1)


def turn_back(gradient, left, right):
    s, c = gradient[:, :SPAN], gradient[:, SPAN:]
    return jnp.concatenate(
        [(s * left - c * right).astype(LOW), (s * right + c * left).astype(LOW)], axis=1)


def feature_pair(sines, cosines):
    sines, cosines = sines.astype(LOW), cosines.astype(LOW)
    return (jnp.concatenate([sines, cosines], axis=1), jnp.concatenate([cosines, sines], axis=1))


def attend_kernel(heads, blocks, me_ref, *refs):
    tok_refs = refs[:blocks]
    (w_ref, bias_ref, pq_ref, pk_ref, sin_ref, cos_ref, alive_ref,
     qkv_ref, soft_ref, share_ref, ctx_ref) = refs[blocks:]
    rows = tok_refs[0].shape[1]
    width = heads * HD
    tok = jnp.concatenate([ref[0] for ref in tok_refs], axis=0)
    sines, cosines = sin_ref[0], cos_ref[0]
    key_feats, query_feats = feature_pair(sines, cosines)
    count = tok.shape[0]
    mask = jnp.broadcast_to(jnp.where(alive_ref[0] > 0, 0.0, -1e30), (128, count)).T[:, :HD]
    lane = lax.broadcasted_iota(jnp.int32, (count, HD), 1)
    mask = jnp.where(lane == 0, mask, 0.0).astype(LOW)
    ones = jnp.where(lane == 0, 1.0, 0.0).astype(LOW)
    qkv = (dot(tok, w_ref[...]) + bias_ref[...]).astype(LOW)
    qkv_ref[0] = qkv
    pieces = []
    for h in range(heads):
        q = qkv[:, h * HD:(h + 1) * HD]
        k = qkv[:, width + h * HD:width + (h + 1) * HD]
        v = qkv[:, 2 * width + h * HD:2 * width + (h + 1) * HD]
        turned_q = turn(dot(q, pq_ref[h]), cosines, sines)
        turned_k = turn(dot(k, pk_ref[h]), sines, cosines)
        raw = dot_nt(jnp.concatenate([turned_q, query_feats, q, ones], axis=1),
                     jnp.concatenate([key_feats, turned_k, k, mask], axis=1))
        lifted = jnp.exp2((raw - jnp.max(raw, axis=1, keepdims=True)) * (SCALING * math.log2(math.e)))
        share = 1.0 / jnp.sum(lifted, axis=1, keepdims=True)
        share_ref[0, :, h:h + 1] = share
        lifted = lifted.astype(LOW)
        soft_ref[0, h] = lifted
        pieces.append((dot(lifted, v) * share).astype(LOW))
    ctx = jnp.concatenate(pieces, axis=1)
    for j in range(blocks):
        ctx_ref[j, 0] = fold(ctx[j * rows:(j + 1) * rows])


def attend_call(me, toks, w_qkv, bias, place_q, place_k, sines, cosines, alive):
    blocks = len(toks)
    pages, rows, _ = toks[0].shape
    heads = place_q.shape[0]
    width = heads * HD
    count = blocks * rows
    by_page = lambda *shape: pl.BlockSpec((1,) + shape, lambda p, *_: (p,) + (0,) * len(shape))
    return pl.pallas_call(
        functools.partial(attend_kernel, heads, blocks),
        grid_spec=pltpu.PrefetchScalarGridSpec(
            num_scalar_prefetch=1,
            grid=(pages,),
            in_specs=[by_page(rows, D)] * blocks + [
                whole((D, 3 * width)), whole((1, 3 * width)),
                whole((heads, HD, 2 * SPAN)), whole((heads, HD, 2 * SPAN)),
                by_page(count, SPAN), by_page(count, SPAN), by_page(1, count)],
            out_specs=[
                by_page(count, 3 * width), by_page(heads, count, count), by_page(count, heads),
                pl.BlockSpec((blocks, 1, rows // 2, 2 * width), lambda p, *_: (0, p, 0, 0))],
        ),
        out_shape=[
            jax.ShapeDtypeStruct((pages, count, 3 * width), LOW),
            jax.ShapeDtypeStruct((pages, heads, count, count), LOW),
            jax.ShapeDtypeStruct((pages, count, heads), WIDE),
            jax.ShapeDtypeStruct((blocks, pages, rows // 2, 2 * width), LOW),
        ],
        compiler_params=pltpu.CompilerParams(vmem_limit_bytes=VMEM_BYTES),
        cost_estimate=cost(20e9, 20e6),
        name="attend",
    )(me, *toks, w_qkv, bias, place_q, place_k, sines, cosines, alive)


def joined_grads(own, size, pages, small, d_w, d_pq, d_pk, d_bias):
    inner = pages // size
    width = D // size
    cut = d_w.reshape(pages, size, own, 3 * width)
    parts = []
    for part in range(3):
        parts.append(jnp.concatenate(
            [cut[:, b, :, part * width:(part + 1) * width] for b in range(size)], axis=2))
    for place in (d_pq, d_pk):
        place = place.reshape(D // size, 2 * SPAN)
        order = [(lo * size + b) * own for b in range(size) for lo in range(inner)]
        parts.append(jnp.concatenate([place[at:at + own][None] for at in order], axis=0))
    row = jnp.concatenate([d_bias, jnp.zeros((1, D - 3 * width), WIDE)], axis=1)
    at = lax.broadcasted_iota(jnp.int32, small.shape, 0)
    rows = jnp.where(at == 10, row, jnp.where(at < 10, small, 0.0))
    parts.append(jnp.broadcast_to(rows[None], (pages,) + rows.shape))
    return jnp.concatenate(parts, axis=1).astype(LOW)


def attend_back_kernel(heads, blocks, joined, me_ref, *refs):
    tok_refs = refs[:blocks]
    (w_ref, small_ref, qkv_ref, soft_ref, share_ref, ctx_ref, dctx_ref, pq_ref, pk_ref, sin_ref, cos_ref,
     kept_ref, sent_ref, *out_refs, dw_sum, dpq_sum, dpk_sum, db_sum) = refs[blocks:]
    step, last = pl.program_id(0), pl.num_programs(0) - 1
    rows = tok_refs[0].shape[1]
    width = heads * HD
    sines, cosines = sin_ref[0], cos_ref[0]
    key_feats, query_feats = feature_pair(sines, cosines)
    qkv = qkv_ref[0]
    dctx = jnp.concatenate([unfold(dctx_ref[me_ref[0] ^ j, 0]) for j in range(blocks)], axis=0)
    ctx = jnp.concatenate([unfold(ctx_ref[j, 0]) for j in range(blocks)], axis=0)
    along = dctx.astype(WIDE) * ctx.astype(WIDE)

    @pl.when(step == 0)
    def _():
        for ref in (dw_sum, dpq_sum, dpk_sum, db_sum):
            ref[...] = jnp.zeros_like(ref)

    d_q, d_k, d_v = [], [], []
    for h in range(heads):
        q = qkv[:, h * HD:(h + 1) * HD]
        k = qkv[:, width + h * HD:width + (h + 1) * HD]
        v = qkv[:, 2 * width + h * HD:2 * width + (h + 1) * HD]
        dc = dctx[:, h * HD:(h + 1) * HD]
        share = share_ref[0, :, h:h + 1]
        lifted = soft_ref[0, h]
        row_dot = jnp.sum(along[:, h * HD:(h + 1) * HD], axis=1, keepdims=True)
        raw_grad = ((dot_nt(dc, v) - row_dot) * (share * SCALING) * lifted.astype(WIDE)).astype(LOW)
        d_v.append(dot_tn(lifted, (dc.astype(WIDE) * share).astype(LOW)).astype(LOW))
        turned = dot(raw_grad, jnp.concatenate([key_feats, k], axis=1))
        spread_q = turn_back(turned[:, :2 * SPAN], cosines, sines)
        d_q.append((turned[:, 2 * SPAN:] + dot_nt(spread_q, pq_ref[h])).astype(LOW))
        dpq_sum[h] += dot_tn(q, spread_q)
        turned = dot_tn(raw_grad, jnp.concatenate([query_feats, q], axis=1))
        spread_k = turn_back(turned[:, :2 * SPAN], sines, cosines)
        d_k.append((turned[:, 2 * SPAN:] + dot_nt(spread_k, pk_ref[h])).astype(LOW))
        dpk_sum[h] += dot_tn(k, spread_k)
    dqkv = jnp.concatenate(d_q + d_k + d_v, axis=1)
    db_sum[...] += jnp.sum(dqkv.astype(WIDE), axis=0, keepdims=True)
    tok = jnp.concatenate([ref[0] for ref in tok_refs], axis=0)
    dw_sum[...] += dot_tn(tok, dqkv)
    part = dot_nt(dqkv, w_ref[...]).astype(LOW)
    for j in range(blocks):
        (sent_ref if j % 2 else kept_ref)[j // 2, 0] = part[j * rows:(j + 1) * rows]

    @pl.when(step == last)
    def _():
        if joined:
            rows = joined_grads(*joined, small_ref[...], dw_sum[...], dpq_sum[...], dpk_sum[...], db_sum[...])
            even = me_ref[1] == 0
            for z in range(rows.shape[0] // 2):
                first, second = rows[2 * z], rows[2 * z + 1]
                out_refs[0][me_ref[2] ^ z] = jnp.where(even, first, second)
                out_refs[1][me_ref[2] ^ z] = jnp.where(even, second, first)
        else:
            for ref, total in zip(out_refs, (dw_sum, dpq_sum, dpk_sum, db_sum)):
                ref[...] = total[...].astype(ref.dtype)


def attend_back_call(joined, me, toks, w_qkv, small, qkv, soft, share, ctx, dctx, place_q, place_k, sines, cosines):
    blocks, pages, rows, width = dctx.shape
    rows, width = 2 * rows, width // 2
    heads = place_q.shape[0]
    count = blocks * rows
    by_page = lambda *shape: pl.BlockSpec((1,) + shape, lambda p, *_: (p,) + (0,) * len(shape))
    place = (heads, HD, 2 * SPAN)
    if joined:
        own, _, owners = joined
        sums = [jax.ShapeDtypeStruct((owners // 2, 5 * own + 16, D), LOW)] * 2
    else:
        sums = [jax.ShapeDtypeStruct((D, 3 * width), LOW), jax.ShapeDtypeStruct(place, LOW),
                jax.ShapeDtypeStruct(place, LOW), jax.ShapeDtypeStruct((1, 3 * width), WIDE)]
    return pl.pallas_call(
        functools.partial(attend_back_kernel, heads, blocks, joined),
        grid_spec=pltpu.PrefetchScalarGridSpec(
            num_scalar_prefetch=1,
            grid=(pages,),
            in_specs=[by_page(rows, D)] * blocks + [
                whole((D, 3 * width)), whole(small.shape),
                by_page(count, 3 * width), by_page(heads, count, count), by_page(count, heads),
                pl.BlockSpec((blocks, 1, rows // 2, 2 * width), lambda p, *_: (0, p, 0, 0)),
                pl.BlockSpec((blocks, 1, rows // 2, 2 * width), lambda p, *_: (0, p, 0, 0)),
                whole(place), whole(place), by_page(count, SPAN), by_page(count, SPAN)],
            out_specs=[
                *[pl.BlockSpec((blocks // 2, 1, rows, D), lambda p, *_: (0, p, 0, 0))] * 2,
                *(whole(item.shape) for item in sums)],
            scratch_shapes=[
                pltpu.VMEM((D, 3 * width), WIDE), pltpu.VMEM(place, WIDE), pltpu.VMEM(place, WIDE),
                pltpu.VMEM((1, 3 * width), WIDE)],
        ),
        out_shape=[*[jax.ShapeDtypeStruct((blocks // 2, pages, rows, D), LOW)] * 2, *sums],
        compiler_params=pltpu.CompilerParams(vmem_limit_bytes=VMEM_BYTES),
        cost_estimate=cost(30e9, 20e6),
        name="attend_back",
    )(me, *toks, w_qkv, small, qkv, soft, share, ctx, dctx, place_q, place_k, sines, cosines)


def normed(values):
    centred = values - jnp.mean(values, axis=1, keepdims=True)
    scale = lax.rsqrt(jnp.mean(centred * centred, axis=1, keepdims=True) + 1e-05)
    return centred * scale, scale


def normed_back(gradient, unit, scale):
    mean = jnp.mean(gradient, axis=1, keepdims=True)
    along = jnp.mean(gradient * unit, axis=1, keepdims=True)
    return scale * (gradient - mean - unit * along)


def summed(values):
    return jnp.sum(values, axis=0, keepdims=True)


def second_half_kernel(cuts, split, at_ref, ctx_ref, tok_ref, cot_ref, wo_ref, vec_ref, wi_ref, *refs):
    n_grads = 4 if split else 2
    wu_ref, out_ref, pre_grad_ref, dctx_ref = refs[:4]
    grad_refs = refs[4:4 + n_grads]
    (small_ref, ctx_all, first, first_low, unit_one, scale_one, act, slope, outer, pre_two_grad,
     outer_grad, first_grad) = refs[4 + n_grads:]
    step = pl.program_id(0)
    core, x_at, y_at = at_ref[0], at_ref[1] >> 1, at_ref[1] & 1
    here = lax.rem(at_ref[3], ctx_ref.shape[0])
    blocks, pages, rows, width = ctx_ref.shape
    rows, width = 2 * rows, width // 2
    count = tok_ref.shape[0]
    b_out, b_outer, gain_one, shift_one, gain_two, shift_two = (vec_ref[i:i + 1] for i in range(6))

    w_outer = wu_ref[...].reshape(D, D)

    @pl.when(step == 0)
    def _():
        small_ref[...] = jnp.zeros_like(small_ref)
        ctx = jnp.concatenate(
            [jnp.concatenate([unfold(ctx_ref[here ^ b, p]) for b in range(blocks)], axis=1)
             for p in range(pages)], axis=0)
        ctx_all[...] = ctx
        pre = tok_ref[...].astype(WIDE) + (dot(ctx, wo_ref[...]) + b_out)
        unit, scale = normed(pre)
        unit_one[...] = unit
        scale_one[...] = jnp.broadcast_to(scale, scale_one.shape)
        value = unit * gain_one + shift_one
        first[...] = value
        first_low[...] = value.astype(LOW)

    @pl.when(step < cuts)
    def _():
        inner = dot(first_low[...], wi_ref[0]) + vec_ref[pl.ds(6 + step, 1)]
        half = 0.5 + 0.5 * lax.erf(inner * (0.5 ** 0.5))
        slope[step] = half + inner * (jnp.exp(inner * inner * -0.5) * ((0.5 / math.pi) ** 0.5))
        activated = (inner * half).astype(LOW)
        act[step] = activated
        product = dot(activated, w_outer)

        @pl.when(step == 0)
        def _():
            outer[...] = product

        @pl.when(step > 0)
        def _():
            outer[...] += product

    @pl.when(step == cuts - 1)
    def _():
        unit, scale = normed(first[...] + (outer[...] + b_outer))
        out_ref[...] = (unit * gain_two + shift_two).astype(LOW)
        cot = cot_ref[...].astype(WIDE)
        grad = normed_back(cot * gain_two, unit, scale)
        pre_two_grad[...] = grad
        low = grad.astype(LOW)
        outer_grad[...] = low
        small_ref[1:2] = summed(low.astype(WIDE))
        small_ref[4:5] = summed(cot * unit)
        small_ref[5:6] = summed(cot)

    def store_24(grad):
        cut = grad.reshape(4, 2, 2, 2, D // 32, D)
        for z in range(4):
            for x in range(2):
                for y in range(2):
                    slot = (0, x_at ^ x, y_at ^ y, z)
                    first, second = cut[z, x, y, 0], cut[z, x, y, 1]
                    grad_refs[2][slot] = jnp.where(core == 0, first, second).astype(LOW)
                    grad_refs[3][slot] = jnp.where(core == 0, second, first).astype(LOW)

    @pl.when((step >= cuts) & (step < 2 * cuts))
    def _():
        j = 2 * cuts - 1 - step
        low = outer_grad[...]
        d_outer = dot_tn(act[j], low).astype(LOW)
        inner_grad = (dot_nt(low, w_outer) * slope[j]).astype(LOW)
        small_ref[pl.ds(6 + j, 1)] = summed(inner_grad.astype(WIDE))
        d_inner = dot_tn(first_low[...], inner_grad)
        if split:
            cut = d_outer.reshape(2, 2, 2, D // 8, D)
            for x in range(2):
                for y in range(2):
                    slot = (0, x_at ^ x, y_at ^ y)
                    first, second = cut[x, y, 0], cut[x, y, 1]
                    grad_refs[0][slot] = jnp.where(core == 0, first, second)
                    grad_refs[1][slot] = jnp.where(core == 0, second, first)
            store_24(d_inner)
        else:
            grad_refs[0][...] = d_outer
            grad_refs[1][0] = d_inner.astype(LOW)
        product = dot_nt(inner_grad, wi_ref[0])

        @pl.when(step == cuts)
        def _():
            first_grad[...] = pre_two_grad[...] + product

        @pl.when(step > cuts)
        def _():
            first_grad[...] += product

    @pl.when(step == 2 * cuts)
    def _():
        grad = first_grad[...]
        unit = unit_one[...]
        small_ref[2:3] = summed(grad * unit)
        small_ref[3:4] = summed(grad)
        grad = normed_back(grad * gain_one, unit, scale_one[:, :1])
        pre_grad_ref[...] = grad
        low = grad.astype(LOW)
        small_ref[0:1] = summed(low.astype(WIDE))
        dctx = dot_nt(low, wo_ref[...]).astype(LOW)
        for b in range(blocks):
            for p in range(pages):
                dctx_ref[b, p] = fold(dctx[p * rows:(p + 1) * rows, b * width:(b + 1) * width])
        d_output = dot_tn(ctx_all[...], low)
        if split:
            store_24(d_output)
        else:
            grad_refs[1][0] = d_output.astype(LOW)


def second_half_call(split, at, ctx, tok, cot, w_output, vectors, w_inner, w_outer):
    blocks, pages, rows, width = ctx.shape
    count = 2 * pages * rows
    cuts = w_inner.shape[0]
    now = lambda i: jnp.where(i < cuts, i, jnp.maximum(2 * cuts - 1 - i, 0))
    late = lambda i: jnp.where(i < cuts, cuts - 1, jnp.maximum(2 * cuts - 1 - i, 0))
    last = lambda i: jnp.where(i < 2 * cuts, late(i), cuts)
    square, tall = (D, D), (count, D)
    eighth = (1, 2, 2, D // 8, D)
    slots = (1, 2, 2, 4, D // 32, D)
    if split:
        grad_specs = [pl.BlockSpec(eighth, lambda i, at: (late(i), 0, 0, 0, 0))] * 2
        grad_specs += [pl.BlockSpec(slots, lambda i, at: (last(i), 0, 0, 0, 0, 0))] * 2
        grads = [(cuts, 2, 2, D // 8, D)] * 2 + [(cuts + 1,) + slots[1:]] * 2
    else:
        grad_specs = [
            pl.BlockSpec(square, lambda i, at: (late(i), 0)),
            pl.BlockSpec((1,) + square, lambda i, at: (last(i), 0, 0))]
        grads = [(cuts * D, D), (cuts + 1,) + square]
    return pl.pallas_call(
        functools.partial(second_half_kernel, cuts, split),
        grid_spec=pltpu.PrefetchScalarGridSpec(
            num_scalar_prefetch=1,
            grid=(2 * cuts + 1,),
            in_specs=[
                whole(ctx.shape), whole(tall), whole(tall), whole(square), whole(vectors.shape),
                pl.BlockSpec((1,) + square, lambda i, at: (now(i), 0, 0)),
                pl.BlockSpec((8, D // 8, D), lambda i, at: (now(i), 0, 0))],
            out_specs=[whole(tall), whole(tall), whole(ctx.shape), *grad_specs, whole(vectors.shape)],
            scratch_shapes=[
                pltpu.VMEM(tall, LOW), pltpu.VMEM(tall, WIDE), pltpu.VMEM(tall, LOW),
                pltpu.VMEM(tall, WIDE), pltpu.VMEM((count, 128), WIDE), pltpu.VMEM((cuts,) + tall, LOW),
                pltpu.VMEM((cuts,) + tall, WIDE), pltpu.VMEM(tall, WIDE), pltpu.VMEM(tall, WIDE),
                pltpu.VMEM(tall, LOW), pltpu.VMEM(tall, WIDE)],
        ),
        out_shape=[
            jax.ShapeDtypeStruct(tall, LOW),
            jax.ShapeDtypeStruct(tall, WIDE),
            jax.ShapeDtypeStruct(ctx.shape, LOW),
            *(jax.ShapeDtypeStruct(shape, LOW) for shape in grads),
            jax.ShapeDtypeStruct(vectors.shape, WIDE),
        ],
        compiler_params=pltpu.CompilerParams(vmem_limit_bytes=44 * 1024 * 1024),
        cost_estimate=cost(20e9, 30e6),
        name="second_half",
    )(at, ctx, tok, cot, w_output, vectors, w_inner, w_outer)


def swap(value, axis, size, bit):
    return lax.ppermute(value, axis, [(i, i ^ bit) for i in range(size)])


def exchange_slots(value):
    return jnp.stack([value[0]] + [swap(value[j], "pb", 4, j) for j in (1, 2, 3)])


def gather_slots(value):
    near = swap(value, "pb", 4, 1)
    far = swap(value, "pb", 4, 2)
    return (value, near, far, swap(far, "pb", 4, 1))


def hop(value, devices, bits):
    return lax.ppermute(value, AXES, [(i, i ^ bits) for i in range(devices)])


def added(*terms):
    return sum(term.astype(WIDE) for term in terms)


def sum_along_z(value, devices):
    return added(value[0], *(hop(value[j], devices, j << 3) for j in (1, 2, 3)))


def exchange_along_z(value, devices):
    lines = [[i + 8 * z for z in range(4)] for i in range(8)]
    return lax.all_to_all(value, AXES, 0, 0, tiled=True, axis_index_groups=lines)


def tie(*values):
    return lax.optimization_barrier(values)


def transpose_roles(value, pages, size):
    inner = pages // size
    pairs = []
    for hi in range(size):
        for lo in range(inner):
            for b in range(size):
                pairs.append(((hi * inner + lo) * size + b, (b * inner + lo) * size + hi))
    return lax.ppermute(value, AXES, pairs)


def sum_slots(kept, sent):
    total = added(kept, swap(sent, "pb", 4, 1))
    return total[0] + swap(total[1].astype(LOW), "pb", 4, 2).astype(WIDE)


def to_halves(place):
    cut = place.reshape(place.shape[:-1] + (2, 2, FREQ))
    return jnp.swapaxes(cut, -3, -2).reshape(place.shape)


def on_device(sizes, tokens, cotangent, boxes, resolution, padding,
              query_weight, keys_weight, values_weight, output_weight, query_place, keys_place,
              inner_weight, outer_weight, query_bias, keys_bias, values_bias, output_bias,
              inner_bias, outer_bias, first_gain, first_shift, second_gain, second_shift):
    page_size, pb_size = sizes
    devices = page_size * pb_size
    inner_pages = page_size // pb_size
    pages, rows, _ = tokens.shape
    count = rows * pb_size
    heads = HEADS // pb_size
    width = heads * HD
    own = query_weight.shape[0]
    ff_own = outer_weight.shape[0]
    ff = ff_own * devices
    cuts = ff // D
    me, page = lax.axis_index("pb"), lax.axis_index("page")
    place_at = (page % inner_pages) * pb_size + me
    number = page * pb_size + me
    me_array = me.astype(jnp.int32).reshape(1)
    by_link = (page_size, pb_size, own) == (8, 4, 24)

    at = jnp.stack([number & 1, (number >> 1) & 3, number >> 3, number, place_at]).astype(jnp.int32)
    small_rows = 16
    vectors = [output_bias, outer_bias, first_gain, first_shift, second_gain, second_shift]
    if by_link:
        lines = list(enumerate(vectors)) + [(8, inner_bias), (16, query_bias), (17, keys_bias), (18, values_bias)]
        lines = added(*(jnp.pad(line.astype(WIDE), (128 * i, 128 * (24 - i) - line.shape[0]))
                        for i, line in lines)).reshape(24, 128)
        packed, cols, mixed = pack_call(
            at, lines, query_weight, keys_weight, values_weight, query_place, keys_place,
            output_weight, inner_weight, outer_weight)
    else:
        cols = jnp.concatenate([query_weight, keys_weight, values_weight], axis=0)
        cols = cols.reshape(3 * own, pb_size, width).swapaxes(0, 1)
        bias_rows = jnp.zeros((3, width), LOW)
        bias_rows = lax.dynamic_update_slice(
            bias_rows, jnp.stack([query_bias, keys_bias, values_bias]), (0, place_at * own))
        bias_rows = jnp.pad(bias_rows.reshape(1, 3 * width), ((0, 7), (0, D - 3 * width)))
        mixed = jnp.concatenate([to_halves(query_place), to_halves(keys_place), bias_rows], axis=0)
        vectors = lax.dynamic_update_slice(jnp.zeros((6, D), LOW), jnp.stack(vectors), (0, number * own))
        b_inner = lax.dynamic_update_slice(jnp.zeros((ff,), LOW), inner_bias, (number * ff_own,))
        vectors = jnp.concatenate(
            [vectors, b_inner.reshape(cuts, D), jnp.zeros((small_rows - 6 - cuts, D), LOW)], axis=0)
        packed = jnp.concatenate(
            [outer_weight] + [inner_weight[:, j * D:(j + 1) * D] for j in range(cuts)]
            + [vectors, output_weight], axis=0)
    cols = lax.all_to_all(cols, "pb", 0, 0, tiled=True)
    cols = cols.swapaxes(0, 1).reshape(3 * own, D)
    mixed = transpose_roles(mixed, page_size, pb_size)
    mixed = jnp.concatenate([cols, mixed], axis=0)
    late = lax.all_gather(packed, AXES, axis=0)

    grid_x = (boxes[0] + boxes[2]) * 500 // resolution[0][:, None]
    grid_y = (boxes[1] + boxes[3]) * 500 // resolution[1][:, None]
    places = lax.all_gather(jnp.stack([grid_x, grid_y, padding]), "pb", axis=0)
    toks = gather_slots(tokens)

    places = jnp.stack([places[me ^ j] for j in range(pb_size)])
    places = places.transpose(1, 2, 0, 3).reshape(3, pages, count)
    rates = jnp.exp(jnp.arange(FREQ).astype(WIDE) * (-math.log(10000.0) / FREQ))
    grids = places[:2].astype(WIDE)
    angles = jnp.concatenate(
        [grids[0][..., None] * rates, grids[1][..., None] * rates], axis=-1)
    sines, cosines = jnp.sin(angles), jnp.cos(angles)
    alive = places[2][:, None, :]

    if by_link:
        mixed = jnp.stack([mixed] + [hop(mixed, devices, j << 3) for j in (1, 2, 3)])
        w_qkv, place_q, place_k, bias_qkv = assemble_call(
            at, mixed, hop(mixed, devices, 4), own, pb_size)
    else:
        mixed = lax.all_gather(mixed, "page", axis=0)
        w_qkv = mixed[:, :3 * own].reshape(page_size, 3, own, pb_size, width)
        w_qkv = w_qkv.transpose(0, 3, 2, 1, 4).reshape(D, 3 * width)
        bias_qkv = jnp.sum(mixed[:, 5 * own, :3 * width].astype(WIDE), axis=0, keepdims=True)
        mixed = mixed[:, 3 * own:5 * own].reshape(pb_size, inner_pages, 2, own, D)
        mixed = mixed.transpose(2, 1, 0, 3, 4).reshape(2, heads, HD, 2 * SPAN)
        place_q, place_k = mixed[0], mixed[1]

    qkv, soft, share, ctx_heads = attend_call(
        me_array, toks, w_qkv, bias_qkv, place_q, place_k, sines, cosines, alive)
    ctx = exchange_slots(ctx_heads)

    spot = ff_own
    w_inner = jnp.stack(
        [late[:, spot + j * own:spot + (j + 1) * own].reshape(D, D) for j in range(cuts)])
    spot += cuts * own
    vectors = jnp.sum(late[:, spot:spot + small_rows].astype(WIDE), axis=0)
    w_output = late[:, spot + small_rows:].reshape(D, D)
    w_outer = late if by_link else late[:, :ff_own].reshape(8 * cuts, D // 8, D)

    tok = tokens.reshape(pages * rows, D)
    output, pre_one_grad, dctx, *grads, small = second_half_call(
        by_link, at, ctx, tok, cotangent.reshape(pages * rows, D), w_output, vectors, w_inner, w_outer)
    dctx = lax.all_to_all(dctx, "pb", 0, 0, tiled=True)

    if by_link:
        outer_kept, outer_sent, inner_kept, inner_sent = grads
        outer_core, inner_core = hop(outer_sent, devices, 1), hop(inner_sent, devices, 1)
        outer_sum = added(outer_kept, outer_core).astype(LOW)
        inner_far = added(inner_kept[:, 1], inner_core[:, 1]).astype(LOW)
        dctx, outer_sum, inner_far = tie(dctx, outer_sum, inner_far)
        outer_got, inner_far = exchange_along_z(outer_sum, devices), hop(inner_far, devices, 4)

    joined = (own, pb_size, page_size) if by_link else None
    me_array = jnp.stack([me, at[1] >> 1, at[2]]).astype(jnp.int32)
    kept, sent, *sums = attend_back_call(
        joined, me_array, toks, w_qkv, small, qkv, soft, share, ctx_heads, dctx, place_q, place_k, sines, cosines)

    if by_link:
        kept, sent, mixed, mixed_far, inner_far = tie(kept, sent, *sums, inner_far)
        mixed_far, sent = hop(mixed_far, devices, 4), hop(sent, devices, 1)
        inner_sent = added(inner_kept[:, 0, 1], inner_core[:, 0, 1], inner_far[:, 1]).astype(LOW)
        inner_sent = hop(inner_sent, devices, 2)
        inner_sum = added(inner_kept[:, 0, 0], inner_core[:, 0, 0], inner_far[:, 0])
        mixed, mixed_far, kept, sent, inner_sum, inner_sent = tie(
            mixed, mixed_far, kept, sent, inner_sum, inner_sent)
        mixed = added(mixed, mixed_far).astype(LOW)
        inner_sum = added(inner_sum, inner_sent).astype(LOW).swapaxes(0, 1).reshape(4, (cuts + 1) * own, D)
        inner_sum = exchange_along_z(inner_sum, devices)
        mixed_z = [hop(mixed[j], devices, j << 3) for j in (1, 2, 3)]
        outer_sent = hop(added(*(outer_got[z, 1] for z in range(4))).astype(LOW), devices, 4)
        far = hop(added(kept[1], sent[1]).astype(LOW), devices, 2)
        outer_sum = added(*(outer_got[z, 0] for z in range(4)))
        mixed, kept, sent, far, outer_sum, outer_sent, *mixed_z = tie(
            mixed, kept, sent, far, outer_sum, outer_sent, *mixed_z)
        mixed = added(mixed[0], *mixed_z).astype(LOW)
        small = mixed[5 * own:].reshape(16, pb_size, width).swapaxes(0, 1).reshape(1, 16 * pb_size, width)
        cols = mixed[:3 * own].reshape(3 * own, pb_size, width).swapaxes(0, 1)
        cols = jnp.concatenate([cols, jnp.broadcast_to(small, (pb_size,) + small.shape[1:])], axis=1)
        cols = jnp.stack([cols[me]] + [swap(cols[me ^ j], "pb", pb_size, j) for j in (1, 2, 3)])
        mixed = transpose_roles(mixed[3 * own:5 * own + 16], page_size, pb_size)
        outer_sum = added(outer_sum, outer_sent)
        outer_sent = hop(outer_sum[1].astype(LOW), devices, 2)
        tokens_grad = pre_one_grad.reshape(pages, rows, D) + added(kept[0], sent[0], far)
        d_outer = added(outer_sum[0], outer_sent)
        d_query, d_keys, d_values, d_place_q, d_place_k, *lines = finish_call(at, cols, mixed, ff_own)
        lines = [line.reshape(-1) for line in lines]
        vectors, d_b_inner, d_bias = lines[:6], lines[6], lines[7:]
        tokens_grad, d_outer, inner_sum = tie(tokens_grad, d_outer, inner_sum)
        inner_sum = added(*(inner_sum[z] for z in range(4))).reshape(cuts + 1, own, D)
        d_inner = jnp.concatenate([inner_sum[j] for j in range(cuts)], axis=1)
        d_output = inner_sum[cuts]
    else:
        d_outer = lax.psum_scatter(
            grads[0].reshape(devices, ff_own, D), AXES, scatter_dimension=0, tiled=False).astype(WIDE)
        inner_sum = grads[1].reshape(cuts + 1, devices, own, D).swapaxes(0, 1)
        inner_sum = lax.psum_scatter(inner_sum, AXES, scatter_dimension=0, tiled=False).astype(WIDE)
        d_inner = jnp.concatenate([inner_sum[j] for j in range(cuts)], axis=1)
        d_output = inner_sum[cuts]
        d_w, d_pq, d_pk, d_bias = sums
        d_w = d_w.reshape(page_size, pb_size, own, 3, width).transpose(0, 3, 2, 1, 4)
        d_w = d_w.reshape(page_size, 3 * own, D)
        d_p = jnp.stack([d_pq, d_pk]).reshape(2, inner_pages, pb_size, own, D)
        d_p = d_p.transpose(2, 1, 0, 3, 4).reshape(page_size, 2 * own, D)
        d_bias = jnp.pad(d_bias, ((0, 7), (0, D - 3 * width))).astype(LOW)
        d_bias = jnp.broadcast_to(d_bias[None], (page_size, 8, D))
        mixed = jnp.concatenate([d_w, d_p, d_bias], axis=1)
        mixed = lax.all_to_all(mixed, "page", 0, 0, tiled=True)
        mixed = jnp.sum(mixed.astype(WIDE), axis=0).astype(LOW)
        tokens_grad = pre_one_grad.reshape(pages, rows, D) + sum_slots(kept, sent)
        cols = mixed[:3 * own].reshape(3 * own, pb_size, width).swapaxes(0, 1)
        cols = lax.all_to_all(cols, "pb", 0, 0, tiled=True)
        d_query, d_keys, d_values = cols.swapaxes(0, 1).reshape(3, own, D).astype(WIDE)
        mixed = transpose_roles(mixed[3 * own:], page_size, pb_size)
        d_place_q, d_place_k = to_halves(mixed[:own].astype(WIDE)), to_halves(mixed[own:2 * own].astype(WIDE))
        d_bias = lax.dynamic_slice(
            mixed[2 * own, :3 * width].astype(WIDE).reshape(3, width), (0, place_at * own), (3, own))
        small = jnp.sum(lax.all_gather(small, AXES, axis=0), axis=0)
        d_b_inner = lax.dynamic_slice(small[6:6 + cuts].reshape(ff), (number * ff_own,), (ff_own,))
        vectors = lax.dynamic_slice(small, (0, number * own), (6, own))

    return (
        output.reshape(pages, rows, D),
        tokens_grad,
        d_query, d_keys, d_values,
        d_output,
        d_place_q, d_place_k,
        d_inner,
        d_outer.reshape(ff_own, D),
        d_bias[0], d_bias[1], d_bias[2],
        vectors[0], d_b_inner, vectors[1], vectors[2], vectors[3], vectors[4], vectors[5],
    )


def solution(mesh):
    rows, vector = P(AXES, None), P(AXES)
    token = P("page", "pb", None)
    in_specs = (token, token, P(None, "page", "pb"), P(None, "page"), P("page", "pb"))
    in_specs = in_specs + (rows,) * 8 + (vector,) * 10
    out_specs = (token, token) + (rows,) * 8 + (vector,) * 10
    sizes = (mesh.shape["page"], mesh.shape["pb"])
    return jax.shard_map(
        functools.partial(on_device, sizes), mesh=mesh, in_specs=in_specs, out_specs=out_specs,
        check_vma=False)
```

```python
import functools
import math

import jax
import jax.numpy as jnp
from jax import lax
from jax.experimental import pallas as pl
from jax.experimental.pallas import tpu as pltpu
from jax.sharding import PartitionSpec as P

HEADS = 12
HD = 64
FREQ = 192
D = HEADS * HD
SPAN = 2 * FREQ
SCALING = (3.0 * HD) ** (-0.5)
LOW = jnp.bfloat16
WIDE = jnp.float32
AXES = ("page", "pb")
VMEM_BYTES = 56 * 1024 * 1024


def dot(a, b):
    return jnp.dot(a, b, preferred_element_type=WIDE)


def dot_nt(a, b):
    return lax.dot_general(a, b, (((1,), (1,)), ((), ())), preferred_element_type=WIDE)


def dot_tn(a, b):
    return lax.dot_general(a, b, (((0,), (0,)), ((), ())), preferred_element_type=WIDE)


def whole(shape):
    return pl.BlockSpec(shape, lambda i, *_: (0,) * len(shape))


def cost(flops, bytes_accessed):
    return pl.CostEstimate(flops=int(flops), bytes_accessed=int(bytes_accessed), transcendentals=0)


def lanes_to(rows, length, start):
    lane = lax.broadcasted_iota(jnp.int32, rows.shape, 1)
    rows = jnp.where(lane < length, rows, 0.0)
    padded = jnp.concatenate([rows, jnp.zeros((rows.shape[0], D - rows.shape[1]), WIDE)], axis=1)
    return pltpu.roll(padded, start, 1)


def halves(place):
    cut = [place[:, i * FREQ:(i + 1) * FREQ] for i in (0, 2, 1, 3)]
    return jnp.concatenate(cut, axis=1)


def pack_kernel(size, at_ref, vec_ref, wq_ref, wk_ref, wv_ref, pq_ref, pk_ref, wo_ref, wi_ref, wu_ref,
                late_ref, cols_ref, mixed_ref):
    number, place_at = at_ref[3], at_ref[4]
    own, ff_own = wq_ref.shape[0], wu_ref.shape[0]
    cuts = wi_ref.shape[1] // D
    width = D // size
    vectors = vec_ref[...]
    lanes = lanes_to(vectors[:8], own, number * own)
    row = lax.broadcasted_iota(jnp.int32, lanes.shape, 0)
    first = jnp.where(row < 6, lanes, 0.0)
    inner = lanes_to(vectors[8:16], ff_own, lax.rem(number, D // ff_own) * ff_own)
    spot = lax.div(number, D // ff_own)
    for j in range(cuts):
        hit = (row == (6 + j) % 8) & (spot == j)
        if 6 + j < 8:
            first = first + jnp.where(hit, pltpu.roll(inner, 6 + j, 0), 0.0)
    second = jnp.zeros_like(first)
    for j in range(2, cuts):
        hit = (row == j - 2) & (spot == j)
        second = second + jnp.where(hit, pltpu.roll(inner, j - 2, 0), 0.0)
    wi = wi_ref[...].astype(WIDE)
    late = [wu_ref[...].astype(WIDE)] + [wi[:, j * D:(j + 1) * D] for j in range(cuts)]
    late += [first, second, wo_ref[...].astype(WIDE)]
    late_ref[...] = jnp.concatenate(late, axis=0).astype(LOW)
    cols = jnp.concatenate([ref[...].astype(WIDE) for ref in (wq_ref, wk_ref, wv_ref)], axis=0)
    for b in range(size):
        cols_ref[b] = cols[:, b * width:(b + 1) * width].astype(LOW)
    lanes = lanes_to(vectors[16:24], own, place_at * own)
    bias = jnp.concatenate(
        [lanes[i:i + 1, :width] for i in range(3)] + [jnp.zeros((1, D - 3 * width), WIDE)], axis=1)
    bias = jnp.concatenate([bias, jnp.zeros((7, D), WIDE)], axis=0)
    places = [halves(pq_ref[...].astype(WIDE)), halves(pk_ref[...].astype(WIDE)), bias]
    mixed_ref[...] = jnp.concatenate(places, axis=0).astype(LOW)


def pack_call(at, vectors, *weights):
    own, ff_own = weights[0].shape[0], weights[-1].shape[0]
    size = 4
    rows = ff_own + weights[-2].shape[1] // D * own + 16 + own
    return pl.pallas_call(
        functools.partial(pack_kernel, size),
        out_shape=[
            jax.ShapeDtypeStruct((rows, D), LOW),
            jax.ShapeDtypeStruct((size, 3 * own, D // size), LOW),
            jax.ShapeDtypeStruct((2 * own + 8, D), LOW),
        ],
        in_specs=[pl.BlockSpec(memory_space=pltpu.SMEM)]
        + [pl.BlockSpec(memory_space=pltpu.VMEM)] * (1 + len(weights)),
        compiler_params=pltpu.CompilerParams(vmem_limit_bytes=VMEM_BYTES),
        name="pack",
    )(at, vectors, *weights)


def finish_kernel(at_ref, cols_ref, mixed_ref, *out_refs):
    grad_refs, line_refs = out_refs[:5], out_refs[5:]
    number, place_at = at_ref[3], at_ref[4]
    own = grad_refs[0].shape[0]
    size, _, width = cols_ref.shape
    cols = [cols_ref[lax.rem(number, size) ^ b].astype(WIDE) for b in range(size)]
    for i in range(3):
        grad_refs[i][...] = jnp.concatenate([c[i * own:(i + 1) * own] for c in cols], axis=1)
    mixed = mixed_ref[...].astype(WIDE)
    for i in range(2):
        grad_refs[3 + i][...] = halves(mixed[i * own:(i + 1) * own])
    total = sum(c[3 * own:] for c in cols)
    quarters = [total[16 * i:16 * (i + 1)] for i in range(size)]
    rows = sum(jnp.where(lax.div(number, 8) == i, part, 0.0) for i, part in enumerate(quarters))
    rows = pltpu.roll(rows, lax.rem(width - lax.rem(number, 8) * own, width), 1)
    inner = sum(jnp.where(lax.div(lax.rem(number, 8), 2) == i, part, 0.0) for i, part in enumerate(quarters))
    inner = sum(jnp.where(lax.div(number, 8) == j, inner[6 + j:7 + j], 0.0) for j in range(4))
    inner = pltpu.roll(jnp.broadcast_to(inner, (8, width)), lax.rem(number, 2) * (width // 2), 1)
    bias = mixed[2 * own + 8:2 * own + 16]
    bias = jnp.concatenate([bias[2:3, i * width:(i + 1) * width] for i in range(3)] + [bias[:5, :width]], axis=0)
    bias = pltpu.roll(bias, lax.rem(width - place_at * own, width), 1)
    for i, ref in enumerate(line_refs):
        source, row = (rows, i) if i < 6 else (inner, 0) if i == 6 else (bias, i - 7)
        ref[...] = source[row:row + 1, :ref.shape[1]]


def finish_call(at, cols, mixed, ff_own):
    own = (mixed.shape[0] - 16) // 2
    return pl.pallas_call(
        finish_kernel,
        out_shape=[jax.ShapeDtypeStruct((own, D), WIDE)] * 5
        + [jax.ShapeDtypeStruct((1, ff_own if i == 6 else own), WIDE) for i in range(10)],
        in_specs=[pl.BlockSpec(memory_space=pltpu.SMEM)] + [pl.BlockSpec(memory_space=pltpu.VMEM)] * 2,
        compiler_params=pltpu.CompilerParams(vmem_limit_bytes=20 * 1024 * 1024),
        name="finish",
    )(at, cols, mixed)


def assemble_kernel(own, size, at_ref, mine_ref, theirs_ref, w_ref, pq_ref, pk_ref, bias_ref, got):
    pages = got.shape[0]
    inner = pages // size
    width = D // size
    even = (at_ref[1] >> 1) == 0
    for z in range(pages // 2):
        mine, theirs = mine_ref[at_ref[2] ^ z].astype(WIDE), theirs_ref[at_ref[2] ^ z].astype(WIDE)
        got[2 * z] = jnp.where(even, mine, theirs)
        got[2 * z + 1] = jnp.where(even, theirs, mine)
    columns = []
    for part in range(3):
        rows = got[:, pl.ds(part * own, own)]
        cut = [rows[:, :, b * width:(b + 1) * width][:, None] for b in range(size)]
        columns.append(jnp.concatenate(cut, axis=1).reshape(D, width))
    w_ref[...] = jnp.concatenate(columns, axis=1).astype(LOW)
    for start, ref in ((3 * own, pq_ref), (4 * own, pk_ref)):
        order = [b * inner + lo for lo in range(inner) for b in range(size)]
        rows = jnp.concatenate([got[p, pl.ds(start, own)] for p in order], axis=0)
        ref[...] = rows.astype(LOW).reshape(ref.shape)
    bias_ref[...] = jnp.sum(got[:, pl.ds(5 * own, 8)], axis=0)[:1, :3 * width]


def assemble_call(at, mine, theirs, own, size):
    width = D // size
    place = (width // HD, HD, 2 * SPAN)
    return pl.pallas_call(
        functools.partial(assemble_kernel, own, size),
        out_shape=[
            jax.ShapeDtypeStruct((D, 3 * width), LOW),
            jax.ShapeDtypeStruct(place, LOW),
            jax.ShapeDtypeStruct(place, LOW),
            jax.ShapeDtypeStruct((1, 3 * width), WIDE),
        ],
        in_specs=[pl.BlockSpec(memory_space=pltpu.SMEM)] + [pl.BlockSpec(memory_space=pltpu.VMEM)] * 2,
        scratch_shapes=[pltpu.VMEM((2 * mine.shape[0],) + mine.shape[1:], WIDE)],
        compiler_params=pltpu.CompilerParams(vmem_limit_bytes=VMEM_BYTES),
        name="assemble",
    )(at, mine, theirs)


def fold(rows):
    half = rows.shape[0] // 2
    return jnp.concatenate([rows[:half], rows[half:]], axis=1)


def unfold(rows):
    half = rows.shape[1] // 2
    return jnp.concatenate([rows[:, :half], rows[:, half:]], axis=0)


def turn(spread, left, right):
    s, c = spread[:, :SPAN], spread[:, SPAN:]
    return jnp.concatenate(
        [(s * left + c * right).astype(LOW), (c * left - s * right).astype(LOW)], axis=1)


def turn_back(gradient, left, right):
    s, c = gradient[:, :SPAN], gradient[:, SPAN:]
    return jnp.concatenate(
        [(s * left - c * right).astype(LOW), (s * right + c * left).astype(LOW)], axis=1)


def feature_pair(sines, cosines):
    sines, cosines = sines.astype(LOW), cosines.astype(LOW)
    return (jnp.concatenate([sines, cosines], axis=1), jnp.concatenate([cosines, sines], axis=1))


def attend_kernel(heads, blocks, me_ref, *refs):
    tok_refs = refs[:blocks]
    (w_ref, bias_ref, pq_ref, pk_ref, sin_ref, cos_ref, alive_ref,
     qkv_ref, soft_ref, share_ref, ctx_ref) = refs[blocks:]
    rows = tok_refs[0].shape[1]
    width = heads * HD
    tok = jnp.concatenate([ref[0] for ref in tok_refs], axis=0)
    sines, cosines = sin_ref[0], cos_ref[0]
    key_feats, query_feats = feature_pair(sines, cosines)
    count = tok.shape[0]
    mask = jnp.broadcast_to(jnp.where(alive_ref[0] > 0, 0.0, -1e30), (128, count)).T[:, :HD]
    lane = lax.broadcasted_iota(jnp.int32, (count, HD), 1)
    mask = jnp.where(lane == 0, mask, 0.0).astype(LOW)
    ones = jnp.where(lane == 0, 1.0, 0.0).astype(LOW)
    qkv = (dot(tok, w_ref[...]) + bias_ref[...]).astype(LOW)
    qkv_ref[0] = qkv
    pieces = []
    for h in range(heads):
        q = qkv[:, h * HD:(h + 1) * HD]
        k = qkv[:, width + h * HD:width + (h + 1) * HD]
        v = qkv[:, 2 * width + h * HD:2 * width + (h + 1) * HD]
        turned_q = turn(dot(q, pq_ref[h]), cosines, sines)
        turned_k = turn(dot(k, pk_ref[h]), sines, cosines)
        raw = dot_nt(jnp.concatenate([turned_q, query_feats, q, ones], axis=1),
                     jnp.concatenate([key_feats, turned_k, k, mask], axis=1))
        lifted = jnp.exp2((raw - jnp.max(raw, axis=1, keepdims=True)) * (SCALING * math.log2(math.e)))
        share = 1.0 / jnp.sum(lifted, axis=1, keepdims=True)
        share_ref[0, :, h:h + 1] = share
        lifted = lifted.astype(LOW)
        soft_ref[0, h] = lifted
        pieces.append((dot(lifted, v) * share).astype(LOW))
    ctx = jnp.concatenate(pieces, axis=1)
    for j in range(blocks):
        ctx_ref[j, 0] = fold(ctx[j * rows:(j + 1) * rows])


def attend_call(me, toks, w_qkv, bias, place_q, place_k, sines, cosines, alive):
    blocks = len(toks)
    pages, rows, _ = toks[0].shape
    heads = place_q.shape[0]
    width = heads * HD
    count = blocks * rows
    by_page = lambda *shape: pl.BlockSpec((1,) + shape, lambda p, *_: (p,) + (0,) * len(shape))
    return pl.pallas_call(
        functools.partial(attend_kernel, heads, blocks),
        grid_spec=pltpu.PrefetchScalarGridSpec(
            num_scalar_prefetch=1,
            grid=(pages,),
            in_specs=[by_page(rows, D)] * blocks + [
                whole((D, 3 * width)), whole((1, 3 * width)),
                whole((heads, HD, 2 * SPAN)), whole((heads, HD, 2 * SPAN)),
                by_page(count, SPAN), by_page(count, SPAN), by_page(1, count)],
            out_specs=[
                by_page(count, 3 * width), by_page(heads, count, count), by_page(count, heads),
                pl.BlockSpec((blocks, 1, rows // 2, 2 * width), lambda p, *_: (0, p, 0, 0))],
        ),
        out_shape=[
            jax.ShapeDtypeStruct((pages, count, 3 * width), LOW),
            jax.ShapeDtypeStruct((pages, heads, count, count), LOW),
            jax.ShapeDtypeStruct((pages, count, heads), WIDE),
            jax.ShapeDtypeStruct((blocks, pages, rows // 2, 2 * width), LOW),
        ],
        compiler_params=pltpu.CompilerParams(vmem_limit_bytes=VMEM_BYTES),
        cost_estimate=cost(20e9, 20e6),
        name="attend",
    )(me, *toks, w_qkv, bias, place_q, place_k, sines, cosines, alive)


def joined_grads(own, size, pages, small, d_w, d_pq, d_pk, d_bias):
    inner = pages // size
    width = D // size
    cut = d_w.reshape(pages, size, own, 3 * width)
    parts = []
    for part in range(3):
        parts.append(jnp.concatenate(
            [cut[:, b, :, part * width:(part + 1) * width] for b in range(size)], axis=2))
    for place in (d_pq, d_pk):
        place = place.reshape(D // size, 2 * SPAN)
        order = [(lo * size + b) * own for b in range(size) for lo in range(inner)]
        parts.append(jnp.concatenate([place[at:at + own][None] for at in order], axis=0))
    row = jnp.concatenate([d_bias, jnp.zeros((1, D - 3 * width), WIDE)], axis=1)
    at = lax.broadcasted_iota(jnp.int32, small.shape, 0)
    rows = jnp.where(at == 10, row, jnp.where(at < 10, small, 0.0))
    parts.append(jnp.broadcast_to(rows[None], (pages,) + rows.shape))
    return jnp.concatenate(parts, axis=1).astype(LOW)


def attend_back_kernel(heads, blocks, joined, me_ref, *refs):
    tok_refs = refs[:blocks]
    (w_ref, small_ref, qkv_ref, soft_ref, share_ref, ctx_ref, dctx_ref, pq_ref, pk_ref, sin_ref, cos_ref,
     kept_ref, sent_ref, *out_refs, dw_sum, dpq_sum, dpk_sum, db_sum) = refs[blocks:]
    step, last = pl.program_id(0), pl.num_programs(0) - 1
    rows = tok_refs[0].shape[1]
    width = heads * HD
    sines, cosines = sin_ref[0], cos_ref[0]
    key_feats, query_feats = feature_pair(sines, cosines)
    qkv = qkv_ref[0]
    dctx = jnp.concatenate([unfold(dctx_ref[me_ref[0] ^ j, 0]) for j in range(blocks)], axis=0)
    ctx = jnp.concatenate([unfold(ctx_ref[j, 0]) for j in range(blocks)], axis=0)
    along = dctx.astype(WIDE) * ctx.astype(WIDE)

    @pl.when(step == 0)
    def _():
        for ref in (dw_sum, dpq_sum, dpk_sum, db_sum):
            ref[...] = jnp.zeros_like(ref)

    d_q, d_k, d_v = [], [], []
    for h in range(heads):
        q = qkv[:, h * HD:(h + 1) * HD]
        k = qkv[:, width + h * HD:width + (h + 1) * HD]
        v = qkv[:, 2 * width + h * HD:2 * width + (h + 1) * HD]
        dc = dctx[:, h * HD:(h + 1) * HD]
        share = share_ref[0, :, h:h + 1]
        lifted = soft_ref[0, h]
        row_dot = jnp.sum(along[:, h * HD:(h + 1) * HD], axis=1, keepdims=True)
        raw_grad = ((dot_nt(dc, v) - row_dot) * (share * SCALING) * lifted.astype(WIDE)).astype(LOW)
        d_v.append(dot_tn(lifted, (dc.astype(WIDE) * share).astype(LOW)).astype(LOW))
        turned = dot(raw_grad, jnp.concatenate([key_feats, k], axis=1))
        spread_q = turn_back(turned[:, :2 * SPAN], cosines, sines)
        d_q.append((turned[:, 2 * SPAN:] + dot_nt(spread_q, pq_ref[h])).astype(LOW))
        dpq_sum[h] += dot_tn(q, spread_q)
        turned = dot_tn(raw_grad, jnp.concatenate([query_feats, q], axis=1))
        spread_k = turn_back(turned[:, :2 * SPAN], sines, cosines)
        d_k.append((turned[:, 2 * SPAN:] + dot_nt(spread_k, pk_ref[h])).astype(LOW))
        dpk_sum[h] += dot_tn(k, spread_k)
    dqkv = jnp.concatenate(d_q + d_k + d_v, axis=1)
    db_sum[...] += jnp.sum(dqkv.astype(WIDE), axis=0, keepdims=True)
    tok = jnp.concatenate([ref[0] for ref in tok_refs], axis=0)
    dw_sum[...] += dot_tn(tok, dqkv)
    part = dot_nt(dqkv, w_ref[...]).astype(LOW)
    for j in range(blocks):
        (sent_ref if j % 2 else kept_ref)[j // 2, 0] = part[j * rows:(j + 1) * rows]

    @pl.when(step == last)
    def _():
        if joined:
            rows = joined_grads(*joined, small_ref[...], dw_sum[...], dpq_sum[...], dpk_sum[...], db_sum[...])
            even = me_ref[1] == 0
            for z in range(rows.shape[0] // 2):
                first, second = rows[2 * z], rows[2 * z + 1]
                out_refs[0][me_ref[2] ^ z] = jnp.where(even, first, second)
                out_refs[1][me_ref[2] ^ z] = jnp.where(even, second, first)
        else:
            for ref, total in zip(out_refs, (dw_sum, dpq_sum, dpk_sum, db_sum)):
                ref[...] = total[...].astype(ref.dtype)


def attend_back_call(joined, me, toks, w_qkv, small, qkv, soft, share, ctx, dctx, place_q, place_k, sines, cosines):
    blocks, pages, rows, width = dctx.shape
    rows, width = 2 * rows, width // 2
    heads = place_q.shape[0]
    count = blocks * rows
    by_page = lambda *shape: pl.BlockSpec((1,) + shape, lambda p, *_: (p,) + (0,) * len(shape))
    place = (heads, HD, 2 * SPAN)
    if joined:
        own, _, owners = joined
        sums = [jax.ShapeDtypeStruct((owners // 2, 5 * own + 16, D), LOW)] * 2
    else:
        sums = [jax.ShapeDtypeStruct((D, 3 * width), LOW), jax.ShapeDtypeStruct(place, LOW),
                jax.ShapeDtypeStruct(place, LOW), jax.ShapeDtypeStruct((1, 3 * width), WIDE)]
    return pl.pallas_call(
        functools.partial(attend_back_kernel, heads, blocks, joined),
        grid_spec=pltpu.PrefetchScalarGridSpec(
            num_scalar_prefetch=1,
            grid=(pages,),
            in_specs=[by_page(rows, D)] * blocks + [
                whole((D, 3 * width)), whole(small.shape),
                by_page(count, 3 * width), by_page(heads, count, count), by_page(count, heads),
                pl.BlockSpec((blocks, 1, rows // 2, 2 * width), lambda p, *_: (0, p, 0, 0)),
                pl.BlockSpec((blocks, 1, rows // 2, 2 * width), lambda p, *_: (0, p, 0, 0)),
                whole(place), whole(place), by_page(count, SPAN), by_page(count, SPAN)],
            out_specs=[
                *[pl.BlockSpec((blocks // 2, 1, rows, D), lambda p, *_: (0, p, 0, 0))] * 2,
                *(whole(item.shape) for item in sums)],
            scratch_shapes=[
                pltpu.VMEM((D, 3 * width), WIDE), pltpu.VMEM(place, WIDE), pltpu.VMEM(place, WIDE),
                pltpu.VMEM((1, 3 * width), WIDE)],
        ),
        out_shape=[*[jax.ShapeDtypeStruct((blocks // 2, pages, rows, D), LOW)] * 2, *sums],
        compiler_params=pltpu.CompilerParams(vmem_limit_bytes=VMEM_BYTES),
        cost_estimate=cost(30e9, 20e6),
        name="attend_back",
    )(me, *toks, w_qkv, small, qkv, soft, share, ctx, dctx, place_q, place_k, sines, cosines)


def normed(values):
    centred = values - jnp.mean(values, axis=1, keepdims=True)
    scale = lax.rsqrt(jnp.mean(centred * centred, axis=1, keepdims=True) + 1e-05)
    return centred * scale, scale


def normed_back(gradient, unit, scale):
    mean = jnp.mean(gradient, axis=1, keepdims=True)
    along = jnp.mean(gradient * unit, axis=1, keepdims=True)
    return scale * (gradient - mean - unit * along)


def summed(values):
    return jnp.sum(values, axis=0, keepdims=True)


def second_half_kernel(cuts, split, at_ref, ctx_ref, tok_ref, cot_ref, wo_ref, vec_ref, wi_ref, *refs):
    n_grads = 4 if split else 2
    wu_ref, out_ref, pre_grad_ref, dctx_ref = refs[:4]
    grad_refs = refs[4:4 + n_grads]
    (small_ref, ctx_all, first, first_low, unit_one, scale_one, act, slope, outer, pre_two_grad,
     outer_grad, first_grad) = refs[4 + n_grads:]
    step = pl.program_id(0)
    core, x_at, y_at = at_ref[0], at_ref[1] >> 1, at_ref[1] & 1
    here = lax.rem(at_ref[3], ctx_ref.shape[0])
    blocks, pages, rows, width = ctx_ref.shape
    rows, width = 2 * rows, width // 2
    count = tok_ref.shape[0]
    b_out, b_outer, gain_one, shift_one, gain_two, shift_two = (vec_ref[i:i + 1] for i in range(6))

    w_outer = wu_ref[...].reshape(D, D)

    @pl.when(step == 0)
    def _():
        small_ref[...] = jnp.zeros_like(small_ref)
        ctx = jnp.concatenate(
            [jnp.concatenate([unfold(ctx_ref[here ^ b, p]) for b in range(blocks)], axis=1)
             for p in range(pages)], axis=0)
        ctx_all[...] = ctx
        pre = tok_ref[...].astype(WIDE) + (dot(ctx, wo_ref[...]) + b_out)
        unit, scale = normed(pre)
        unit_one[...] = unit
        scale_one[...] = jnp.broadcast_to(scale, scale_one.shape)
        value = unit * gain_one + shift_one
        first[...] = value
        first_low[...] = value.astype(LOW)

    @pl.when(step < cuts)
    def _():
        inner = dot(first_low[...], wi_ref[0]) + vec_ref[pl.ds(6 + step, 1)]
        half = 0.5 + 0.5 * lax.erf(inner * (0.5 ** 0.5))
        slope[step] = half + inner * (jnp.exp(inner * inner * -0.5) * ((0.5 / math.pi) ** 0.5))
        activated = (inner * half).astype(LOW)
        act[step] = activated
        product = dot(activated, w_outer)

        @pl.when(step == 0)
        def _():
            outer[...] = product

        @pl.when(step > 0)
        def _():
            outer[...] += product

    @pl.when(step == cuts - 1)
    def _():
        unit, scale = normed(first[...] + (outer[...] + b_outer))
        out_ref[...] = (unit * gain_two + shift_two).astype(LOW)
        cot = cot_ref[...].astype(WIDE)
        grad = normed_back(cot * gain_two, unit, scale)
        pre_two_grad[...] = grad
        low = grad.astype(LOW)
        outer_grad[...] = low
        small_ref[1:2] = summed(low.astype(WIDE))
        small_ref[4:5] = summed(cot * unit)
        small_ref[5:6] = summed(cot)

    def store_24(grad):
        cut = grad.reshape(4, 2, 2, 2, D // 32, D)
        for z in range(4):
            for x in range(2):
                for y in range(2):
                    slot = (0, x_at ^ x, y_at ^ y, z)
                    first, second = cut[z, x, y, 0], cut[z, x, y, 1]
                    grad_refs[2][slot] = jnp.where(core == 0, first, second).astype(LOW)
                    grad_refs[3][slot] = jnp.where(core == 0, second, first).astype(LOW)

    @pl.when((step >= cuts) & (step < 2 * cuts))
    def _():
        j = 2 * cuts - 1 - step
        low = outer_grad[...]
        d_outer = dot_tn(act[j], low).astype(LOW)
        inner_grad = (dot_nt(low, w_outer) * slope[j]).astype(LOW)
        small_ref[pl.ds(6 + j, 1)] = summed(inner_grad.astype(WIDE))
        d_inner = dot_tn(first_low[...], inner_grad)
        if split:
            cut = d_outer.reshape(2, 2, 2, D // 8, D)
            for x in range(2):
                for y in range(2):
                    slot = (0, x_at ^ x, y_at ^ y)
                    first, second = cut[x, y, 0], cut[x, y, 1]
                    grad_refs[0][slot] = jnp.where(core == 0, first, second)
                    grad_refs[1][slot] = jnp.where(core == 0, second, first)
            store_24(d_inner)
        else:
            grad_refs[0][...] = d_outer
            grad_refs[1][0] = d_inner.astype(LOW)
        product = dot_nt(inner_grad, wi_ref[0])

        @pl.when(step == cuts)
        def _():
            first_grad[...] = pre_two_grad[...] + product

        @pl.when(step > cuts)
        def _():
            first_grad[...] += product

    @pl.when(step == 2 * cuts)
    def _():
        grad = first_grad[...]
        unit = unit_one[...]
        small_ref[2:3] = summed(grad * unit)
        small_ref[3:4] = summed(grad)
        grad = normed_back(grad * gain_one, unit, scale_one[:, :1])
        pre_grad_ref[...] = grad
        low = grad.astype(LOW)
        small_ref[0:1] = summed(low.astype(WIDE))
        dctx = dot_nt(low, wo_ref[...]).astype(LOW)
        for b in range(blocks):
            for p in range(pages):
                dctx_ref[b, p] = fold(dctx[p * rows:(p + 1) * rows, b * width:(b + 1) * width])
        d_output = dot_tn(ctx_all[...], low)
        if split:
            store_24(d_output)
        else:
            grad_refs[1][0] = d_output.astype(LOW)


def second_half_call(split, at, ctx, tok, cot, w_output, vectors, w_inner, w_outer):
    blocks, pages, rows, width = ctx.shape
    count = 2 * pages * rows
    cuts = w_inner.shape[0]
    now = lambda i: jnp.where(i < cuts, i, jnp.maximum(2 * cuts - 1 - i, 0))
    late = lambda i: jnp.where(i < cuts, cuts - 1, jnp.maximum(2 * cuts - 1 - i, 0))
    last = lambda i: jnp.where(i < 2 * cuts, late(i), cuts)
    square, tall = (D, D), (count, D)
    eighth = (1, 2, 2, D // 8, D)
    slots = (1, 2, 2, 4, D // 32, D)
    if split:
        grad_specs = [pl.BlockSpec(eighth, lambda i, at: (late(i), 0, 0, 0, 0))] * 2
        grad_specs += [pl.BlockSpec(slots, lambda i, at: (last(i), 0, 0, 0, 0, 0))] * 2
        grads = [(cuts, 2, 2, D // 8, D)] * 2 + [(cuts + 1,) + slots[1:]] * 2
    else:
        grad_specs = [
            pl.BlockSpec(square, lambda i, at: (late(i), 0)),
            pl.BlockSpec((1,) + square, lambda i, at: (last(i), 0, 0))]
        grads = [(cuts * D, D), (cuts + 1,) + square]
    return pl.pallas_call(
        functools.partial(second_half_kernel, cuts, split),
        grid_spec=pltpu.PrefetchScalarGridSpec(
            num_scalar_prefetch=1,
            grid=(2 * cuts + 1,),
            in_specs=[
                whole(ctx.shape), whole(tall), whole(tall), whole(square), whole(vectors.shape),
                pl.BlockSpec((1,) + square, lambda i, at: (now(i), 0, 0)),
                pl.BlockSpec((8, D // 8, D), lambda i, at: (now(i), 0, 0))],
            out_specs=[whole(tall), whole(tall), whole(ctx.shape), *grad_specs, whole(vectors.shape)],
            scratch_shapes=[
                pltpu.VMEM(tall, LOW), pltpu.VMEM(tall, WIDE), pltpu.VMEM(tall, LOW),
                pltpu.VMEM(tall, WIDE), pltpu.VMEM((count, 128), WIDE), pltpu.VMEM((cuts,) + tall, LOW),
                pltpu.VMEM((cuts,) + tall, WIDE), pltpu.VMEM(tall, WIDE), pltpu.VMEM(tall, WIDE),
                pltpu.VMEM(tall, LOW), pltpu.VMEM(tall, WIDE)],
        ),
        out_shape=[
            jax.ShapeDtypeStruct(tall, LOW),
            jax.ShapeDtypeStruct(tall, WIDE),
            jax.ShapeDtypeStruct(ctx.shape, LOW),
            *(jax.ShapeDtypeStruct(shape, LOW) for shape in grads),
            jax.ShapeDtypeStruct(vectors.shape, WIDE),
        ],
        compiler_params=pltpu.CompilerParams(vmem_limit_bytes=48 * 1024 * 1024),
        cost_estimate=cost(20e9, 30e6),
        name="second_half",
    )(at, ctx, tok, cot, w_output, vectors, w_inner, w_outer)


def swap(value, axis, size, bit):
    return lax.ppermute(value, axis, [(i, i ^ bit) for i in range(size)])


def exchange_slots(value):
    return jnp.stack([value[0]] + [swap(value[j], "pb", 4, j) for j in (1, 2, 3)])


def gather_slots(value):
    near = swap(value, "pb", 4, 1)
    far = swap(value, "pb", 4, 2)
    return (value, near, far, swap(far, "pb", 4, 1))


def hop(value, devices, bits):
    return lax.ppermute(value, AXES, [(i, i ^ bits) for i in range(devices)])


def added(*terms):
    return sum(term.astype(WIDE) for term in terms)


def sum_along_z(value, devices):
    return added(value[0], *(hop(value[j], devices, j << 3) for j in (1, 2, 3)))


def exchange_along_z(value, devices):
    lines = [[i + 8 * z for z in range(4)] for i in range(8)]
    return lax.all_to_all(value, AXES, 0, 0, tiled=True, axis_index_groups=lines)


def tie(*values):
    return lax.optimization_barrier(values)


def transpose_roles(value, pages, size):
    inner = pages // size
    pairs = []
    for hi in range(size):
        for lo in range(inner):
            for b in range(size):
                pairs.append(((hi * inner + lo) * size + b, (b * inner + lo) * size + hi))
    return lax.ppermute(value, AXES, pairs)


def sum_slots(kept, sent):
    total = added(kept, swap(sent, "pb", 4, 1))
    return total[0] + swap(total[1].astype(LOW), "pb", 4, 2).astype(WIDE)


def to_halves(place):
    cut = place.reshape(place.shape[:-1] + (2, 2, FREQ))
    return jnp.swapaxes(cut, -3, -2).reshape(place.shape)


def on_device(sizes, tokens, cotangent, boxes, resolution, padding,
              query_weight, keys_weight, values_weight, output_weight, query_place, keys_place,
              inner_weight, outer_weight, query_bias, keys_bias, values_bias, output_bias,
              inner_bias, outer_bias, first_gain, first_shift, second_gain, second_shift):
    page_size, pb_size = sizes
    devices = page_size * pb_size
    inner_pages = page_size // pb_size
    pages, rows, _ = tokens.shape
    count = rows * pb_size
    heads = HEADS // pb_size
    width = heads * HD
    own = query_weight.shape[0]
    ff_own = outer_weight.shape[0]
    ff = ff_own * devices
    cuts = ff // D
    me, page = lax.axis_index("pb"), lax.axis_index("page")
    place_at = (page % inner_pages) * pb_size + me
    number = page * pb_size + me
    me_array = me.astype(jnp.int32).reshape(1)
    by_link = (page_size, pb_size, own) == (8, 4, 24)

    at = jnp.stack([number & 1, (number >> 1) & 3, number >> 3, number, place_at]).astype(jnp.int32)
    small_rows = 16
    vectors = [output_bias, outer_bias, first_gain, first_shift, second_gain, second_shift]
    if by_link:
        lines = list(enumerate(vectors)) + [(8, inner_bias), (16, query_bias), (17, keys_bias), (18, values_bias)]
        lines = added(*(jnp.pad(line.astype(WIDE), (128 * i, 128 * (24 - i) - line.shape[0]))
                        for i, line in lines)).reshape(24, 128)
        packed, cols, mixed = pack_call(
            at, lines, query_weight, keys_weight, values_weight, query_place, keys_place,
            output_weight, inner_weight, outer_weight)
    else:
        cols = jnp.concatenate([query_weight, keys_weight, values_weight], axis=0)
        cols = cols.reshape(3 * own, pb_size, width).swapaxes(0, 1)
        bias_rows = jnp.zeros((3, width), LOW)
        bias_rows = lax.dynamic_update_slice(
            bias_rows, jnp.stack([query_bias, keys_bias, values_bias]), (0, place_at * own))
        bias_rows = jnp.pad(bias_rows.reshape(1, 3 * width), ((0, 7), (0, D - 3 * width)))
        mixed = jnp.concatenate([to_halves(query_place), to_halves(keys_place), bias_rows], axis=0)
        vectors = lax.dynamic_update_slice(jnp.zeros((6, D), LOW), jnp.stack(vectors), (0, number * own))
        b_inner = lax.dynamic_update_slice(jnp.zeros((ff,), LOW), inner_bias, (number * ff_own,))
        vectors = jnp.concatenate(
            [vectors, b_inner.reshape(cuts, D), jnp.zeros((small_rows - 6 - cuts, D), LOW)], axis=0)
        packed = jnp.concatenate(
            [outer_weight] + [inner_weight[:, j * D:(j + 1) * D] for j in range(cuts)]
            + [vectors, output_weight], axis=0)
    cols = lax.all_to_all(cols, "pb", 0, 0, tiled=True)
    cols = cols.swapaxes(0, 1).reshape(3 * own, D)
    mixed = transpose_roles(mixed, page_size, pb_size)
    mixed = jnp.concatenate([cols, mixed], axis=0)
    late = lax.all_gather(packed, AXES, axis=0)

    grid_x = (boxes[0] + boxes[2]) * 500 // resolution[0][:, None]
    grid_y = (boxes[1] + boxes[3]) * 500 // resolution[1][:, None]
    places = lax.all_gather(jnp.stack([grid_x, grid_y, padding]), "pb", axis=0)
    toks = gather_slots(tokens)

    places = jnp.stack([places[me ^ j] for j in range(pb_size)])
    places = places.transpose(1, 2, 0, 3).reshape(3, pages, count)
    rates = jnp.exp(jnp.arange(FREQ).astype(WIDE) * (-math.log(10000.0) / FREQ))
    grids = places[:2].astype(WIDE)
    angles = jnp.concatenate(
        [grids[0][..., None] * rates, grids[1][..., None] * rates], axis=-1)
    sines, cosines = jnp.sin(angles), jnp.cos(angles)
    alive = places[2][:, None, :]

    if by_link:
        mixed = jnp.stack([mixed] + [hop(mixed, devices, j << 3) for j in (1, 2, 3)])
        w_qkv, place_q, place_k, bias_qkv = assemble_call(
            at, mixed, hop(mixed, devices, 4), own, pb_size)
    else:
        mixed = lax.all_gather(mixed, "page", axis=0)
        w_qkv = mixed[:, :3 * own].reshape(page_size, 3, own, pb_size, width)
        w_qkv = w_qkv.transpose(0, 3, 2, 1, 4).reshape(D, 3 * width)
        bias_qkv = jnp.sum(mixed[:, 5 * own, :3 * width].astype(WIDE), axis=0, keepdims=True)
        mixed = mixed[:, 3 * own:5 * own].reshape(pb_size, inner_pages, 2, own, D)
        mixed = mixed.transpose(2, 1, 0, 3, 4).reshape(2, heads, HD, 2 * SPAN)
        place_q, place_k = mixed[0], mixed[1]

    qkv, soft, share, ctx_heads = attend_call(
        me_array, toks, w_qkv, bias_qkv, place_q, place_k, sines, cosines, alive)
    ctx = exchange_slots(ctx_heads)

    spot = ff_own
    w_inner = jnp.stack(
        [late[:, spot + j * own:spot + (j + 1) * own].reshape(D, D) for j in range(cuts)])
    spot += cuts * own
    vectors = jnp.sum(late[:, spot:spot + small_rows].astype(WIDE), axis=0)
    w_output = late[:, spot + small_rows:].reshape(D, D)
    w_outer = late if by_link else late[:, :ff_own].reshape(8 * cuts, D // 8, D)

    tok = tokens.reshape(pages * rows, D)
    output, pre_one_grad, dctx, *grads, small = second_half_call(
        by_link, at, ctx, tok, cotangent.reshape(pages * rows, D), w_output, vectors, w_inner, w_outer)
    dctx = lax.all_to_all(dctx, "pb", 0, 0, tiled=True)

    if by_link:
        outer_kept, outer_sent, inner_kept, inner_sent = grads
        outer_core, inner_core = hop(outer_sent, devices, 1), hop(inner_sent, devices, 1)
        outer_sum = added(outer_kept, outer_core).astype(LOW)
        inner_far = added(inner_kept[:, 1], inner_core[:, 1]).astype(LOW)
        dctx, outer_sum, inner_far = tie(dctx, outer_sum, inner_far)
        outer_got, inner_far = exchange_along_z(outer_sum, devices), hop(inner_far, devices, 4)

    joined = (own, pb_size, page_size) if by_link else None
    me_array = jnp.stack([me, at[1] >> 1, at[2]]).astype(jnp.int32)
    kept, sent, *sums = attend_back_call(
        joined, me_array, toks, w_qkv, small, qkv, soft, share, ctx_heads, dctx, place_q, place_k, sines, cosines)

    if by_link:
        kept, sent, mixed, mixed_far, inner_far = tie(kept, sent, *sums, inner_far)
        mixed_far, sent = hop(mixed_far, devices, 4), hop(sent, devices, 1)
        inner_sent = added(inner_kept[:, 0, 1], inner_core[:, 0, 1], inner_far[:, 1]).astype(LOW)
        inner_sent = hop(inner_sent, devices, 2)
        inner_sum = added(inner_kept[:, 0, 0], inner_core[:, 0, 0], inner_far[:, 0])
        mixed, mixed_far, kept, sent, inner_sum, inner_sent = tie(
            mixed, mixed_far, kept, sent, inner_sum, inner_sent)
        mixed = added(mixed, mixed_far).astype(LOW)
        inner_sum = added(inner_sum, inner_sent).astype(LOW).swapaxes(0, 1).reshape(4, (cuts + 1) * own, D)
        inner_sum = exchange_along_z(inner_sum, devices)
        mixed_z = [hop(mixed[j], devices, j << 3) for j in (1, 2, 3)]
        outer_sent = hop(added(*(outer_got[z, 1] for z in range(4))).astype(LOW), devices, 4)
        far = hop(added(kept[1], sent[1]).astype(LOW), devices, 2)
        outer_sum = added(*(outer_got[z, 0] for z in range(4)))
        mixed, kept, sent, far, outer_sum, outer_sent, *mixed_z = tie(
            mixed, kept, sent, far, outer_sum, outer_sent, *mixed_z)
        mixed = added(mixed[0], *mixed_z).astype(LOW)
        small = mixed[5 * own:].reshape(16, pb_size, width).swapaxes(0, 1).reshape(1, 16 * pb_size, width)
        cols = mixed[:3 * own].reshape(3 * own, pb_size, width).swapaxes(0, 1)
        cols = jnp.concatenate([cols, jnp.broadcast_to(small, (pb_size,) + small.shape[1:])], axis=1)
        cols = jnp.stack([cols[me]] + [swap(cols[me ^ j], "pb", pb_size, j) for j in (1, 2, 3)])
        mixed = transpose_roles(mixed[3 * own:5 * own + 16], page_size, pb_size)
        outer_sum = added(outer_sum, outer_sent)
        outer_sent = hop(outer_sum[1].astype(LOW), devices, 2)
        tokens_grad = pre_one_grad.reshape(pages, rows, D) + added(kept[0], sent[0], far)
        d_outer = added(outer_sum[0], outer_sent)
        d_query, d_keys, d_values, d_place_q, d_place_k, *lines = finish_call(at, cols, mixed, ff_own)
        lines = [line.reshape(-1) for line in lines]
        vectors, d_b_inner, d_bias = lines[:6], lines[6], lines[7:]
        tokens_grad, d_outer, inner_sum = tie(tokens_grad, d_outer, inner_sum)
        inner_sum = added(*(inner_sum[z] for z in range(4))).reshape(cuts + 1, own, D)
        d_inner = jnp.concatenate([inner_sum[j] for j in range(cuts)], axis=1)
        d_output = inner_sum[cuts]
    else:
        d_outer = lax.psum_scatter(
            grads[0].reshape(devices, ff_own, D), AXES, scatter_dimension=0, tiled=False).astype(WIDE)
        inner_sum = grads[1].reshape(cuts + 1, devices, own, D).swapaxes(0, 1)
        inner_sum = lax.psum_scatter(inner_sum, AXES, scatter_dimension=0, tiled=False).astype(WIDE)
        d_inner = jnp.concatenate([inner_sum[j] for j in range(cuts)], axis=1)
        d_output = inner_sum[cuts]
        d_w, d_pq, d_pk, d_bias = sums
        d_w = d_w.reshape(page_size, pb_size, own, 3, width).transpose(0, 3, 2, 1, 4)
        d_w = d_w.reshape(page_size, 3 * own, D)
        d_p = jnp.stack([d_pq, d_pk]).reshape(2, inner_pages, pb_size, own, D)
        d_p = d_p.transpose(2, 1, 0, 3, 4).reshape(page_size, 2 * own, D)
        d_bias = jnp.pad(d_bias, ((0, 7), (0, D - 3 * width))).astype(LOW)
        d_bias = jnp.broadcast_to(d_bias[None], (page_size, 8, D))
        mixed = jnp.concatenate([d_w, d_p, d_bias], axis=1)
        mixed = lax.all_to_all(mixed, "page", 0, 0, tiled=True)
        mixed = jnp.sum(mixed.astype(WIDE), axis=0).astype(LOW)
        tokens_grad = pre_one_grad.reshape(pages, rows, D) + sum_slots(kept, sent)
        cols = mixed[:3 * own].reshape(3 * own, pb_size, width).swapaxes(0, 1)
        cols = lax.all_to_all(cols, "pb", 0, 0, tiled=True)
        d_query, d_keys, d_values = cols.swapaxes(0, 1).reshape(3, own, D).astype(WIDE)
        mixed = transpose_roles(mixed[3 * own:], page_size, pb_size)
        d_place_q, d_place_k = to_halves(mixed[:own].astype(WIDE)), to_halves(mixed[own:2 * own].astype(WIDE))
        d_bias = lax.dynamic_slice(
            mixed[2 * own, :3 * width].astype(WIDE).reshape(3, width), (0, place_at * own), (3, own))
        small = jnp.sum(lax.all_gather(small, AXES, axis=0), axis=0)
        d_b_inner = lax.dynamic_slice(small[6:6 + cuts].reshape(ff), (number * ff_own,), (ff_own,))
        vectors = lax.dynamic_slice(small, (0, number * own), (6, own))

    return (
        output.reshape(pages, rows, D),
        tokens_grad,
        d_query, d_keys, d_values,
        d_output,
        d_place_q, d_place_k,
        d_inner,
        d_outer.reshape(ff_own, D),
        d_bias[0], d_bias[1], d_bias[2],
        vectors[0], d_b_inner, vectors[1], vectors[2], vectors[3], vectors[4], vectors[5],
    )


def solution(mesh):
    rows, vector = P(AXES, None), P(AXES)
    token = P("page", "pb", None)
    in_specs = (token, token, P(None, "page", "pb"), P(None, "page"), P("page", "pb"))
    in_specs = in_specs + (rows,) * 8 + (vector,) * 10
    out_specs = (token, token) + (rows,) * 8 + (vector,) * 10
    sizes = (mesh.shape["page"], mesh.shape["pb"])
    return jax.shard_map(
        functools.partial(on_device, sizes), mesh=mesh, in_specs=in_specs, out_specs=out_specs,
        check_vma=False)
```
